32 devices in a mesh: group: 2 (over y), dev: 4 (over z), tp: 4 (over x, core).
Axes of the slice: x: 2, y: 2, z: 4, core: 2. Of those that a mesh axis runs over, the one named last changes fastest.
Arguments:
- hidden: bfloat16 [256, 3584], P(('group', 'dev')), parts along dimension 0, may hold values from -6 to 6
- routes: int32 [256, 8], P(('group', 'dev')), parts along dimension 0, may hold values from 0 to 31, all different within a row; in each aligned block of 32 rows (0 to 31, 32 to 63, ...) at most 16 rows name the same one
- router_weight: bfloat16 [3584, 32], replicated, may hold values from -0.1875 to 0.1875
- gate_weight: bfloat16 [32, 3584, 1024], P('dev', None, 'tp'), may hold values from -0.09375 to 0.09375
- up_weight: bfloat16 [32, 3584, 1024], P('dev', None, 'tp'), may hold values from -0.09375 to 0.09375
- down_weight: bfloat16 [32, 1024, 3584], P('dev', 'tp'), may hold values from -0.1875 to 0.1875
- q_latent: bfloat16 [16, 128, 512], P(('group', 'dev')), parts along dimension 0, may hold values from -16 to 16
- q_rope: bfloat16 [16, 64, 128], P(('group', 'dev')), parts along dimension 0, may hold values from -4.2 to 4.2
- cache_latent: bfloat16 [16, 2048, 512], P(('group', 'dev'), 'tp'), parts along dimension 0, may hold values from -6 to 6
- cache_rope: bfloat16 [16, 64, 2048], P(('group', 'dev'), None, 'tp'), parts along dimension 0, may hold values from -8 to 8
- cache_len: int32 [16], P(('group', 'dev')), parts along dimension 0, may hold values from 512 to 2048, as said below
Outputs:
- moe_out: bfloat16 [256, 3584], P(('group', 'dev'), 'tp'), parts along dimension 0
- attended: bfloat16 [16, 128, 512], P(('group', 'dev')), parts along dimension 0
The draws below stay inside these ranges and needn't reach their ends.
There are 2 independent parts, one for each index of `group`. The reference program is written for one: setup_inputs(seed, part) draws one part's arguments, and reference() takes and returns one part's arrays. A program takes and returns all parts, laid end to end along the dimension named above; an argument that names none is the same for every part. Nothing has to cross between parts.
Inputs may be any that keep to these rules, and one draw needn't show every extreme that they name: `routes`: each row names 8 different experts. In each aligned block of 32 rows (the rows of one device) no expert is named by more than 16 rows, and in some block one expert is named by exactly 16 rows. `cache_len`: some row is full in every draw.
All inputs are finite; a program needn't handle non-finite values.
Results may differ from the reference program's by a relative error of at most 0.012.
Values may be sent and summed in bfloat16 or wider, within the bound.
No kernel may reach another device: no remote copies, remote signals or barrier semaphores. Data moves between devices by JAX's collectives and lax.ppermute only.
A program may use at most 192 MiB of HBM per device.

```python
import math
import jax
import jax.numpy as jnp
import numpy as np
from jax import lax

D = 3584
FFE = 1024
HEADS = 128
LAT = 512
ROPE = 64
TOP = 8
TOK_DEV = 32
CTX = 2048
CAP = 16
EXPERTS = 32
TOKENS = 128
ATT_ROWS = 8
FFE_BLK = 256
N_DEV = 4
N_TP = 4


score_scale = 0.13524


def noise_field(key, shape, share):
    normal_part = jnp.clip(jax.random.normal(jax.random.fold_in(key, 1), shape, jnp.float32), -6.0, 6.0)
    flat_part = jax.random.uniform(jax.random.fold_in(key, 2), shape, jnp.float32, -1.7, 1.7)
    return (1.0 - share) * normal_part + share * flat_part


def sign_field(key, shape):
    return (2 * jax.random.randint(key, shape, 0, 2) - 1).astype(jnp.float32)


def attention_fields(key, share):
    keys = jax.random.split(key, 9)
    latent_keys = noise_field(keys[0], (ATT_ROWS, CTX, LAT), share)
    rope_keys = noise_field(keys[1], (ATT_ROWS, ROPE, CTX), share)
    latent_query = 0.7 * noise_field(keys[2], (ATT_ROWS, HEADS, LAT), share)
    rope_query = 0.7 * noise_field(keys[3], (ATT_ROWS, ROPE, HEADS), share)
    first_pos = jax.random.randint(keys[4], (ATT_ROWS,), 0, CTX // 8)
    second_pos = first_pos + 1 + jax.random.randint(keys[5], (ATT_ROWS,), 0, CTX // 8 - 1)
    sign_one = sign_field(keys[6], (ATT_ROWS, LAT))
    sign_two = sign_field(jax.random.fold_in(keys[6], 5), (ATT_ROWS, LAT))
    rope_sign = sign_field(keys[7], (ATT_ROWS, ROPE))
    gap_size = jax.random.uniform(keys[8], (ATT_ROWS,), jnp.float32, 1.0, 3.0) / (score_scale * ROPE)
    head_pick = (jax.random.randint(jax.random.fold_in(keys[8], 3), (ATT_ROWS, HEADS), 0, 8) == 0).astype(jnp.float32)
    power = jax.random.uniform(jax.random.fold_in(keys[8], 4), (ATT_ROWS, HEADS), jnp.float32, 75.0, 250.0) / (score_scale * LAT)
    places = jnp.arange(CTX)
    at_first = (places[None, :] == first_pos[:, None]).astype(jnp.float32)
    at_second = (places[None, :] == second_pos[:, None]).astype(jnp.float32)
    latent_keys = latent_keys * (1.0 - at_first - at_second)[:, :, None] + at_first[:, :, None] * sign_one[:, None, :] + at_second[:, :, None] * sign_two[:, None, :]
    rope_first = jnp.take_along_axis(rope_keys, jnp.broadcast_to(first_pos[:, None, None], (ATT_ROWS, ROPE, 1)), axis=2)
    rope_target = rope_first - gap_size[:, None, None] * rope_sign[:, :, None]
    rope_keys = rope_keys + at_second[:, None, :] * (rope_target - rope_keys)
    latent_query = latent_query * (1.0 - head_pick)[:, :, None] + (head_pick * power)[:, :, None] * (sign_one + sign_two)[:, None, :]
    rope_query = rope_query * (1.0 - head_pick)[:, None, :] + head_pick[:, None, :] * rope_sign[:, :, None]
    return (latent_query, rope_query, latent_keys, rope_keys)


def draw_q_latent(key, part):
    fields = attention_fields(key, 0.0)
    return fields[0].astype(jnp.bfloat16)


def draw_q_rope(key, part):
    fields = attention_fields(key, 0.0)
    return fields[1].astype(jnp.bfloat16)


def draw_cache_latent(key, part):
    fields = attention_fields(key, 0.0)
    return fields[2].astype(jnp.bfloat16)


def draw_cache_rope(key, part):
    fields = attention_fields(key, 0.0)
    return fields[3].astype(jnp.bfloat16)


def draw_cache_len(key, part):
    key = jax.random.fold_in(key, 17)
    lengths = jax.random.randint(jax.random.fold_in(key, 1), (ATT_ROWS,), CTX // 4, CTX + 1)
    full_row = jax.random.randint(jax.random.fold_in(key, 2), (), 0, ATT_ROWS)
    return jnp.where(jnp.arange(ATT_ROWS) == full_row, CTX, lengths).astype(jnp.int32)


def levels(stream_key, extent, shards, least, high):
    level, own = 1.0, jax.random.fold_in(stream_key, 6)
    for dim, blocks in shards:
        heights = jnp.exp(jax.random.uniform(jax.random.fold_in(own, dim), (blocks,), jnp.float32, least / len(shards), high / len(shards)))
        level = level * jnp.repeat(heights, extent[dim] // blocks).reshape([-1 if axis == dim else 1 for axis in range(len(extent))])
    return level


def shared_out(key, own, number, rows, amount, top, most, skew):
    ranking = jax.random.permutation(key, amount)
    heavy_load, ordinary = shares(amount, rows * top, most, skew, True), shares(amount, rows * top, most, skew, False)
    places = jnp.arange(amount)

    def named(sizes, rotation):
        used = int((sizes > 0).sum())
        fixed = max(1, used // 4)
        shifted = fixed + (places - fixed + rotation * (used - fixed)) % max(1, amount - fixed)
        return jnp.zeros((amount,), jnp.int32).at[ranking[jnp.where(places < fixed, places, shifted)]].set(jnp.asarray(sizes, jnp.int32))

    sizes = jnp.where(number % 4 == 0, named(heavy_load, number // 4), named(ordinary, number - number // 4 - 1))
    mixed = jax.random.permutation(jax.random.fold_in(own, 3), amount)
    donor, sink = mixed[0:amount // 2 * 2:2], mixed[1:amount // 2 * 2:2]
    room = jnp.minimum(sizes[donor] - 1, most - sizes[sink]) // 2
    room = jnp.where((donor == ranking[0]) | (sink == ranking[0]) | (sizes[sink] == 0), 0, jnp.maximum(room, 0))
    shifted = jax.random.randint(jax.random.fold_in(own, 4), (amount // 2,), 0, 1 << 20) % (room + 1)
    sizes = sizes.at[donor].add(-shifted).at[sink].add(shifted)
    members = jnp.searchsorted(jnp.cumsum(sizes), jnp.arange(rows * top), side="right").astype(jnp.int32)
    grid = members.reshape(top, rows).T
    grid = grid[jax.random.permutation(jax.random.fold_in(own, 1), rows)]
    rotation = jax.random.randint(jax.random.fold_in(own, 2), (rows, 1), 0, top)
    return jnp.take_along_axis(grid, (jnp.arange(top)[None, :] + rotation) % top, axis=1)


def shares(amount, total, most, slope, full):
    loads = [(1 << 20) // math.isqrt(rank ** slope) + 1 for rank in range(1, amount + 1)]
    largest = most if full else min(most, max(-(-total // amount), total * loads[0] // sum(loads)))
    least = 1 if total - largest >= amount - 1 else 0
    holding, rest = [largest] + [least] * (amount - 1), total - largest - least * (amount - 1)
    while rest > 0:
        candidates = [i for i in range(1, amount) if holding[i] < largest] or [i for i in range(1, amount) if holding[i] < most]
        whole, left = sum([loads[i] for i in candidates]), rest
        for i in candidates:
            addition = min(most - holding[i], max(1, left * loads[i] // whole), rest)
            holding[i] = holding[i] + addition
            rest = rest - addition
    return np.array(holding)


def centred(stream_key, shape, deviation, reach, cuts=(), kind=jnp.bfloat16):
    drawn = jax.random.normal(stream_key, shape, jnp.float32) * deviation
    if len(cuts) > 0:
        drawn = levels(stream_key, shape, cuts, -0.22, 0.18) * drawn
    return jnp.clip(drawn, min=-reach, max=reach).astype(kind)


def setup_inputs(seed: int = 0, part: int = 0) -> dict:
    arg_keys = jax.random.split(jax.random.key(seed), 12)
    part_keys = jax.random.split(jax.random.fold_in(arg_keys[11], part), 12)
    hidden = centred(part_keys[0], (TOKENS, D), 1.0, 6.0, ((0, 4),))
    routes_keys = jax.random.split(jax.random.fold_in(part_keys[1], 1), TOKENS // TOK_DEV)
    routes_turns = jax.random.permutation(jax.random.fold_in(part_keys[1], 3), TOKENS // TOK_DEV)
    routes = jax.vmap(lambda own, number: shared_out(jax.random.fold_in(part_keys[1], 2), own, number, TOK_DEV, EXPERTS, TOP, CAP, 2))(routes_keys, routes_turns).reshape((TOKENS, TOP))
    router_weight = centred(arg_keys[2], (D, EXPERTS), (D // 4) ** -0.5, 0.1875)
    gate_weight = centred(arg_keys[3], (EXPERTS, D, FFE), D ** -0.5, 0.09375, ((0, 4), (2, 4)))
    up_weight = centred(arg_keys[4], (EXPERTS, D, FFE), D ** -0.5, 0.09375, ((0, 4), (2, 4)))
    down_weight = centred(arg_keys[5], (EXPERTS, FFE, D), FFE ** -0.5, 0.1875, ((0, 4), (1, 4)))
    q_latent = draw_q_latent(jax.random.fold_in(jax.random.fold_in(arg_keys[11], part), 71), part)
    q_rope = draw_q_rope(jax.random.fold_in(jax.random.fold_in(arg_keys[11], part), 71), part)
    cache_latent = draw_cache_latent(jax.random.fold_in(jax.random.fold_in(arg_keys[11], part), 71), part)
    cache_rope = draw_cache_rope(jax.random.fold_in(jax.random.fold_in(arg_keys[11], part), 71), part)
    cache_len = draw_cache_len(jax.random.fold_in(jax.random.fold_in(arg_keys[11], part), 71), part)
    return dict(hidden=hidden, routes=routes, router_weight=router_weight, gate_weight=gate_weight, up_weight=up_weight, down_weight=down_weight, q_latent=q_latent, q_rope=q_rope, cache_latent=cache_latent, cache_rope=cache_rope, cache_len=cache_len)


score_scale = 0.13524
route_scale = 2.5
very_low = -1.0e30


def route_weights(hidden, router_weight, routes):
    logits = jnp.dot(hidden, router_weight, preferred_element_type=jnp.float32)
    scores = jax.nn.sigmoid(logits)
    chosen = jnp.take_along_axis(scores, routes, axis=1)
    return route_scale * chosen / jnp.sum(chosen, axis=1, keepdims=True)


def mixture(hidden, routes, router_weight, gate_weight, up_weight, down_weight):
    weights = route_weights(hidden, router_weight, routes)
    limit = N_DEV * CAP

    def serve(expert):
        hit = jnp.any(routes == expert, axis=1)
        count = jnp.sum(hit.astype(jnp.int32))
        index = jnp.nonzero(hit, size=limit, fill_value=0)[0].astype(jnp.int32)
        rows = hidden[index]
        gate = jnp.dot(rows, gate_weight[expert], preferred_element_type=jnp.float32)
        up = jnp.dot(rows, up_weight[expert], preferred_element_type=jnp.float32)
        act = (jax.nn.silu(gate) * up).astype(jnp.bfloat16)
        blocks = act.reshape(limit, N_TP, FFE_BLK).astype(jnp.float32)
        down = down_weight[expert].reshape(N_TP, FFE_BLK, D).astype(jnp.float32)
        parts = jnp.einsum('lbf,bfd->lbd', blocks, down).astype(jnp.bfloat16)
        parts = lax.optimization_barrier(parts)
        summed = jnp.sum(parts.astype(jnp.float32), axis=1)
        live = jnp.arange(limit) < count
        share = jnp.sum(jnp.where(routes == expert, weights, 0.0), axis=1)[index]
        share = jnp.where(live, share, 0.0)
        return index, summed * share[:, None]

    indexes, values = lax.map(serve, jnp.arange(EXPERTS, dtype=jnp.int32))
    total = jnp.zeros((TOKENS, D), jnp.float32).at[indexes.reshape(-1)].add(values.reshape(-1, D))
    return total.astype(jnp.bfloat16)


def attention(q_latent, q_rope, cache_latent, cache_rope, cache_len):
    def one_row(items):
        query_lat, query_rot, keys_lat, keys_rot, length = items
        logits = jnp.dot(query_lat, keys_lat.T, preferred_element_type=jnp.float32)
        logits = logits + jnp.dot(query_rot.T, keys_rot, preferred_element_type=jnp.float32)
        logits = score_scale * logits
        valid = jnp.arange(CTX) < length
        logits = jnp.where(valid[None, :], logits, very_low)
        top = jnp.max(logits, axis=1, keepdims=True)
        probs = jnp.where(valid[None, :], jnp.exp(logits - top), 0.0)
        total = jnp.sum(probs, axis=1, keepdims=True)
        summed = jnp.dot(probs.astype(jnp.bfloat16), keys_lat, preferred_element_type=jnp.float32)
        return (summed / total).astype(jnp.bfloat16)

    return lax.map(one_row, (q_latent, q_rope, cache_latent, cache_rope, cache_len))


def reference(hidden, routes, router_weight, gate_weight, up_weight, down_weight, q_latent, q_rope, cache_latent, cache_rope, cache_len):
    moe_out = mixture(hidden, routes, router_weight, gate_weight, up_weight, down_weight)
    attended = attention(q_latent, q_rope, cache_latent, cache_rope, cache_len)
    return (moe_out, attended)
```

```python
import functools

import jax
import jax.numpy as jnp
from jax import lax
from jax.experimental import pallas as pl
from jax.experimental.pallas import tpu as pltpu
from jax.sharding import PartitionSpec as P

score_scale = 0.13524
route_scale = 2.5
very_low = -1e30
LANES = 128

f32, bf16 = jnp.float32, jnp.bfloat16
ANY = pl.BlockSpec(memory_space=pl.ANY)
VMEM = pl.BlockSpec(memory_space=pltpu.VMEM)
SMEM = pl.BlockSpec(memory_space=pltpu.SMEM)


def dot(a, b, contract=((1,), (0,))):
    return lax.dot_general(a, b, (contract, ((), ())), preferred_element_type=f32)


def send(value, axis, target):
    size = lax.axis_size(axis)
    return lax.ppermute(value, axis, [(i, target(i)) for i in range(size)])


def attend_kernel(place, q_lat, q_rope, keys, rope, lengths, *rest):
    outs, state = rest[:-1], rest[-1]
    parts = len(outs)
    rows, heads, width = q_lat.shape
    span = keys.shape[1]
    me = place[0]
    start = me * span
    lane = lax.broadcasted_iota(jnp.int32, (heads, LANES), 1)
    for r in range(rows):
        logits = dot(q_lat[r], keys[r], ((1,), (1,)))
        logits += dot(q_rope[r], rope[r], ((0,), (0,)))
        valid = lax.broadcasted_iota(jnp.int32, (heads, span), 1) + start < lengths[r]
        logits = jnp.where(valid, score_scale * logits, very_low)
        top = jnp.max(logits, axis=1, keepdims=True).astype(bf16).astype(f32)
        probs = jnp.where(valid, jnp.exp(logits - top), 0.0)
        total = jnp.sum(probs, axis=1, keepdims=True)
        high = total.astype(bf16).astype(f32)
        stats = jnp.where(lane == 0, top, jnp.where(lane == 1, high, jnp.where(lane == 2, total - high, 0.0)))
        state[r, :, :width] = dot(probs.astype(bf16), keys[r]).astype(bf16)
        state[r, :, width:] = stats.astype(bf16)
    block = heads // parts
    for s in range(parts):
        offset = pl.multiple_of(lax.rem(me + s, parts) * block, block)
        outs[s][...] = state[:, pl.ds(offset, block), :]


def attend(tp, q_latent, q_rope, cache_latent, cache_rope, cache_len, parts):
    rows, heads, width = q_latent.shape
    span = cache_latent.shape[1]
    shape = jax.ShapeDtypeStruct((rows, heads // parts, width + LANES), bf16)
    return pl.pallas_call(
        attend_kernel,
        out_shape=[shape] * parts,
        in_specs=[SMEM, VMEM, VMEM, VMEM, VMEM, SMEM],
        out_specs=[VMEM] * parts,
        scratch_shapes=[pltpu.VMEM((rows, heads, width + LANES), bf16)],
        cost_estimate=pl.CostEstimate(
            flops=4 * rows * heads * span * width, bytes_accessed=2 * rows * span * width, transcendentals=rows * heads * span
        ),
        compiler_params=pltpu.CompilerParams(vmem_limit_bytes=16 << 20),
    )(tp, q_latent, q_rope, cache_latent, cache_rope, cache_len)


def join_kernel(*refs):
    states, out = refs[:-1], refs[-1]
    rows, heads, width = out.shape
    for r in range(rows):
        stats = [s[r, :, width:].astype(f32) for s in states]
        tops = [t[:, 0:1] for t in stats]
        top = functools.reduce(jnp.maximum, tops)
        scales = [jnp.exp(t - top) for t in tops]
        total = sum(c * (t[:, 1:2] + t[:, 2:3]) for c, t in zip(scales, stats))
        summed = sum(c * s[r, :, :width].astype(f32) for c, s in zip(scales, states))
        out[r] = (summed / total).astype(bf16)


def join(states):
    rows, heads, width = states[0].shape
    return pl.pallas_call(
        join_kernel,
        out_shape=jax.ShapeDtypeStruct((rows, heads, width - LANES), bf16),
        in_specs=[VMEM] * len(states),
        out_specs=VMEM,
        cost_estimate=pl.CostEstimate(flops=1 << 20, bytes_accessed=1 << 20, transcendentals=1 << 10),
        compiler_params=pltpu.CompilerParams(vmem_limit_bytes=16 << 20),
    )(*states)


def place_kernel(place, *refs):
    blocks, out = refs[:-1], refs[-1]
    parts, size = len(blocks), blocks[0].shape[1]
    for s in range(parts):
        owner = lax.rem(place[0] + parts - s, parts)
        out[:, pl.ds(pl.multiple_of(owner * size, size), size), :] = blocks[s][...]


def place_heads(tp, blocks):
    rows, size, width = blocks[0].shape
    return pl.pallas_call(
        place_kernel,
        out_shape=jax.ShapeDtypeStruct((rows, size * len(blocks), width), bf16),
        in_specs=[SMEM] + [VMEM] * len(blocks),
        out_specs=VMEM,
        cost_estimate=pl.CostEstimate(flops=0, bytes_accessed=1 << 20, transcendentals=0),
        compiler_params=pltpu.CompilerParams(vmem_limit_bytes=16 << 20),
    )(tp, *blocks)


def pack_kernel(place, hidden, routes, out):
    half = hidden.shape[1] // 2
    picks, rows = routes.shape
    start = pl.multiple_of(lax.rem(place[1], 2) * half, half)
    out[:, :half] = hidden[:, pl.ds(start, half)]
    eye = lax.broadcasted_iota(jnp.int32, (rows, rows), 0) == lax.broadcasted_iota(jnp.int32, (rows, rows), 1)
    turned = dot(eye.astype(f32).astype(bf16), routes[...].astype(f32).astype(bf16), ((1,), (1,)))
    out[:, half:] = jnp.zeros((rows, LANES), bf16)
    out[:, half : half + picks] = turned.astype(bf16)


def pack_rows(place, hidden, routes):
    rows, width = hidden.shape
    return pl.pallas_call(
        pack_kernel,
        out_shape=jax.ShapeDtypeStruct((rows, width // 2 + LANES), bf16),
        in_specs=[SMEM, VMEM, VMEM],
        out_specs=VMEM,
        compiler_params=pltpu.CompilerParams(vmem_limit_bytes=16 << 20),
    )(place, hidden, routes.T)


def experts_kernel(shape, place, own, packs, halves, router, gate, up, down, outs, x, tags, g, u, w, act, sems):
    dev, tp = place[0], place[1]
    core = lax.rem(tp, 2)
    n_dev = len(packs)
    rows, width = own.shape
    half = width // 2
    local, _, hidden = gate.shape
    mine = pl.multiple_of(core * half, half)
    theirs = pl.multiple_of((1 - core) * half, half)

    def copies(e):
        return (
            pltpu.make_async_copy(gate.at[e], g.at[e], sems.at[0, e]),
            pltpu.make_async_copy(up.at[e], u.at[e], sems.at[1, e]),
        )

    def down_copy(e):
        return pltpu.make_async_copy(down.at[e], w.at[pl.ds(e * hidden, hidden), :], sems.at[2, e])

    for e in range(local):
        for copy in copies(e):
            copy.start()
    for e in range(local):
        down_copy(e).start()
    x[pl.ds(0, rows), :] = own[...]
    for s in range(n_dev):
        block = pl.ds(s * rows, rows)
        tags[block, :] = packs[s][:, half:]
        if s:
            x[block, pl.ds(mine, half)] = packs[s][:, :half]
            x[block, pl.ds(theirs, half)] = halves[s - 1][...]

    scores = jax.nn.sigmoid(dot(x[...], router[...], ((1,), (1,))))
    count = x.shape[0]
    experts = scores.shape[1]
    labels = lax.broadcasted_iota(jnp.int32, (count, experts), 1)
    chosen = tags[...].astype(f32).astype(jnp.int32)
    picked = labels < 0
    for k in range(shape):
        picked = picked | (labels == chosen[:, k : k + 1])
    kept = jnp.where(picked, scores, 0.0)
    weights = route_scale * kept / jnp.sum(kept, axis=1, keepdims=True)

    def expert(e, carry):
        for copy in copies(e):
            copy.wait()
        rate = jnp.sum(jnp.where(labels == dev * local + e, weights, 0.0), axis=1, keepdims=True)
        a = dot(x[...], g[e])
        b = dot(x[...], u[e])
        value = a / (1.0 + jnp.exp(-a)) * b * rate
        act[:, pl.ds(pl.multiple_of(e * hidden, hidden), hidden)] = value.astype(bf16)
        return carry

    lax.fori_loop(0, local, expert, 0)
    for e in range(local):
        down_copy(e).wait()
    if len(outs) == 1:
        outs[0][...] = dot(act[...], w[...]).astype(bf16)
        return
    ways = len(outs) // 2
    size = outs[0].shape[1]
    spot = tp // 2
    for i, out in enumerate(outs):
        side = 1 - core if i < ways else core
        owner = lax.rem(spot + i % ways, ways) * 2 + side
        start = pl.multiple_of(owner * size, size)
        out[...] = dot(act[...], w[:, pl.ds(start, size)]).astype(bf16)


def experts_call(place, own, packs, halves, router, gate, up, down, picks, n_tp):
    rows, width = own.shape
    n_dev = len(packs)
    local, _, hidden = gate.shape
    count = rows * n_dev
    n_in = 1 + len(packs) + len(halves)

    def kernel(place, *refs):
        own, rest = refs[0], refs[1:]
        packs, rest = rest[:n_dev], rest[n_dev:]
        halves, rest = rest[: n_dev - 1], rest[n_dev - 1 :]
        router, gate, up, down = rest[:4]
        outs, scratch = rest[4 : 4 + n_out], rest[4 + n_out :]
        experts_kernel(picks, place, own, packs, halves, router, gate, up, down, outs, *scratch)

    size = width // n_tp
    n_out = n_tp if size % LANES == 0 else 1
    shape = jax.ShapeDtypeStruct((count, width // n_out), bf16)
    parts = pl.pallas_call(
        kernel,
        out_shape=[shape] * n_out,
        in_specs=[SMEM] + [VMEM] * n_in + [VMEM] + [ANY] * 3,
        out_specs=[VMEM] * n_out,
        scratch_shapes=[
            pltpu.VMEM((count, width), bf16),
            pltpu.VMEM((count, LANES), bf16),
            pltpu.VMEM(gate.shape, bf16),
            pltpu.VMEM(up.shape, bf16),
            pltpu.VMEM((local * hidden, width), bf16),
            pltpu.VMEM((count, local * hidden), bf16),
            pltpu.SemaphoreType.DMA((3, local)),
        ],
        cost_estimate=pl.CostEstimate(
            flops=6 * count * local * hidden * width, bytes_accessed=6 * local * hidden * width, transcendentals=0
        ),
        compiler_params=pltpu.CompilerParams(vmem_limit_bytes=56 << 20),
    )(place, own, *packs, *halves, router, gate, up, down)
    if n_out == n_tp:
        return parts
    ways = n_tp // 2
    spot, core = place[1] // 2, place[1] % 2
    owners = [((spot + i) % ways) * 2 + side for side in (1 - core, core) for i in range(ways)]
    return [lax.dynamic_slice_in_dim(parts[0], owner * size, size, 1) for owner in owners]


def on_device(
    hidden,
    routes,
    router_weight,
    gate_weight,
    up_weight,
    down_weight,
    q_latent,
    q_rope,
    cache_latent,
    cache_rope,
    cache_len,
):
    rows, width = hidden.shape
    n_dev, n_tp = lax.axis_size("dev"), lax.axis_size("tp")
    ways = n_tp // 2
    dev, tp = lax.axis_index("dev"), lax.axis_index("tp")
    half = width // 2
    place = jnp.stack([dev, tp]).astype(jnp.int32)
    here = tp.reshape(1).astype(jnp.int32)

    def other_core(i):
        return i ^ 1

    def along_x(s):
        return lambda i: ((i // 2 + s) % ways) * 2 + i % 2

    pack = pack_rows(place, hidden, routes)
    packs = [pack] + [send(pack, "dev", lambda i: (i + s) % n_dev) for s in range(1, n_dev)]
    halves = [send(p[:, :half], "tp", other_core) for p in packs[1:]]

    states = attend(here, q_latent, q_rope, cache_latent, cache_rope, cache_len, n_tp)
    halves, states = lax.optimization_barrier((halves, states))
    parts = experts_call(place, hidden, packs, halves, router_weight.T, gate_weight, up_weight, down_weight, routes.shape[1], n_tp)
    states = [states[0]] + [send(states[s], "tp", lambda i: (i + s) % n_tp) for s in range(1, n_tp)]
    joined = join(states)
    blocks = [joined] + [send(joined, "tp", lambda i: (i + s) % n_tp) for s in range(1, n_tp)]
    attended = place_heads(here, blocks)

    got = [send(p, "tp", other_core) for p in parts[:ways]]
    sums = [(a.astype(f32) + b.astype(f32)) for a, b in zip(got, parts[ways:])]
    total = sums[0]
    for s in range(1, ways):
        total = total + send(sums[s].astype(bf16), "tp", along_x(s)).astype(f32)
    total = total.reshape(n_dev, rows, -1)
    moe = total[0]
    for s in range(1, n_dev):
        moe = moe + send(total[s].astype(bf16), "dev", lambda i: (i - s) % n_dev).astype(f32)
    return (moe.astype(bf16), attended)


def solution(mesh):
    in_specs = (
        P(("group", "dev"), None),
        P(("group", "dev"), None),
        P(),
        P("dev", None, "tp"),
        P("dev", None, "tp"),
        P("dev", "tp", None),
        P(("group", "dev"), None, None),
        P(("group", "dev"), None, None),
        P(("group", "dev"), "tp", None),
        P(("group", "dev"), None, "tp"),
        P(("group", "dev")),
    )
    out_specs = (P(("group", "dev"), "tp"), P(("group", "dev"), None, None))
    return jax.shard_map(
        on_device, mesh=mesh, in_specs=in_specs, out_specs=out_specs, check_vma=False
    )
```

```python
import functools

import jax
import jax.numpy as jnp
from jax import lax
from jax.experimental import pallas as pl
from jax.experimental.pallas import tpu as pltpu
from jax.sharding import PartitionSpec as P

score_scale = 0.13524
route_scale = 2.5
very_low = -1e30
LANES = 128
WAIT_FLOPS = 20_000_000_000

f32, bf16 = jnp.float32, jnp.bfloat16
ANY = pl.BlockSpec(memory_space=pl.ANY)
VMEM = pl.BlockSpec(memory_space=pltpu.VMEM)
SMEM = pl.BlockSpec(memory_space=pltpu.SMEM)


def dot(a, b, contract=((1,), (0,))):
    return lax.dot_general(a, b, (contract, ((), ())), preferred_element_type=f32)


def send(value, axis, target):
    size = lax.axis_size(axis)
    return lax.ppermute(value, axis, [(i, target(i)) for i in range(size)])


def attend_kernel(q_lat, q_rope, keys, rope, lengths, *rest):
    outs, state = rest[:-1], rest[-1]
    parts = len(outs)
    rows, heads, width = q_lat.shape
    span = keys.shape[1]
    me = lax.axis_index("tp")
    start = me * span
    lane = lax.broadcasted_iota(jnp.int32, (heads, LANES), 1)
    for r in range(rows):
        logits = dot(q_lat[r], keys[r], ((1,), (1,)))
        logits += dot(q_rope[r], rope[r], ((0,), (0,)))
        valid = lax.broadcasted_iota(jnp.int32, (heads, span), 1) + start < lengths[r]
        logits = jnp.where(valid, score_scale * logits, very_low)
        top = jnp.max(logits, axis=1, keepdims=True).astype(bf16).astype(f32)
        probs = jnp.where(valid, jnp.exp(logits - top), 0.0)
        total = jnp.sum(probs, axis=1, keepdims=True)
        high = total.astype(bf16).astype(f32)
        stats = jnp.where(lane == 0, top, jnp.where(lane == 1, high, jnp.where(lane == 2, total - high, 0.0)))
        state[r, :, :width] = dot(probs.astype(bf16), keys[r]).astype(bf16)
        state[r, :, width:] = stats.astype(bf16)
    block = heads // parts
    for s in range(parts):
        offset = pl.multiple_of(lax.rem(me + s, parts) * block, block)
        outs[s][...] = state[:, pl.ds(offset, block), :]


def attend(q_latent, q_rope, cache_latent, cache_rope, cache_len, parts):
    rows, heads, width = q_latent.shape
    span = cache_latent.shape[1]
    shape = jax.ShapeDtypeStruct((rows, heads // parts, width + LANES), bf16)
    return pl.pallas_call(
        attend_kernel,
        out_shape=[shape] * parts,
        in_specs=[VMEM, VMEM, VMEM, VMEM, SMEM],
        out_specs=[VMEM] * parts,
        scratch_shapes=[pltpu.VMEM((rows, heads, width + LANES), bf16)],
        cost_estimate=pl.CostEstimate(
            flops=4 * rows * heads * span * width, bytes_accessed=2 * rows * span * width, transcendentals=rows * heads * span
        ),
        compiler_params=pltpu.CompilerParams(vmem_limit_bytes=8 << 20),
    )(q_latent, q_rope, cache_latent, cache_rope, cache_len)


def join_kernel(*refs):
    states, out = refs[:-1], refs[-1]
    rows, heads, width = out.shape
    for r in range(rows):
        stats = [s[r, :, width:].astype(f32) for s in states]
        tops = [t[:, 0:1] for t in stats]
        top = functools.reduce(jnp.maximum, tops)
        scales = [jnp.exp(t - top) for t in tops]
        total = sum(c * (t[:, 1:2] + t[:, 2:3]) for c, t in zip(scales, stats))
        summed = sum(c * s[r, :, :width].astype(f32) for c, s in zip(scales, states))
        out[r] = (summed / total).astype(bf16)


def join(states):
    rows, heads, width = states[0].shape
    return pl.pallas_call(
        join_kernel,
        out_shape=jax.ShapeDtypeStruct((rows, heads, width - LANES), bf16),
        in_specs=[VMEM] * len(states),
        out_specs=VMEM,
        cost_estimate=pl.CostEstimate(flops=1 << 20, bytes_accessed=1 << 20, transcendentals=1 << 10),
        compiler_params=pltpu.CompilerParams(vmem_limit_bytes=8 << 20),
    )(*states)


def place_kernel(*refs):
    blocks, out = refs[:-1], refs[-1]
    parts, size = len(blocks), blocks[0].shape[1]
    for s in range(parts):
        owner = lax.rem(lax.axis_index("tp") + parts - s, parts)
        out[:, pl.ds(pl.multiple_of(owner * size, size), size), :] = blocks[s][...]


def place_heads(blocks):
    rows, size, width = blocks[0].shape
    return pl.pallas_call(
        place_kernel,
        out_shape=jax.ShapeDtypeStruct((rows, size * len(blocks), width), bf16),
        in_specs=[VMEM] * len(blocks),
        out_specs=VMEM,
        cost_estimate=pl.CostEstimate(flops=0, bytes_accessed=1 << 20, transcendentals=0),
        compiler_params=pltpu.CompilerParams(vmem_limit_bytes=8 << 20),
    )(*blocks)


def pack_kernel(hidden, routes, out, tags, sems):
    half = hidden.shape[1] // 2
    picks, rows = routes.shape
    start = pl.multiple_of(lax.rem(lax.axis_index("tp"), 2) * half, half)
    columns = pltpu.make_async_copy(hidden.at[:, pl.ds(start, half)], out.at[:, pl.ds(0, half)], sems.at[0])
    named = pltpu.make_async_copy(routes, tags, sems.at[1])
    columns.start()
    named.start()
    out[:, half:] = jnp.zeros((rows, LANES), bf16)
    named.wait()
    eye = lax.broadcasted_iota(jnp.int32, (rows, rows), 0) == lax.broadcasted_iota(jnp.int32, (rows, rows), 1)
    turned = dot(eye.astype(f32).astype(bf16), tags[...].astype(f32).astype(bf16), ((1,), (1,)))
    out[:, half : half + picks] = turned.astype(bf16)
    columns.wait()


def pack_rows(hidden, routes):
    rows, width = hidden.shape
    operands = [pltpu.with_memory_space_constraint(a, pltpu.HBM) for a in (hidden, routes.T)]
    return pl.pallas_call(
        pack_kernel,
        out_shape=jax.ShapeDtypeStruct((rows, width // 2 + LANES), bf16),
        in_specs=[ANY, ANY],
        out_specs=VMEM,
        scratch_shapes=[pltpu.VMEM(routes.shape[::-1], jnp.int32), pltpu.SemaphoreType.DMA((2,))],
        cost_estimate=pl.CostEstimate(flops=WAIT_FLOPS, bytes_accessed=1 << 18, transcendentals=0),
        compiler_params=pltpu.CompilerParams(vmem_limit_bytes=2 << 20),
    )(*operands)


def experts_kernel(shape, own, packs, halves, router, gate, up, down, outs, x, tags, act):
    dev, tp = lax.axis_index("dev"), lax.axis_index("tp")
    core = lax.rem(tp, 2)
    n_dev = len(packs)
    rows, width = own.shape
    half = width // 2
    local, _, hidden = gate.shape
    mine = pl.multiple_of(core * half, half)
    theirs = pl.multiple_of((1 - core) * half, half)

    x[pl.ds(0, rows), :] = own[...]
    for s in range(n_dev):
        block = pl.ds(s * rows, rows)
        tags[block, :] = packs[s][:, half:]
        if s:
            x[block, pl.ds(mine, half)] = packs[s][:, :half]
            x[block, pl.ds(theirs, half)] = halves[s - 1][...]

    scores = jax.nn.sigmoid(dot(x[...], router[...], ((1,), (1,))))
    count = x.shape[0]
    experts = scores.shape[1]
    labels = lax.broadcasted_iota(jnp.int32, (count, experts), 1)
    chosen = tags[...].astype(f32).astype(jnp.int32)
    picked = labels < 0
    for k in range(shape):
        picked = picked | (labels == chosen[:, k : k + 1])
    kept = jnp.where(picked, scores, 0.0)
    weights = route_scale * kept / jnp.sum(kept, axis=1, keepdims=True)

    def expert(e, carry):
        rate = jnp.sum(jnp.where(labels == dev * local + e, weights, 0.0), axis=1, keepdims=True)
        a = dot(x[...], gate[e])
        b = dot(x[...], up[e])
        value = a / (1.0 + jnp.exp(-a)) * b * rate
        act[:, pl.ds(pl.multiple_of(e * hidden, hidden), hidden)] = value.astype(bf16)
        return carry

    lax.fori_loop(0, local, expert, 0)
    if len(outs) == 1:
        outs[0][...] = dot(act[...], down[...]).astype(bf16)
        return
    ways = len(outs) // 2
    size = outs[0].shape[1]
    spot = tp // 2
    for i, out in enumerate(outs):
        side = 1 - core if i < ways else core
        owner = lax.rem(spot + i % ways, ways) * 2 + side
        start = pl.multiple_of(owner * size, size)
        out[...] = dot(act[...], down[:, pl.ds(start, size)]).astype(bf16)


def experts_call(own, packs, halves, router, gate, up, down, picks, n_tp):
    rows, width = own.shape
    n_dev = len(packs)
    local, _, hidden = gate.shape
    count = rows * n_dev
    n_in = 1 + len(packs) + len(halves)

    def kernel(*refs):
        own, rest = refs[0], refs[1:]
        packs, rest = rest[:n_dev], rest[n_dev:]
        halves, rest = rest[: n_dev - 1], rest[n_dev - 1 :]
        router, gate, up, down = rest[:4]
        outs, scratch = rest[4 : 4 + n_out], rest[4 + n_out :]
        experts_kernel(picks, own, packs, halves, router, gate, up, down, outs, *scratch)

    size = width // n_tp
    n_out = n_tp if size % LANES == 0 else 1
    shape = jax.ShapeDtypeStruct((count, width // n_out), bf16)
    parts = pl.pallas_call(
        kernel,
        out_shape=[shape] * n_out,
        in_specs=[VMEM] * n_in + [VMEM] + [VMEM] * 3,
        out_specs=[VMEM] * n_out,
        scratch_shapes=[
            pltpu.VMEM((count, width), bf16),
            pltpu.VMEM((count, LANES), bf16),
            pltpu.VMEM((count, local * hidden), bf16),
        ],
        cost_estimate=pl.CostEstimate(
            flops=6 * count * local * hidden * width, bytes_accessed=6 * local * hidden * width, transcendentals=0
        ),
        compiler_params=pltpu.CompilerParams(vmem_limit_bytes=(10 if count <= 256 else 48) << 20),
    )(own, *packs, *halves, router, *[pltpu.with_memory_space_constraint(w, pltpu.VMEM) for w in (gate, up, down.reshape(local * hidden, width))])
    if n_out == n_tp:
        return parts
    ways = n_tp // 2
    spot, core = lax.axis_index("tp") // 2, lax.axis_index("tp") % 2
    owners = [((spot + i) % ways) * 2 + side for side in (1 - core, core) for i in range(ways)]
    return [lax.dynamic_slice_in_dim(parts[0], owner * size, size, 1) for owner in owners]


def on_device(
    hidden,
    routes,
    router_weight,
    gate_weight,
    up_weight,
    down_weight,
    q_latent,
    q_rope,
    cache_latent,
    cache_rope,
    cache_len,
):
    rows, width = hidden.shape
    n_dev, n_tp = lax.axis_size("dev"), lax.axis_size("tp")
    ways = n_tp // 2
    half = width // 2

    def other_core(i):
        return i ^ 1

    def along_x(s):
        return lambda i: ((i // 2 + s) % ways) * 2 + i % 2

    pack = pack_rows(hidden, routes)
    pack, q_latent = lax.optimization_barrier((pack, q_latent))
    packs = [pack] + [send(pack, "dev", lambda i: (i + s) % n_dev) for s in range(1, n_dev)]
    halves = [send(p[:, :half], "tp", other_core) for p in packs[1:]]

    states = attend(q_latent, q_rope, cache_latent, cache_rope, cache_len, n_tp)
    states = [states[0]] + [send(states[s], "tp", lambda i: (i + s) % n_tp) for s in range(1, n_tp)]
    joined = join(states)
    blocks = [joined] + [send(joined, "tp", lambda i: (i + s) % n_tp) for s in range(1, n_tp)]
    halves, blocks = lax.optimization_barrier((halves, blocks))
    parts = experts_call(hidden, packs, halves, router_weight.T, gate_weight, up_weight, down_weight, routes.shape[1], n_tp)
    got = [send(p, "tp", other_core) for p in parts[:ways]]
    sums = [(a.astype(f32) + b.astype(f32)) for a, b in zip(got, parts[ways:])]
    total = sums[0]
    for s in range(1, ways):
        total = total + send(sums[s].astype(bf16), "tp", along_x(s)).astype(f32)
    total = total.reshape(n_dev, rows, -1)
    moe = total[0]
    for s in range(1, n_dev):
        moe = moe + send(total[s].astype(bf16), "dev", lambda i: (i - s) % n_dev).astype(f32)
    return (moe.astype(bf16), place_heads(blocks))


def solution(mesh):
    in_specs = (
        P(("group", "dev"), None),
        P(("group", "dev"), None),
        P(),
        P("dev", None, "tp"),
        P("dev", None, "tp"),
        P("dev", "tp", None),
        P(("group", "dev"), None, None),
        P(("group", "dev"), None, None),
        P(("group", "dev"), "tp", None),
        P(("group", "dev"), None, "tp"),
        P(("group", "dev")),
    )
    out_specs = (P(("group", "dev"), "tp"), P(("group", "dev"), None, None))
    return jax.shard_map(
        on_device, mesh=mesh, in_specs=in_specs, out_specs=out_specs, check_vma=False
    )
```

```python
import functools

import jax
import jax.numpy as jnp
from jax import lax
from jax.experimental import pallas as pl
from jax.experimental.pallas import tpu as pltpu
from jax.sharding import PartitionSpec as P

score_scale = 0.13524
route_scale = 2.5
very_low = -1e30
LANES = 128
WAIT_FLOPS = 20_000_000_000

f32, bf16 = jnp.float32, jnp.bfloat16
ANY = pl.BlockSpec(memory_space=pl.ANY)
VMEM = pl.BlockSpec(memory_space=pltpu.VMEM)
SMEM = pl.BlockSpec(memory_space=pltpu.SMEM)


def dot(a, b, contract=((1,), (0,))):
    return lax.dot_general(a, b, (contract, ((), ())), preferred_element_type=f32)


def send(value, axis, target):
    size = lax.axis_size(axis)
    return lax.ppermute(value, axis, [(i, target(i)) for i in range(size)])


def other_core(i):
    return i ^ 1


def along_x(shift, ways):
    return lambda i: ((i // 2 + shift) % ways) * 2 + i % 2


def spot_and_core():
    tp = lax.axis_index("tp")
    return tp // 2, lax.rem(tp, 2)


def local_call(kernel, outs, operands, specs, scratch=(), flops=0, nbytes=0, exps=0, limit=8):
    return pl.pallas_call(
        kernel,
        out_shape=outs,
        in_specs=specs,
        out_specs=jax.tree.map(lambda _: VMEM, outs),
        scratch_shapes=list(scratch),
        cost_estimate=pl.CostEstimate(flops=flops, bytes_accessed=nbytes, transcendentals=exps),
        compiler_params=pltpu.CompilerParams(vmem_limit_bytes=limit << 20),
    )(*operands)


def shaped(*shape):
    return jax.ShapeDtypeStruct(shape, bf16)


def stats_of(top, total, heads):
    lane = lax.broadcasted_iota(jnp.int32, (heads, LANES), 1)
    high = total.astype(bf16).astype(f32)
    stats = jnp.where(lane == 0, top, jnp.where(lane == 1, high, jnp.where(lane == 2, total - high, 0.0)))
    return stats.astype(bf16)


def attend_kernel(q_lat, q_rope, keys, rope, lengths, keep, give, state):
    rows, heads, width = q_lat.shape
    span = keys.shape[1]
    start = lax.axis_index("tp") * span
    for r in range(rows):
        logits = dot(q_lat[r], keys[r], ((1,), (1,)))
        logits += dot(q_rope[r], rope[r], ((0,), (0,)))
        valid = lax.broadcasted_iota(jnp.int32, (heads, span), 1) + start < lengths[r]
        logits = jnp.where(valid, score_scale * logits, very_low)
        top = jnp.max(logits, axis=1, keepdims=True).astype(bf16).astype(f32)
        probs = jnp.where(valid, jnp.exp(logits - top), 0.0)
        total = jnp.sum(probs, axis=1, keepdims=True)
        state[r, :, :width] = dot(probs.astype(bf16), keys[r]).astype(bf16)
        state[r, :, width:] = stats_of(top, total, heads)
    half = heads // 2
    core = lax.rem(lax.axis_index("tp"), 2)
    keep[...] = state[:, pl.ds(pl.multiple_of(core * half, half), half), :]
    give[...] = state[:, pl.ds(pl.multiple_of((1 - core) * half, half), half), :]


def attend(q_latent, q_rope, cache_latent, cache_rope, cache_len):
    rows, heads, width = q_latent.shape
    span = cache_latent.shape[1]
    half = shaped(rows, heads // 2, width + LANES)
    return local_call(
        attend_kernel,
        [half, half],
        [q_latent, q_rope, cache_latent, cache_rope, cache_len],
        [VMEM, VMEM, VMEM, VMEM, SMEM],
        [pltpu.VMEM((rows, heads, width + LANES), bf16)],
        flops=2_000_000_000,
    )


def join_kernel(last, *refs):
    states, out = refs[:-1], refs[-1]
    rows, heads, full = states[0].shape
    width = full - LANES
    for r in range(rows):
        stats = [s[r, :, width:].astype(f32) for s in states]
        tops = [t[:, 0:1] for t in stats]
        top = functools.reduce(jnp.maximum, tops)
        scales = [jnp.exp(t - top) for t in tops]
        total = sum(c * (t[:, 1:2] + t[:, 2:3]) for c, t in zip(scales, stats))
        summed = sum(c * s[r, :, :width].astype(f32) for c, s in zip(scales, states))
        if last:
            out[r] = (summed / total).astype(bf16)
        else:
            out[r, :, :width] = summed.astype(bf16)
            out[r, :, width:] = stats_of(top, total, heads)


def join(states, last):
    rows, heads, width = states[0].shape
    out = shaped(rows, heads, width - LANES if last else width)
    return local_call(functools.partial(join_kernel, last), out, states, [VMEM] * len(states))


def place_kernel(mine, theirs, out):
    half = mine.shape[1]
    core = lax.rem(lax.axis_index("tp"), 2)
    out[:, pl.ds(pl.multiple_of(core * half, half), half), :] = mine[...]
    out[:, pl.ds(pl.multiple_of((1 - core) * half, half), half), :] = theirs[...]


def place_heads(mine, theirs):
    rows, half, width = mine.shape
    return local_call(place_kernel, shaped(rows, 2 * half, width), [mine, theirs], [VMEM, VMEM])


def pack_kernel(spots, hidden, routes, out, tags, sems):
    size = out.shape[1] - LANES
    picks, rows = routes.shape
    spot, core = spot_and_core()
    start = pl.multiple_of((spot * 2 + core if spots > 1 else core) * size, size)
    columns = pltpu.make_async_copy(hidden.at[:, pl.ds(start, size)], out.at[:, pl.ds(0, size)], sems.at[0])
    named = pltpu.make_async_copy(routes, tags, sems.at[1])
    columns.start()
    named.start()
    out[:, size:] = jnp.zeros((rows, LANES), bf16)
    named.wait()
    eye = lax.broadcasted_iota(jnp.int32, (rows, rows), 0) == lax.broadcasted_iota(jnp.int32, (rows, rows), 1)
    turned = dot(eye.astype(f32).astype(bf16), tags[...].astype(f32).astype(bf16), ((1,), (1,)))
    out[:, size : size + picks] = turned.astype(bf16)
    columns.wait()


def pack_rows(hidden, routes, spots):
    rows, width = hidden.shape
    return local_call(
        functools.partial(pack_kernel, spots),
        shaped(rows, width // (2 * spots) + LANES),
        [pltpu.with_memory_space_constraint(a, pltpu.HBM) for a in (hidden, routes.T)],
        [ANY, ANY],
        [pltpu.VMEM(routes.shape[::-1], jnp.int32), pltpu.SemaphoreType.DMA((2,))],
        flops=WAIT_FLOPS,
        limit=2,
    )


def act_kernel(picks, ways, packs, own, mine, theirs, router, gate, up, down, act, outs, x, tags):
    rows = own.shape[0]
    spots = len(mine)
    size = mine[0].shape[1]
    local, _, hidden = gate.shape
    spot, core = spot_and_core()
    x[pl.ds(0, rows), :] = own[...]
    later = pl.ds(rows, mine[0].shape[0])
    for s in range(spots):
        first = lax.rem(spot + ways - s, ways) * 2 if spots > 1 else 0
        x[later, pl.ds(pl.multiple_of((first + core) * size, size), size)] = mine[s][...]
        x[later, pl.ds(pl.multiple_of((first + 1 - core) * size, size), size)] = theirs[s][...]
    for s, pack in enumerate(packs):
        tags[pl.ds(s * rows, rows), :] = pack[:, size:]

    scores = jax.nn.sigmoid(dot(x[...], router[...], ((1,), (1,))))
    labels = lax.broadcasted_iota(jnp.int32, scores.shape, 1)
    chosen = tags[...].astype(f32).astype(jnp.int32)
    picked = labels < 0
    for k in range(picks):
        picked = picked | (labels == chosen[:, k : k + 1])
    kept = jnp.where(picked, scores, 0.0)
    weights = route_scale * kept / jnp.sum(kept, axis=1, keepdims=True)
    first = lax.axis_index("dev") * local

    for e in range(local):
        rate = jnp.sum(jnp.where(labels == first + e, weights, 0.0), axis=1, keepdims=True)
        a = dot(x[...], gate[e])
        b = dot(x[...], up[e])
        act[:, e * hidden : (e + 1) * hidden] = (a / (1.0 + jnp.exp(-a)) * b * rate).astype(bf16)
    for out in outs:
        out[...] = dot(act[...], down[0][...]).astype(bf16)


def act_call(packs, own, mine, theirs, router, gate, up, down, picks, ways, whole):
    rows, width = own.shape
    local, _, hidden = gate.shape
    count = rows * len(packs)
    down = [down] if whole else []
    cuts = [len(packs), 1, len(mine), len(theirs), 3, len(down)]

    def kernel(*refs):
        groups = []
        for cut in cuts:
            groups.append(refs[:cut])
            refs = refs[cut:]
        packs, (own,), mine, theirs, (router, gate, up), down = groups
        act_kernel(picks, ways, packs, own, mine, theirs, router, gate, up, down, refs[0], refs[1:-2], *refs[-2:])

    parts = [shaped(count, width)] if whole else []
    operands = [*packs, own, *mine, *theirs, router, gate, up, *down]
    return local_call(
        kernel,
        [pltpu.VMEM((count, local * hidden), bf16)] + parts,
        operands,
        [VMEM] * len(operands),
        [pltpu.VMEM((count, width), bf16), pltpu.VMEM((count, LANES), bf16)],
        flops=4 * count * local * hidden * width,
        limit=10 if count <= 256 else 48,
    )


def down_call(act, down, pairs, ways):
    count, depth = act.shape
    width = down.shape[1]

    def kernel(act, down, *outs):
        spot, core = spot_and_core()
        for out, (shift, side) in zip(outs, pairs):
            size = out.shape[1]
            owner = lax.rem(spot + shift, ways) * 2 + (1 - core if side else core)
            out[...] = dot(act[...], down[:, pl.ds(pl.multiple_of(owner * size, size), size)]).astype(bf16)

    return local_call(
        kernel,
        [shaped(count, width // (2 * ways))] * len(pairs),
        [act, down],
        [VMEM, VMEM],
        flops=2 * count * depth * (width // (2 * ways)) * len(pairs),
    )


def on_device(
    hidden,
    routes,
    router_weight,
    gate_weight,
    up_weight,
    down_weight,
    q_latent,
    q_rope,
    cache_latent,
    cache_rope,
    cache_len,
):
    rows, width = hidden.shape
    local, _, units = gate_weight.shape
    n_dev, n_tp = lax.axis_size("dev"), lax.axis_size("tp")
    ways = n_tp // 2
    aligned = width % (n_tp * LANES) == 0
    spots = ways if aligned else 1
    share = width // (2 * spots)

    pack = pack_rows(hidden, routes, spots)
    packs = [pack] + [send(pack, "dev", lambda i: (i + s) % n_dev) for s in range(1, n_dev)]
    packs[1], q_latent = lax.optimization_barrier((packs[1], q_latent))
    near = jnp.concatenate([p[:, :share] for p in packs[1:]], axis=0)
    mine = [near] + [send(near, "tp", along_x(s, ways)) for s in range(1, spots)]
    theirs = [send(near, "tp", other_core)]

    keep, give = attend(q_latent, q_rope, cache_latent, cache_rope, cache_len)
    mine[1:], keep, give = lax.optimization_barrier((mine[1:], keep, give))
    theirs += [send(m, "tp", other_core) for m in mine[1:]]
    state = join([keep, send(give, "tp", other_core)], False)
    theirs, state = lax.optimization_barrier((theirs, state))
    states = [state] + [send(state, "tp", along_x(s, ways)) for s in range(1, ways)]

    gate, up, down = [
        pltpu.with_memory_space_constraint(w, pltpu.VMEM)
        for w in (gate_weight, up_weight, down_weight.reshape(local * units, width))
    ]
    act, *parts = act_call(
        packs, hidden, mine, theirs, router_weight.T, gate, up, down, routes.shape[1], ways, not aligned
    )
    act, states = lax.optimization_barrier((act, states))
    if aligned:
        shifts = range(1, ways)
        far = [send(p, "tp", other_core) for p in down_call(act, down, [(s, 1) for s in shifts], ways)]
        *own, there = down_call(act, down, [(s, 0) for s in shifts] + [(0, 1)], ways)
        there = send(there, "tp", other_core)
        sums = [(a.astype(f32) + b.astype(f32)).astype(bf16) for a, b in zip(own, far)]
        act, sums = lax.optimization_barrier((act, sums))
        (here,) = down_call(act, down, [(0, 0)], ways)
        total = here.astype(f32) + there.astype(f32)
    else:
        spot, core = spot_and_core()
        size = width // n_tp

        def block(shift, side):
            return lax.dynamic_slice_in_dim(parts[0], ((spot + shift) % ways * 2 + side) * size, size, 1)

        both = [
            block(s, core).astype(f32) + send(block(s, 1 - core), "tp", other_core).astype(f32) for s in range(ways)
        ]
        total, sums = both[0], [b.astype(bf16) for b in both[1:]]
    for s in range(1, ways):
        total = total + send(sums[s - 1], "tp", along_x(s, ways)).astype(f32)
    total = total.reshape(n_dev, rows, -1)
    moe = total[0]
    for s in range(1, n_dev):
        moe = moe + send(total[s].astype(bf16), "dev", lambda i: (i - s) % n_dev).astype(f32)
    joined = join(states, True)
    attended = place_heads(joined, send(joined, "tp", other_core))
    return (moe.astype(bf16), attended)


def solution(mesh):
    in_specs = (
        P(("group", "dev"), None),
        P(("group", "dev"), None),
        P(),
        P("dev", None, "tp"),
        P("dev", None, "tp"),
        P("dev", "tp", None),
        P(("group", "dev"), None, None),
        P(("group", "dev"), None, None),
        P(("group", "dev"), "tp", None),
        P(("group", "dev"), None, "tp"),
        P(("group", "dev")),
    )
    out_specs = (P(("group", "dev"), "tp"), P(("group", "dev"), None, None))
    return jax.shard_map(
        on_device, mesh=mesh, in_specs=in_specs, out_specs=out_specs, check_vma=False
    )
```

```python
import functools

import jax
import jax.numpy as jnp
from jax import lax
from jax.experimental import pallas as pl
from jax.experimental.pallas import tpu as pltpu
from jax.sharding import PartitionSpec as P

score_scale = 0.13524
route_scale = 2.5
very_low = -1e30
LANES = 128
WAIT_FLOPS = 20_000_000_000

f32, bf16 = jnp.float32, jnp.bfloat16
ANY = pl.BlockSpec(memory_space=pl.ANY)
VMEM = pl.BlockSpec(memory_space=pltpu.VMEM)
SMEM = pl.BlockSpec(memory_space=pltpu.SMEM)


def dot(a, b, contract=((1,), (0,))):
    return lax.dot_general(a, b, (contract, ((), ())), preferred_element_type=f32)


def send(value, axis, target):
    size = lax.axis_size(axis)
    return lax.ppermute(value, axis, [(i, target(i)) for i in range(size)])


def other_core(i):
    return i ^ 1


def partner(place, step, size):
    return place ^ step if size & (size - 1) == 0 else (step - place) % size


def along_x(step, ways):
    return lambda i: partner(i // 2, step, ways) * 2 + i % 2


def over_dev(value, step, size):
    return send(value, "dev", lambda i: partner(i, step, size))


def spot_and_core():
    tp = lax.axis_index("tp")
    return tp // 2, lax.rem(tp, 2)


def local_call(kernel, outs, operands, specs, scratch=(), flops=0, nbytes=0, exps=0, limit=8):
    return pl.pallas_call(
        kernel,
        out_shape=outs,
        in_specs=specs,
        out_specs=jax.tree.map(lambda _: VMEM, outs),
        scratch_shapes=list(scratch),
        cost_estimate=pl.CostEstimate(flops=flops, bytes_accessed=nbytes, transcendentals=exps),
        compiler_params=pltpu.CompilerParams(vmem_limit_bytes=limit << 20),
    )(*operands)


def shaped(*shape):
    return jax.ShapeDtypeStruct(shape, bf16)


def stats_of(top, total, heads):
    lane = lax.broadcasted_iota(jnp.int32, (heads, LANES), 1)
    high = total.astype(bf16).astype(f32)
    stats = jnp.where(lane == 0, top, jnp.where(lane == 1, high, jnp.where(lane == 2, total - high, 0.0)))
    return stats.astype(bf16)


def attend_kernel(q_lat, q_rope, keys, rope, lengths, keep, give, state):
    rows, heads, width = q_lat.shape
    span = keys.shape[1]
    start = lax.axis_index("tp") * span
    for r in range(rows):
        logits = dot(q_lat[r], keys[r], ((1,), (1,)))
        logits += dot(q_rope[r], rope[r], ((0,), (0,)))
        valid = lax.broadcasted_iota(jnp.int32, (heads, span), 1) + start < lengths[r]
        logits = jnp.where(valid, score_scale * logits, very_low)
        top = jnp.max(logits, axis=1, keepdims=True).astype(bf16).astype(f32)
        probs = jnp.where(valid, jnp.exp(logits - top), 0.0)
        total = jnp.sum(probs, axis=1, keepdims=True)
        state[r, :, :width] = dot(probs.astype(bf16), keys[r]).astype(bf16)
        state[r, :, width:] = stats_of(top, total, heads)
    half = heads // 2
    core = lax.rem(lax.axis_index("tp"), 2)
    keep[...] = state[:, pl.ds(pl.multiple_of(core * half, half), half), :]
    give[...] = state[:, pl.ds(pl.multiple_of((1 - core) * half, half), half), :]


def attend(q_latent, q_rope, cache_latent, cache_rope, cache_len):
    rows, heads, width = q_latent.shape
    span = cache_latent.shape[1]
    half = shaped(rows, heads // 2, width + LANES)
    return local_call(
        attend_kernel,
        [half, half],
        [q_latent, q_rope, cache_latent, cache_rope, cache_len],
        [VMEM, VMEM, VMEM, VMEM, SMEM],
        [pltpu.VMEM((rows, heads, width + LANES), bf16)],
        flops=2_000_000_000,
    )


def join_kernel(last, *refs):
    states, out = refs[:-1], refs[-1]
    rows, heads, full = states[0].shape
    width = full - LANES
    for r in range(rows):
        stats = [s[r, :, width:].astype(f32) for s in states]
        tops = [t[:, 0:1] for t in stats]
        top = functools.reduce(jnp.maximum, tops)
        scales = [jnp.exp(t - top) for t in tops]
        total = sum(c * (t[:, 1:2] + t[:, 2:3]) for c, t in zip(scales, stats))
        summed = sum(c * s[r, :, :width].astype(f32) for c, s in zip(scales, states))
        if last:
            out[r] = (summed / total).astype(bf16)
        else:
            out[r, :, :width] = summed.astype(bf16)
            out[r, :, width:] = stats_of(top, total, heads)


def join(states, last):
    rows, heads, width = states[0].shape
    out = shaped(rows, heads, width - LANES if last else width)
    return local_call(functools.partial(join_kernel, last), out, states, [VMEM] * len(states))


def place_kernel(mine, theirs, out):
    half = mine.shape[1]
    core = lax.rem(lax.axis_index("tp"), 2)
    out[:, pl.ds(pl.multiple_of(core * half, half), half), :] = mine[...]
    out[:, pl.ds(pl.multiple_of((1 - core) * half, half), half), :] = theirs[...]


def place_heads(mine, theirs):
    rows, half, width = mine.shape
    return local_call(place_kernel, shaped(rows, 2 * half, width), [mine, theirs], [VMEM, VMEM])


def pack_kernel(spots, hidden, routes, out, tags, sems):
    size = out.shape[1] - LANES
    picks, rows = routes.shape
    spot, core = spot_and_core()
    start = pl.multiple_of((spot * 2 + core if spots > 1 else core) * size, size)
    columns = pltpu.make_async_copy(hidden.at[:, pl.ds(start, size)], out.at[:, pl.ds(0, size)], sems.at[0])
    named = pltpu.make_async_copy(routes, tags, sems.at[1])
    columns.start()
    named.start()
    out[:, size:] = jnp.zeros((rows, LANES), bf16)
    named.wait()
    eye = lax.broadcasted_iota(jnp.int32, (rows, rows), 0) == lax.broadcasted_iota(jnp.int32, (rows, rows), 1)
    turned = dot(eye.astype(f32).astype(bf16), tags[...].astype(f32).astype(bf16), ((1,), (1,)))
    out[:, size : size + picks] = turned.astype(bf16)
    columns.wait()


def pack_rows(hidden, routes, spots):
    rows, width = hidden.shape
    return local_call(
        functools.partial(pack_kernel, spots),
        shaped(rows, width // (2 * spots) + LANES),
        [pltpu.with_memory_space_constraint(a, pltpu.HBM) for a in (hidden, routes.T)],
        [ANY, ANY],
        [pltpu.VMEM(routes.shape[::-1], jnp.int32), pltpu.SemaphoreType.DMA((2,))],
        flops=WAIT_FLOPS,
        limit=2,
    )


def act_kernel(picks, ways, packs, own, mine, theirs, router, gate, up, down, act, outs, x, tags):
    rows = own.shape[0]
    spots = len(mine)
    size = mine[0].shape[1]
    local, _, hidden = gate.shape
    spot, core = spot_and_core()
    x[pl.ds(0, rows), :] = own[...]
    later = pl.ds(rows, mine[0].shape[0])
    for s in range(spots):
        first = partner(spot, s, ways) * 2 if spots > 1 else 0
        x[later, pl.ds(pl.multiple_of((first + core) * size, size), size)] = mine[s][...]
        x[later, pl.ds(pl.multiple_of((first + 1 - core) * size, size), size)] = theirs[s][...]
    for s, pack in enumerate(packs):
        tags[pl.ds(s * rows, rows), :] = pack[:, size:]

    scores = jax.nn.sigmoid(dot(x[...], router[...], ((1,), (1,))))
    labels = lax.broadcasted_iota(jnp.int32, scores.shape, 1)
    chosen = tags[...].astype(f32).astype(jnp.int32)
    picked = labels < 0
    for k in range(picks):
        picked = picked | (labels == chosen[:, k : k + 1])
    kept = jnp.where(picked, scores, 0.0)
    weights = route_scale * kept / jnp.sum(kept, axis=1, keepdims=True)
    first = lax.axis_index("dev") * local

    for e in range(local):
        rate = jnp.sum(jnp.where(labels == first + e, weights, 0.0), axis=1, keepdims=True)
        a = dot(x[...], gate[e])
        b = dot(x[...], up[e])
        act[:, e * hidden : (e + 1) * hidden] = (a / (1.0 + jnp.exp(-a)) * b * rate).astype(bf16)
    for out in outs:
        out[...] = dot(act[...], down[0][...]).astype(bf16)


def act_call(packs, own, mine, theirs, router, gate, up, down, picks, ways, whole):
    rows, width = own.shape
    local, _, hidden = gate.shape
    count = rows * len(packs)
    down = [down] if whole else []
    cuts = [len(packs), 1, len(mine), len(theirs), 3, len(down)]

    def kernel(*refs):
        groups = []
        for cut in cuts:
            groups.append(refs[:cut])
            refs = refs[cut:]
        packs, (own,), mine, theirs, (router, gate, up), down = groups
        act_kernel(picks, ways, packs, own, mine, theirs, router, gate, up, down, refs[0], refs[1:-2], *refs[-2:])

    parts = [shaped(count, width)] if whole else []
    operands = [*packs, own, *mine, *theirs, router, gate, up, *down]
    return local_call(
        kernel,
        [pltpu.VMEM((count, local * hidden), bf16)] + parts,
        operands,
        [VMEM] * len(operands),
        [pltpu.VMEM((count, width), bf16), pltpu.VMEM((count, LANES), bf16)],
        flops=4 * count * local * hidden * width,
        limit=10 if count <= 256 else 48,
    )


def down_call(act, down, pairs, ways):
    count, depth = act.shape
    width = down.shape[1]

    def kernel(act, down, *outs):
        spot, core = spot_and_core()
        for out, (shift, side) in zip(outs, pairs):
            size = out.shape[1]
            owner = partner(spot, shift, ways) * 2 + (1 - core if side else core)
            out[...] = dot(act[...], down[:, pl.ds(pl.multiple_of(owner * size, size), size)]).astype(bf16)

    return local_call(
        kernel,
        [shaped(count, width // (2 * ways))] * len(pairs),
        [act, down],
        [VMEM, VMEM],
        flops=2 * count * depth * (width // (2 * ways)) * len(pairs),
    )


def on_device(
    hidden,
    routes,
    router_weight,
    gate_weight,
    up_weight,
    down_weight,
    q_latent,
    q_rope,
    cache_latent,
    cache_rope,
    cache_len,
):
    rows, width = hidden.shape
    local, _, units = gate_weight.shape
    n_dev, n_tp = lax.axis_size("dev"), lax.axis_size("tp")
    ways = n_tp // 2
    aligned = width % (n_tp * LANES) == 0
    spots = ways if aligned else 1
    share = width // (2 * spots)

    pack = pack_rows(hidden, routes, spots)
    packs = [pack] + [over_dev(pack, s, n_dev) for s in range(1, n_dev)]
    near = [p[:, :share] for p in packs[1:]]
    first = n_dev // 2 - 1
    rest = jnp.concatenate(near[:first] + near[first + 1 :], axis=0)
    early = [send(near[first], "tp", along_x(s, ways)) for s in range(1, spots)]
    late = [send(rest, "tp", along_x(s, ways)) for s in range(1, spots)]
    early, q_latent = lax.optimization_barrier((early, q_latent))
    mine = [jnp.concatenate(near, axis=0)]
    theirs = [send(mine[0], "tp", other_core)]

    keep, give = attend(q_latent, q_rope, cache_latent, cache_rope, cache_len)
    late, keep, give = lax.optimization_barrier((late, keep, give))
    cut = first * rows
    mine += [jnp.concatenate([b[:cut], a, b[cut:]], axis=0) for a, b in zip(early, late)]
    theirs += [send(m, "tp", other_core) for m in mine[1:]]
    state = join([keep, send(give, "tp", other_core)], False)
    theirs, state = lax.optimization_barrier((theirs, state))
    states = [state] + [send(state, "tp", along_x(s, ways)) for s in range(1, ways)]

    gate, up, down = [
        pltpu.with_memory_space_constraint(w, pltpu.VMEM)
        for w in (gate_weight, up_weight, down_weight.reshape(local * units, width))
    ]
    act, *parts = act_call(
        packs, hidden, mine, theirs, router_weight.T, gate, up, down, routes.shape[1], ways, not aligned
    )
    def added(a, b):
        return a.astype(f32) + b.astype(f32)

    act, states = lax.optimization_barrier((act, states))
    if aligned:
        steps = range(1, ways)
        far = [send(p, "tp", other_core) for p in down_call(act, down, [(s, 1) for s in steps], ways)]
        *own, there = down_call(act, down, [(s, 0) for s in steps] + [(0, 1)], ways)
        there = send(there, "tp", other_core)
        sums = [added(a, b).astype(bf16) for a, b in zip(own, far)]
        act, sums, states = lax.optimization_barrier((act, sums, states))
        (here,) = down_call(act, down, [(0, 0)], ways)
    else:
        spot, core = spot_and_core()
        size = width // n_tp

        def block(step, side):
            return lax.dynamic_slice_in_dim(parts[0], (partner(spot, step, ways) * 2 + side) * size, size, 1)

        own = [block(s, core) for s in range(ways)]
        far = [send(block(s, 1 - core), "tp", other_core) for s in range(ways)]
        sums = [added(a, b).astype(bf16) for a, b in zip(own[1:], far[1:])]
        here, there = own[0], far[0]
    total = added(here, there)
    for s, p in enumerate(sums, 1):
        total = total + send(p, "tp", along_x(s, ways)).astype(f32)
    blocks = [total[i : i + rows] for i in range(0, total.shape[0], rows)]
    moe = blocks[0]
    for s in range(1, n_dev):
        moe = moe + over_dev(blocks[s].astype(bf16), s, n_dev).astype(f32)
    joined = join(states, True)
    attended = place_heads(joined, send(joined, "tp", other_core))
    return (moe.astype(bf16), attended)


def solution(mesh):
    in_specs = (
        P(("group", "dev"), None),
        P(("group", "dev"), None),
        P(),
        P("dev", None, "tp"),
        P("dev", None, "tp"),
        P("dev", "tp", None),
        P(("group", "dev"), None, None),
        P(("group", "dev"), None, None),
        P(("group", "dev"), "tp", None),
        P(("group", "dev"), None, "tp"),
        P(("group", "dev")),
    )
    out_specs = (P(("group", "dev"), "tp"), P(("group", "dev"), None, None))
    return jax.shard_map(
        on_device, mesh=mesh, in_specs=in_specs, out_specs=out_specs, check_vma=False
    )
```

```python
import functools

import jax
import jax.numpy as jnp
from jax import lax
from jax.experimental import pallas as pl
from jax.experimental.pallas import tpu as pltpu
from jax.sharding import PartitionSpec as P

score_scale = 0.13524
route_scale = 2.5
very_low = -1e30
LANES = 128
WAIT_FLOPS = 20_000_000_000

f32, bf16 = jnp.float32, jnp.bfloat16
ANY = pl.BlockSpec(memory_space=pl.ANY)
VMEM = pl.BlockSpec(memory_space=pltpu.VMEM)
SMEM = pl.BlockSpec(memory_space=pltpu.SMEM)


def dot(a, b, contract=((1,), (0,))):
    return lax.dot_general(a, b, (contract, ((), ())), preferred_element_type=f32)


def send(value, axis, target):
    size = lax.axis_size(axis)
    return lax.ppermute(value, axis, [(i, target(i)) for i in range(size)])


def other_core(i):
    return i ^ 1


def partner(place, step, size):
    return place ^ step if size & (size - 1) == 0 else (step - place) % size


def along_x(step, ways):
    return lambda i: partner(i // 2, step, ways) * 2 + i % 2


def over_dev(value, step, size):
    return send(value, "dev", lambda i: partner(i, step, size))


def spot_and_core():
    tp = lax.axis_index("tp")
    return tp // 2, lax.rem(tp, 2)


def local_call(kernel, outs, operands, specs, scratch=(), flops=0, nbytes=0, exps=0, limit=8):
    return pl.pallas_call(
        kernel,
        out_shape=outs,
        in_specs=specs,
        out_specs=jax.tree.map(lambda _: VMEM, outs),
        scratch_shapes=list(scratch),
        cost_estimate=pl.CostEstimate(flops=flops, bytes_accessed=nbytes, transcendentals=exps),
        compiler_params=pltpu.CompilerParams(vmem_limit_bytes=limit << 20),
    )(*operands)


def shaped(*shape):
    return jax.ShapeDtypeStruct(shape, bf16)


def stats_of(top, total, heads):
    lane = lax.broadcasted_iota(jnp.int32, (heads, LANES), 1)
    high = total.astype(bf16).astype(f32)
    stats = jnp.where(lane == 0, top, jnp.where(lane == 1, high, jnp.where(lane == 2, total - high, 0.0)))
    return stats.astype(bf16)


def attend_kernel(q_lat, q_rope, keys, rope, lengths, keep, give, state):
    rows, heads, width = q_lat.shape
    span = keys.shape[1]
    start = lax.axis_index("tp") * span
    for r in range(rows):
        logits = dot(q_lat[r], keys[r], ((1,), (1,)))
        logits += dot(q_rope[r], rope[r], ((0,), (0,)))
        valid = lax.broadcasted_iota(jnp.int32, (heads, span), 1) + start < lengths[r]
        logits = jnp.where(valid, score_scale * logits, very_low)
        top = jnp.max(logits, axis=1, keepdims=True).astype(bf16).astype(f32)
        probs = jnp.where(valid, jnp.exp(logits - top), 0.0)
        total = jnp.sum(probs, axis=1, keepdims=True)
        state[r, :, :width] = dot(probs.astype(bf16), keys[r]).astype(bf16)
        state[r, :, width:] = stats_of(top, total, heads)
    half = heads // 2
    core = lax.rem(lax.axis_index("tp"), 2)
    keep[...] = state[:, pl.ds(pl.multiple_of(core * half, half), half), :]
    give[...] = state[:, pl.ds(pl.multiple_of((1 - core) * half, half), half), :]


def attend(q_latent, q_rope, cache_latent, cache_rope, cache_len):
    rows, heads, width = q_latent.shape
    span = cache_latent.shape[1]
    half = shaped(rows, heads // 2, width + LANES)
    return local_call(
        attend_kernel,
        [half, half],
        [q_latent, q_rope, cache_latent, cache_rope, cache_len],
        [VMEM, VMEM, VMEM, VMEM, SMEM],
        [pltpu.VMEM((rows, heads, width + LANES), bf16)],
        flops=2_000_000_000,
    )


def join_kernel(last, *refs):
    states, out = refs[:-1], refs[-1]
    rows, heads, full = states[0].shape
    width = full - LANES
    for r in range(rows):
        stats = [s[r, :, width:].astype(f32) for s in states]
        tops = [t[:, 0:1] for t in stats]
        top = functools.reduce(jnp.maximum, tops)
        scales = [jnp.exp(t - top) for t in tops]
        total = sum(c * (t[:, 1:2] + t[:, 2:3]) for c, t in zip(scales, stats))
        summed = sum(c * s[r, :, :width].astype(f32) for c, s in zip(scales, states))
        if last:
            out[r] = (summed / total).astype(bf16)
        else:
            out[r, :, :width] = summed.astype(bf16)
            out[r, :, width:] = stats_of(top, total, heads)


def join(states, last):
    rows, heads, width = states[0].shape
    out = shaped(rows, heads, width - LANES if last else width)
    return local_call(functools.partial(join_kernel, last), out, states, [VMEM] * len(states))


def place_kernel(mine, theirs, out):
    half = mine.shape[1]
    core = lax.rem(lax.axis_index("tp"), 2)
    out[:, pl.ds(pl.multiple_of(core * half, half), half), :] = mine[...]
    out[:, pl.ds(pl.multiple_of((1 - core) * half, half), half), :] = theirs[...]


def place_heads(mine, theirs):
    rows, half, width = mine.shape
    return local_call(place_kernel, shaped(rows, 2 * half, width), [mine, theirs], [VMEM, VMEM])


def pack_kernel(spots, hidden, routes, out, tags, sems):
    size = out.shape[1] - LANES
    picks, rows = routes.shape
    spot, core = spot_and_core()
    start = pl.multiple_of((spot * 2 + core if spots > 1 else core) * size, size)
    columns = pltpu.make_async_copy(hidden.at[:, pl.ds(start, size)], out.at[:, pl.ds(0, size)], sems.at[0])
    named = pltpu.make_async_copy(routes, tags, sems.at[1])
    columns.start()
    named.start()
    out[:, size:] = jnp.zeros((rows, LANES), bf16)
    named.wait()
    eye = lax.broadcasted_iota(jnp.int32, (rows, rows), 0) == lax.broadcasted_iota(jnp.int32, (rows, rows), 1)
    turned = dot(eye.astype(f32).astype(bf16), tags[...].astype(f32).astype(bf16), ((1,), (1,)))
    out[:, size : size + picks] = turned.astype(bf16)
    columns.wait()


def pack_rows(hidden, routes, spots):
    rows, width = hidden.shape
    return local_call(
        functools.partial(pack_kernel, spots),
        shaped(rows, width // (2 * spots) + LANES),
        [pltpu.with_memory_space_constraint(a, pltpu.HBM) for a in (hidden, routes.T)],
        [ANY, ANY],
        [pltpu.VMEM(routes.shape[::-1], jnp.int32), pltpu.SemaphoreType.DMA((2,))],
        flops=WAIT_FLOPS,
        limit=2,
    )


def act_kernel(picks, ways, packs, own, mine, theirs, router, gate, up, down, act, outs, x, tags):
    rows = own.shape[0]
    spots = len(mine)
    size = mine[0].shape[1]
    local, _, hidden = gate.shape
    spot, core = spot_and_core()
    dev = lax.axis_index("dev")
    n_dev = len(packs)
    for p in range(n_dev):
        there = pl.ds(pl.multiple_of(partner(dev, p, n_dev) * rows, rows), rows)
        tags[there, :] = packs[p][:, size:]
        if p == 0:
            x[there, :] = own[...]
            continue
        here = pl.ds((p - 1) * rows, rows)
        for s in range(spots):
            first = partner(spot, s, ways) * 2 if spots > 1 else 0
            x[there, pl.ds(pl.multiple_of((first + core) * size, size), size)] = mine[s][here, :]
            x[there, pl.ds(pl.multiple_of((first + 1 - core) * size, size), size)] = theirs[s][here, :]

    scores = jax.nn.sigmoid(dot(x[...], router[...], ((1,), (1,))))
    labels = lax.broadcasted_iota(jnp.int32, scores.shape, 1)
    chosen = tags[...].astype(f32).astype(jnp.int32)
    picked = labels < 0
    for k in range(picks):
        picked = picked | (labels == chosen[:, k : k + 1])
    kept = jnp.where(picked, scores, 0.0)
    weights = route_scale * kept / jnp.sum(kept, axis=1, keepdims=True)
    first = dev * local

    for e in range(local):
        rate = jnp.sum(jnp.where(labels == first + e, weights, 0.0), axis=1, keepdims=True)
        a = dot(x[...], gate[e])
        b = dot(x[...], up[e])
        act[:, e * hidden : (e + 1) * hidden] = (a / (1.0 + jnp.exp(-a)) * b * rate).astype(bf16)
    for out in outs:
        out[...] = dot(act[...], down[0][...]).astype(bf16)


def act_call(packs, own, mine, theirs, router, gate, up, down, picks, ways, whole):
    rows, width = own.shape
    local, _, hidden = gate.shape
    count = rows * len(packs)
    down = [down] if whole else []
    cuts = [len(packs), 1, len(mine), len(theirs), 3, len(down)]

    def kernel(*refs):
        groups = []
        for cut in cuts:
            groups.append(refs[:cut])
            refs = refs[cut:]
        packs, (own,), mine, theirs, (router, gate, up), down = groups
        act_kernel(picks, ways, packs, own, mine, theirs, router, gate, up, down, refs[0], refs[1:-2], *refs[-2:])

    parts = [shaped(count, width)] if whole else []
    operands = [*packs, own, *mine, *theirs, router, gate, up, *down]
    return local_call(
        kernel,
        [pltpu.VMEM((count, local * hidden), bf16)] + parts,
        operands,
        [VMEM] * len(operands),
        [pltpu.VMEM((count, width), bf16), pltpu.VMEM((count, LANES), bf16)],
        limit=10 if count <= 256 else 48,
    )


def down_call(act, down, pairs, ways):
    count, depth = act.shape
    width = down.shape[1]

    def kernel(act, down, *outs):
        spot, core = spot_and_core()
        for out, (shift, side) in zip(outs, pairs):
            size = out.shape[1]
            owner = partner(spot, shift, ways) * 2 + (1 - core if side else core)
            out[...] = dot(act[...], down[:, pl.ds(pl.multiple_of(owner * size, size), size)]).astype(bf16)

    return local_call(
        kernel,
        [shaped(count, width // (2 * ways))] * len(pairs),
        [act, down],
        [VMEM, VMEM],
        flops=2 * count * depth * (width // (2 * ways)) * len(pairs),
    )


def on_device(
    hidden,
    routes,
    router_weight,
    gate_weight,
    up_weight,
    down_weight,
    q_latent,
    q_rope,
    cache_latent,
    cache_rope,
    cache_len,
):
    rows, width = hidden.shape
    local, _, units = gate_weight.shape
    n_dev, n_tp = lax.axis_size("dev"), lax.axis_size("tp")
    ways = n_tp // 2
    aligned = width % (n_tp * LANES) == 0
    spots = ways if aligned else 1
    share = width // (2 * spots)

    pack = pack_rows(hidden, routes, spots)
    pack, q_latent = lax.optimization_barrier((pack, q_latent))
    first = n_dev // 2
    far = over_dev(pack, first, n_dev)
    keep, give = attend(q_latent, q_rope, cache_latent, cache_rope, cache_len)
    again, keep, give = lax.optimization_barrier((pack, keep, give))
    packs = [pack] + [far if s == first else over_dev(again, s, n_dev) for s in range(1, n_dev)]
    near = [p[:, :share] for p in packs[1:]]
    first -= 1
    early = [send(near[first], "tp", along_x(s, ways)) for s in range(1, spots)]
    state = join([keep, send(give, "tp", other_core)], False)
    rest = jnp.concatenate(near[:first] + near[first + 1 :], axis=0)
    rest, state = lax.optimization_barrier((rest, state))
    late = [send(rest, "tp", along_x(s, ways)) for s in range(1, spots)]
    mine = [jnp.concatenate(near, axis=0)]
    cut = first * rows
    mine += [jnp.concatenate([b[:cut], a, b[cut:]], axis=0) for a, b in zip(early, late)]
    theirs = [send(m, "tp", other_core) for m in mine]
    states = [send(state, "tp", along_x(s, ways)) for s in range(1, ways)]
    theirs, state = lax.optimization_barrier((theirs, state))
    states = [state] + states

    gate, up, down = [
        pltpu.with_memory_space_constraint(w, pltpu.VMEM)
        for w in (gate_weight, up_weight, down_weight.reshape(local * units, width))
    ]
    act, *parts = act_call(
        packs, hidden, mine, theirs, router_weight.T, gate, up, down, routes.shape[1], ways, not aligned
    )
    def added(a, b):
        return a.astype(f32) + b.astype(f32)

    act, states = lax.optimization_barrier((act, states))
    if aligned:
        steps = range(1, ways)
        far = [send(p, "tp", other_core) for p in down_call(act, down, [(s, 1) for s in steps], ways)]
        *own, there = down_call(act, down, [(s, 0) for s in steps] + [(0, 1)], ways)
        there = send(there, "tp", other_core)
        sums = [added(a, b).astype(bf16) for a, b in zip(own, far)]
        act, sums, states = lax.optimization_barrier((act, sums, states))
        (here,) = down_call(act, down, [(0, 0)], ways)
    else:
        spot, core = spot_and_core()
        size = width // n_tp

        def block(step, side):
            return lax.dynamic_slice_in_dim(parts[0], (partner(spot, step, ways) * 2 + side) * size, size, 1)

        own = [block(s, core) for s in range(ways)]
        far = [send(block(s, 1 - core), "tp", other_core) for s in range(ways)]
        sums = [added(a, b).astype(bf16) for a, b in zip(own[1:], far[1:])]
        here, there = own[0], far[0]
    total = added(here, there)
    for s, p in enumerate(sums, 1):
        total = total + send(p, "tp", along_x(s, ways)).astype(f32)
    back = lax.all_to_all(total.astype(bf16), "dev", split_axis=0, concat_axis=0, tiled=True)
    moe = jnp.sum(back.reshape(n_dev, rows, -1).astype(f32), axis=0)
    joined = join(states, True)
    attended = place_heads(joined, send(joined, "tp", other_core))
    return (moe.astype(bf16), attended)


def solution(mesh):
    in_specs = (
        P(("group", "dev"), None),
        P(("group", "dev"), None),
        P(),
        P("dev", None, "tp"),
        P("dev", None, "tp"),
        P("dev", "tp", None),
        P(("group", "dev"), None, None),
        P(("group", "dev"), None, None),
        P(("group", "dev"), "tp", None),
        P(("group", "dev"), None, "tp"),
        P(("group", "dev")),
    )
    out_specs = (P(("group", "dev"), "tp"), P(("group", "dev"), None, None))
    return jax.shard_map(
        on_device, mesh=mesh, in_specs=in_specs, out_specs=out_specs, check_vma=False
    )
```

```python
import functools

import jax
import jax.numpy as jnp
from jax import lax
from jax.experimental import pallas as pl
from jax.experimental.pallas import tpu as pltpu
from jax.sharding import PartitionSpec as P

score_scale = 0.13524
route_scale = 2.5
very_low = -1e30
LANES = 128
WAIT_FLOPS = 20_000_000_000

f32, bf16 = jnp.float32, jnp.bfloat16
ANY = pl.BlockSpec(memory_space=pl.ANY)
VMEM = pl.BlockSpec(memory_space=pltpu.VMEM)
SMEM = pl.BlockSpec(memory_space=pltpu.SMEM)


def dot(a, b, contract=((1,), (0,))):
    return lax.dot_general(a, b, (contract, ((), ())), preferred_element_type=f32)


def send(value, axis, target):
    size = lax.axis_size(axis)
    return lax.ppermute(value, axis, [(i, target(i)) for i in range(size)])


def other_core(i):
    return i ^ 1


def partner(place, step, size):
    return place ^ step if size & (size - 1) == 0 else (step - place) % size


def along_x(step, ways):
    return lambda i: partner(i // 2, step, ways) * 2 + i % 2


def over_dev(value, step, size):
    return send(value, "dev", lambda i: partner(i, step, size))


def spot_and_core():
    tp = lax.axis_index("tp")
    return tp // 2, lax.rem(tp, 2)


def local_call(kernel, outs, operands, specs, scratch=(), flops=0, nbytes=0, exps=0, limit=8):
    return pl.pallas_call(
        kernel,
        out_shape=outs,
        in_specs=specs,
        out_specs=jax.tree.map(lambda _: VMEM, outs),
        scratch_shapes=list(scratch),
        cost_estimate=pl.CostEstimate(flops=flops, bytes_accessed=nbytes, transcendentals=exps),
        compiler_params=pltpu.CompilerParams(vmem_limit_bytes=limit << 20),
    )(*operands)


def shaped(*shape):
    return jax.ShapeDtypeStruct(shape, bf16)


def stats_of(top, total, heads):
    lane = lax.broadcasted_iota(jnp.int32, (heads, LANES), 1)
    high = total.astype(bf16).astype(f32)
    stats = jnp.where(lane == 0, top, jnp.where(lane == 1, high, jnp.where(lane == 2, total - high, 0.0)))
    return stats.astype(bf16)


def attend_kernel(q_lat, q_rope, keys, rope, lengths, keep, give, state):
    rows, heads, width = q_lat.shape
    span = keys.shape[1]
    start = lax.axis_index("tp") * span
    for r in range(rows):
        logits = dot(q_lat[r], keys[r], ((1,), (1,)))
        logits += dot(q_rope[r], rope[r], ((0,), (0,)))
        valid = lax.broadcasted_iota(jnp.int32, (heads, span), 1) + start < lengths[r]
        logits = jnp.where(valid, score_scale * logits, very_low)
        top = jnp.max(logits, axis=1, keepdims=True).astype(bf16).astype(f32)
        probs = jnp.where(valid, jnp.exp(logits - top), 0.0)
        total = jnp.sum(probs, axis=1, keepdims=True)
        state[r, :, :width] = dot(probs.astype(bf16), keys[r]).astype(bf16)
        state[r, :, width:] = stats_of(top, total, heads)
    half = heads // 2
    core = lax.rem(lax.axis_index("tp"), 2)
    keep[...] = state[:, pl.ds(pl.multiple_of(core * half, half), half), :]
    give[...] = state[:, pl.ds(pl.multiple_of((1 - core) * half, half), half), :]


def attend(q_latent, q_rope, cache_latent, cache_rope, cache_len):
    rows, heads, width = q_latent.shape
    span = cache_latent.shape[1]
    half = shaped(rows, heads // 2, width + LANES)
    return local_call(
        attend_kernel,
        [half, half],
        [q_latent, q_rope, cache_latent, cache_rope, cache_len],
        [VMEM, VMEM, VMEM, VMEM, SMEM],
        [pltpu.VMEM((rows, heads, width + LANES), bf16)],
    )


def join_kernel(last, *refs):
    states, out = refs[:-1], refs[-1]
    rows, heads, full = states[0].shape
    width = full - LANES
    for r in range(rows):
        stats = [s[r, :, width:].astype(f32) for s in states]
        tops = [t[:, 0:1] for t in stats]
        top = functools.reduce(jnp.maximum, tops)
        scales = [jnp.exp(t - top) for t in tops]
        total = sum(c * (t[:, 1:2] + t[:, 2:3]) for c, t in zip(scales, stats))
        summed = sum(c * s[r, :, :width].astype(f32) for c, s in zip(scales, states))
        if last:
            out[r] = (summed / total).astype(bf16)
        else:
            out[r, :, :width] = summed.astype(bf16)
            out[r, :, width:] = stats_of(top, total, heads)


def join(states, last):
    rows, heads, width = states[0].shape
    out = shaped(rows, heads, width - LANES if last else width)
    return local_call(functools.partial(join_kernel, last), out, states, [VMEM] * len(states))


def place_kernel(mine, theirs, out):
    half = mine.shape[1]
    core = lax.rem(lax.axis_index("tp"), 2)
    out[:, pl.ds(pl.multiple_of(core * half, half), half), :] = mine[...]
    out[:, pl.ds(pl.multiple_of((1 - core) * half, half), half), :] = theirs[...]


def place_heads(mine, theirs):
    rows, half, width = mine.shape
    return local_call(place_kernel, shaped(rows, 2 * half, width), [mine, theirs], [VMEM, VMEM])


def pack_kernel(hidden, routes, out, tags, sems):
    size = out.shape[1] - LANES
    picks, rows = routes.shape
    _, core = spot_and_core()
    start = pl.multiple_of(core * size, size)
    columns = pltpu.make_async_copy(hidden.at[:, pl.ds(start, size)], out.at[:, pl.ds(0, size)], sems.at[0])
    named = pltpu.make_async_copy(routes, tags, sems.at[1])
    columns.start()
    named.start()
    out[:, size:] = jnp.zeros((rows, LANES), bf16)
    named.wait()
    eye = lax.broadcasted_iota(jnp.int32, (rows, rows), 0) == lax.broadcasted_iota(jnp.int32, (rows, rows), 1)
    turned = dot(eye.astype(f32).astype(bf16), tags[...].astype(f32).astype(bf16), ((1,), (1,)))
    out[:, size : size + picks] = turned.astype(bf16)
    columns.wait()


def pack_rows(hidden, routes):
    rows, width = hidden.shape
    return local_call(
        pack_kernel,
        shaped(rows, width // 2 + LANES),
        [pltpu.with_memory_space_constraint(a, pltpu.HBM) for a in (hidden, routes.T)],
        [ANY, ANY],
        [pltpu.VMEM(routes.shape[::-1], jnp.int32), pltpu.SemaphoreType.DMA((2,))],
        flops=WAIT_FLOPS,
        limit=2,
    )


def act_kernel(picks, packs, own, theirs, router, gate, up, down, act, outs, x, tags):
    rows = own.shape[0]
    size = packs[0].shape[1] - LANES
    local, _, hidden = gate.shape
    _, core = spot_and_core()
    mine = pl.ds(pl.multiple_of(core * size, size), size)
    other = pl.ds(pl.multiple_of((1 - core) * size, size), size)
    x[pl.ds(0, rows), :] = own[...]
    for s, pack in enumerate(packs):
        if s:
            x[pl.ds(s * rows, rows), mine] = pack[:, :size]
    for ref, start, first in theirs:
        x[pl.ds(first, rows), other] = ref[pl.ds(start, rows), :]
    for s, pack in enumerate(packs):
        tags[pl.ds(s * rows, rows), :] = pack[:, size:]

    scores = jax.nn.sigmoid(dot(x[...], router[...], ((1,), (1,))))
    labels = lax.broadcasted_iota(jnp.int32, scores.shape, 1)
    chosen = tags[...].astype(f32).astype(jnp.int32)
    picked = labels < 0
    for k in range(picks):
        picked = picked | (labels == chosen[:, k : k + 1])
    kept = jnp.where(picked, scores, 0.0)
    weights = route_scale * kept / jnp.sum(kept, axis=1, keepdims=True)
    first = lax.axis_index("dev") * local

    for e in range(local):
        rate = jnp.sum(jnp.where(labels == first + e, weights, 0.0), axis=1, keepdims=True)
        a = dot(x[...], gate[e])
        b = dot(x[...], up[e])
        act[:, e * hidden : (e + 1) * hidden] = (a / (1.0 + jnp.exp(-a)) * b * rate).astype(bf16)
    for out in outs:
        out[...] = dot(act[...], down[0][...]).astype(bf16)


def act_call(packs, own, theirs, places, router, gate, up, down, picks, whole):
    rows, width = own.shape
    local, _, hidden = gate.shape
    count = rows * len(packs)
    down = [down] if whole else []
    cuts = [len(packs), 1, len(theirs), 3, len(down)]

    def kernel(*refs):
        groups = []
        for cut in cuts:
            groups.append(refs[:cut])
            refs = refs[cut:]
        packs, (own,), theirs, (router, gate, up), down = groups
        theirs = [(ref, i * rows, s * rows) for ref, steps in zip(theirs, places) for i, s in enumerate(steps)]
        act_kernel(picks, packs, own, theirs, router, gate, up, down, refs[0], refs[1:-2], *refs[-2:])

    parts = [shaped(count, width)] if whole else []
    operands = [*packs, own, *theirs, router, gate, up, *down]
    return local_call(
        kernel,
        [pltpu.VMEM((count, local * hidden), bf16)] + parts,
        operands,
        [VMEM] * len(operands),
        [pltpu.VMEM((count, width), bf16), pltpu.VMEM((count, LANES), bf16)],
        limit=10 if count <= 256 else 48,
    )


def down_call(act, down, pairs, ways):
    count = act.shape[0]
    width = down.shape[1]

    def kernel(act, down, *outs):
        spot, core = spot_and_core()
        for out, (shift, side) in zip(outs, pairs):
            size = out.shape[1]
            owner = partner(spot, shift, ways) * 2 + (1 - core if side else core)
            out[...] = dot(act[...], down[:, pl.ds(pl.multiple_of(owner * size, size), size)]).astype(bf16)

    return local_call(
        kernel,
        [shaped(count, width // (2 * ways))] * len(pairs),
        [act, down],
        [VMEM, VMEM],
    )


def on_device(
    hidden,
    routes,
    router_weight,
    gate_weight,
    up_weight,
    down_weight,
    q_latent,
    q_rope,
    cache_latent,
    cache_rope,
    cache_len,
):
    rows, width = hidden.shape
    local, _, units = gate_weight.shape
    n_dev, n_tp = lax.axis_size("dev"), lax.axis_size("tp")
    ways = n_tp // 2
    aligned = width % (n_tp * LANES) == 0
    half = width // 2

    pack = pack_rows(hidden, routes)
    packs = [pack] + [over_dev(pack, s, n_dev) for s in range(1, n_dev)]
    first = n_dev // 2
    places = [[first], [s for s in range(1, n_dev) if s != first]]
    early, q_latent = lax.optimization_barrier((packs[first], q_latent))
    keep, give = attend(q_latent, q_rope, cache_latent, cache_rope, cache_len)
    packs, keep, give = lax.optimization_barrier((packs, keep, give))
    packs[first] = early
    theirs = [send(jnp.concatenate([packs[s][:, :half] for s in p], axis=0), "tp", other_core) for p in places]
    state = join([keep, send(give, "tp", other_core)], False)
    theirs, state = lax.optimization_barrier((theirs, state))
    states = [state] + [send(state, "tp", along_x(s, ways)) for s in range(1, ways)]

    gate, up, down = [
        pltpu.with_memory_space_constraint(w, pltpu.VMEM)
        for w in (gate_weight, up_weight, down_weight.reshape(local * units, width))
    ]
    act, *parts = act_call(
        packs, hidden, theirs, places, router_weight.T, gate, up, down, routes.shape[1], not aligned
    )
    def added(a, b):
        return a.astype(f32) + b.astype(f32)

    act, states = lax.optimization_barrier((act, states))
    if aligned:
        steps = range(1, ways)
        far = [send(p, "tp", other_core) for p in down_call(act, down, [(s, 1) for s in steps], ways)]
        *own, there = down_call(act, down, [(s, 0) for s in steps] + [(0, 1)], ways)
        there = send(there, "tp", other_core)
        sums = [added(a, b).astype(bf16) for a, b in zip(own, far)]
        act, sums, states = lax.optimization_barrier((act, sums, states))
        (here,) = down_call(act, down, [(0, 0)], ways)
    else:
        spot, core = spot_and_core()
        size = width // n_tp

        def block(step, side):
            return lax.dynamic_slice_in_dim(parts[0], (partner(spot, step, ways) * 2 + side) * size, size, 1)

        own = [block(s, core) for s in range(ways)]
        far = [send(block(s, 1 - core), "tp", other_core) for s in range(ways)]
        sums = [added(a, b).astype(bf16) for a, b in zip(own[1:], far[1:])]
        here, there = own[0], far[0]
    total = added(here, there)
    for s, p in enumerate(sums, 1):
        total = total + send(p, "tp", along_x(s, ways)).astype(f32)
    blocks = [total[i : i + rows] for i in range(0, total.shape[0], rows)]
    moe = blocks[0]
    for s in range(1, n_dev):
        moe = moe + over_dev(blocks[s].astype(bf16), s, n_dev).astype(f32)
    joined = join(states, True)
    attended = place_heads(joined, send(joined, "tp", other_core))
    return (moe.astype(bf16), attended)


def solution(mesh):
    in_specs = (
        P(("group", "dev"), None),
        P(("group", "dev"), None),
        P(),
        P("dev", None, "tp"),
        P("dev", None, "tp"),
        P("dev", "tp", None),
        P(("group", "dev"), None, None),
        P(("group", "dev"), None, None),
        P(("group", "dev"), "tp", None),
        P(("group", "dev"), None, "tp"),
        P(("group", "dev")),
    )
    out_specs = (P(("group", "dev"), "tp"), P(("group", "dev"), None, None))
    return jax.shard_map(
        on_device, mesh=mesh, in_specs=in_specs, out_specs=out_specs, check_vma=False
    )
```

```python
import functools

import jax
import jax.numpy as jnp
from jax import lax
from jax.experimental import pallas as pl
from jax.experimental.pallas import tpu as pltpu
from jax.sharding import PartitionSpec as P

score_scale = 0.13524
route_scale = 2.5
very_low = -1e30
LANES = 128
WAIT_FLOPS = 100_000_000_000

f32, bf16 = jnp.float32, jnp.bfloat16
ANY = pl.BlockSpec(memory_space=pl.ANY)
VMEM = pl.BlockSpec(memory_space=pltpu.VMEM)
SMEM = pl.BlockSpec(memory_space=pltpu.SMEM)


def dot(a, b, contract=((1,), (0,))):
    return lax.dot_general(a, b, (contract, ((), ())), preferred_element_type=f32)


def send(value, axis, target):
    size = lax.axis_size(axis)
    return lax.ppermute(value, axis, [(i, target(i)) for i in range(size)])


def other_core(i):
    return i ^ 1


def partner(place, step, size):
    return place ^ step if size & (size - 1) == 0 else (step - place) % size


def along_x(step, ways):
    return lambda i: partner(i // 2, step, ways) * 2 + i % 2


def over_dev(value, step, size):
    return send(value, "dev", lambda i: partner(i, step, size))


def spot_and_core():
    tp = lax.axis_index("tp")
    return tp // 2, lax.rem(tp, 2)


def local_call(kernel, outs, operands, specs, scratch=(), flops=0, nbytes=0, exps=0, limit=8):
    return pl.pallas_call(
        kernel,
        out_shape=outs,
        in_specs=specs,
        out_specs=jax.tree.map(lambda _: VMEM, outs),
        scratch_shapes=list(scratch),
        cost_estimate=pl.CostEstimate(flops=flops, bytes_accessed=nbytes, transcendentals=exps),
        compiler_params=pltpu.CompilerParams(vmem_limit_bytes=limit << 20),
    )(*operands)


def shaped(*shape):
    return jax.ShapeDtypeStruct(shape, bf16)


def stats_of(top, total, heads):
    lane = lax.broadcasted_iota(jnp.int32, (heads, LANES), 1)
    high = total.astype(bf16).astype(f32)
    stats = jnp.where(lane == 0, top, jnp.where(lane == 1, high, jnp.where(lane == 2, total - high, 0.0)))
    return stats.astype(bf16)


def attend_kernel(q_lat, q_rope, keys, rope, lengths, keep, give, state):
    rows, heads, width = q_lat.shape
    span = keys.shape[1]
    start = lax.axis_index("tp") * span
    for r in range(rows):
        logits = dot(q_lat[r], keys[r], ((1,), (1,)))
        logits += dot(q_rope[r], rope[r], ((0,), (0,)))
        valid = lax.broadcasted_iota(jnp.int32, (heads, span), 1) + start < lengths[r]
        logits = jnp.where(valid, score_scale * logits, very_low)
        top = jnp.max(logits, axis=1, keepdims=True).astype(bf16).astype(f32)
        probs = jnp.where(valid, jnp.exp(logits - top), 0.0)
        total = jnp.sum(probs, axis=1, keepdims=True)
        state[r, :, :width] = dot(probs.astype(bf16), keys[r]).astype(bf16)
        state[r, :, width:] = stats_of(top, total, heads)
    half = heads // 2
    core = lax.rem(lax.axis_index("tp"), 2)
    keep[...] = state[:, pl.ds(pl.multiple_of(core * half, half), half), :]
    give[...] = state[:, pl.ds(pl.multiple_of((1 - core) * half, half), half), :]


def attend(q_latent, q_rope, cache_latent, cache_rope, cache_len):
    rows, heads, width = q_latent.shape
    span = cache_latent.shape[1]
    half = shaped(rows, heads // 2, width + LANES)
    return local_call(
        attend_kernel,
        [half, half],
        [q_latent, q_rope, cache_latent, cache_rope, cache_len],
        [VMEM, VMEM, VMEM, VMEM, SMEM],
        [pltpu.VMEM((rows, heads, width + LANES), bf16)],
        flops=2_000_000_000,
    )


def join_kernel(last, *refs):
    states, out = refs[:-1], refs[-1]
    rows, heads, full = states[0].shape
    width = full - LANES
    for r in range(rows):
        stats = [s[r, :, width:].astype(f32) for s in states]
        tops = [t[:, 0:1] for t in stats]
        top = functools.reduce(jnp.maximum, tops)
        scales = [jnp.exp(t - top) for t in tops]
        total = sum(c * (t[:, 1:2] + t[:, 2:3]) for c, t in zip(scales, stats))
        summed = sum(c * s[r, :, :width].astype(f32) for c, s in zip(scales, states))
        if last:
            out[r] = (summed / total).astype(bf16)
        else:
            out[r, :, :width] = summed.astype(bf16)
            out[r, :, width:] = stats_of(top, total, heads)


def join(states, last):
    rows, heads, width = states[0].shape
    out = shaped(rows, heads, width - LANES if last else width)
    return local_call(functools.partial(join_kernel, last), out, states, [VMEM] * len(states))


def place_kernel(mine, theirs, out):
    half = mine.shape[1]
    core = lax.rem(lax.axis_index("tp"), 2)
    out[:, pl.ds(pl.multiple_of(core * half, half), half), :] = mine[...]
    out[:, pl.ds(pl.multiple_of((1 - core) * half, half), half), :] = theirs[...]


def place_heads(mine, theirs):
    rows, half, width = mine.shape
    return local_call(place_kernel, shaped(rows, 2 * half, width), [mine, theirs], [VMEM, VMEM])


def pack_kernel(spots, hidden, routes, out, tags, sems):
    size = out.shape[1] - LANES
    picks, rows = routes.shape
    spot, core = spot_and_core()
    start = pl.multiple_of((spot * 2 + core if spots > 1 else core) * size, size)
    columns = pltpu.make_async_copy(hidden.at[:, pl.ds(start, size)], out.at[:, pl.ds(0, size)], sems.at[0])
    named = pltpu.make_async_copy(routes, tags, sems.at[1])
    columns.start()
    named.start()
    out[:, size:] = jnp.zeros((rows, LANES), bf16)
    named.wait()
    eye = lax.broadcasted_iota(jnp.int32, (rows, rows), 0) == lax.broadcasted_iota(jnp.int32, (rows, rows), 1)
    turned = dot(eye.astype(f32).astype(bf16), tags[...].astype(f32).astype(bf16), ((1,), (1,)))
    out[:, size : size + picks] = turned.astype(bf16)
    columns.wait()


def pack_rows(hidden, routes, spots):
    rows, width = hidden.shape
    return local_call(
        functools.partial(pack_kernel, spots),
        shaped(rows, width // (2 * spots) + LANES),
        [pltpu.with_memory_space_constraint(a, pltpu.HBM) for a in (hidden, routes.T)],
        [ANY, ANY],
        [pltpu.VMEM(routes.shape[::-1], jnp.int32), pltpu.SemaphoreType.DMA((2,))],
        flops=WAIT_FLOPS,
        limit=2,
    )


def act_kernel(picks, ways, packs, own, mine, theirs, router, gate, up, down, act, outs, x, tags):
    rows = own.shape[0]
    spots = len(mine)
    size = mine[0].shape[1]
    local, _, hidden = gate.shape
    spot, core = spot_and_core()
    x[pl.ds(0, rows), :] = own[...]
    later = pl.ds(rows, mine[0].shape[0])
    for s in range(spots):
        first = partner(spot, s, ways) * 2 if spots > 1 else 0
        x[later, pl.ds(pl.multiple_of((first + core) * size, size), size)] = mine[s][...]
        x[later, pl.ds(pl.multiple_of((first + 1 - core) * size, size), size)] = theirs[s][...]
    for s, pack in enumerate(packs):
        tags[pl.ds(s * rows, rows), :] = pack[:, size:]

    scores = jax.nn.sigmoid(dot(x[...], router[...], ((1,), (1,))))
    labels = lax.broadcasted_iota(jnp.int32, scores.shape, 1)
    chosen = tags[...].astype(f32).astype(jnp.int32)
    picked = labels < 0
    for k in range(picks):
        picked = picked | (labels == chosen[:, k : k + 1])
    kept = jnp.where(picked, scores, 0.0)
    weights = route_scale * kept / jnp.sum(kept, axis=1, keepdims=True)
    first = lax.axis_index("dev") * local

    for e in range(local):
        rate = jnp.sum(jnp.where(labels == first + e, weights, 0.0), axis=1, keepdims=True)
        a = dot(x[...], gate[e])
        b = dot(x[...], up[e])
        act[:, e * hidden : (e + 1) * hidden] = (a / (1.0 + jnp.exp(-a)) * b * rate).astype(bf16)
    for out in outs:
        out[...] = dot(act[...], down[0][...]).astype(bf16)


def act_call(packs, own, mine, theirs, router, gate, up, down, picks, ways, whole):
    rows, width = own.shape
    local, _, hidden = gate.shape
    count = rows * len(packs)
    down = [down] if whole else []
    cuts = [len(packs), 1, len(mine), len(theirs), 3, len(down)]

    def kernel(*refs):
        groups = []
        for cut in cuts:
            groups.append(refs[:cut])
            refs = refs[cut:]
        packs, (own,), mine, theirs, (router, gate, up), down = groups
        act_kernel(picks, ways, packs, own, mine, theirs, router, gate, up, down, refs[0], refs[1:-2], *refs[-2:])

    parts = [shaped(count, width)] if whole else []
    operands = [*packs, own, *mine, *theirs, router, gate, up, *down]
    return local_call(
        kernel,
        [pltpu.VMEM((count, local * hidden), bf16)] + parts,
        operands,
        [VMEM] * len(operands),
        [pltpu.VMEM((count, width), bf16), pltpu.VMEM((count, LANES), bf16)],
        limit=10 if count <= 256 else 48,
    )


def down_call(act, down, pairs, ways):
    count = act.shape[0]
    width = down.shape[1]

    def kernel(act, down, *outs):
        spot, core = spot_and_core()
        for out, (shift, side) in zip(outs, pairs):
            size = out.shape[1]
            owner = partner(spot, shift, ways) * 2 + (1 - core if side else core)
            out[...] = dot(act[...], down[:, pl.ds(pl.multiple_of(owner * size, size), size)]).astype(bf16)

    return local_call(
        kernel,
        [shaped(count, width // (2 * ways))] * len(pairs),
        [act, down],
        [VMEM, VMEM],
    )


def on_device(
    hidden,
    routes,
    router_weight,
    gate_weight,
    up_weight,
    down_weight,
    q_latent,
    q_rope,
    cache_latent,
    cache_rope,
    cache_len,
):
    rows, width = hidden.shape
    local, _, units = gate_weight.shape
    n_dev, n_tp = lax.axis_size("dev"), lax.axis_size("tp")
    ways = n_tp // 2
    aligned = width % (n_tp * LANES) == 0
    spots = ways if aligned else 1
    share = width // (2 * spots)

    pack = pack_rows(hidden, routes, spots)
    packs = [pack] + [over_dev(pack, s, n_dev) for s in range(1, n_dev)]
    first = n_dev // 2
    early, q_latent = lax.optimization_barrier((packs[first], q_latent))
    keep, give = attend(q_latent, q_rope, cache_latent, cache_rope, cache_len)
    early = early[:, :share]
    early_x = [send(early, "tp", along_x(s, ways)) for s in range(1, spots)]
    packs, early_x, keep, give = lax.optimization_barrier((packs, early_x, keep, give))
    near = [early if s == first else packs[s][:, :share] for s in range(1, n_dev)]
    rest = jnp.concatenate(near[: first - 1] + near[first:], axis=0)
    late_x = [send(rest, "tp", along_x(s, ways)) for s in range(1, spots)]
    mine = [jnp.concatenate(near, axis=0)]
    theirs = [send(mine[0], "tp", other_core)]
    state = join([keep, send(give, "tp", other_core)], False)
    late_x, state = lax.optimization_barrier((late_x, state))
    cut = (first - 1) * rows
    mine += [jnp.concatenate([b[:cut], a, b[cut:]], axis=0) for a, b in zip(early_x, late_x)]
    theirs += [send(m, "tp", other_core) for m in mine[1:]]
    states = [state] + [send(state, "tp", along_x(s, ways)) for s in range(1, ways)]

    gate, up, down = [
        pltpu.with_memory_space_constraint(w, pltpu.VMEM)
        for w in (gate_weight, up_weight, down_weight.reshape(local * units, width))
    ]
    act, *parts = act_call(
        packs, hidden, mine, theirs, router_weight.T, gate, up, down, routes.shape[1], ways, not aligned
    )
    def added(a, b):
        return a.astype(f32) + b.astype(f32)

    act, states = lax.optimization_barrier((act, states))
    if aligned:
        steps = range(1, ways)
        far = [send(p, "tp", other_core) for p in down_call(act, down, [(s, 1) for s in steps], ways)]
        *own, there = down_call(act, down, [(s, 0) for s in steps] + [(0, 1)], ways)
        there = send(there, "tp", other_core)
        sums = [added(a, b).astype(bf16) for a, b in zip(own, far)]
        act, sums, states = lax.optimization_barrier((act, sums, states))
        (here,) = down_call(act, down, [(0, 0)], ways)
    else:
        spot, core = spot_and_core()
        size = width // n_tp

        def block(step, side):
            return lax.dynamic_slice_in_dim(parts[0], (partner(spot, step, ways) * 2 + side) * size, size, 1)

        own = [block(s, core) for s in range(ways)]
        far = [send(block(s, 1 - core), "tp", other_core) for s in range(ways)]
        sums = [added(a, b).astype(bf16) for a, b in zip(own[1:], far[1:])]
        here, there = own[0], far[0]
    total = added(here, there)
    for s, p in enumerate(sums, 1):
        total = total + send(p, "tp", along_x(s, ways)).astype(f32)
    blocks = [total[i : i + rows] for i in range(0, total.shape[0], rows)]
    moe = blocks[0]
    for s in range(1, n_dev):
        moe = moe + over_dev(blocks[s].astype(bf16), s, n_dev).astype(f32)
    joined = join(states, True)
    attended = place_heads(joined, send(joined, "tp", other_core))
    return (moe.astype(bf16), attended)


def solution(mesh):
    in_specs = (
        P(("group", "dev"), None),
        P(("group", "dev"), None),
        P(),
        P("dev", None, "tp"),
        P("dev", None, "tp"),
        P("dev", "tp", None),
        P(("group", "dev"), None, None),
        P(("group", "dev"), None, None),
        P(("group", "dev"), "tp", None),
        P(("group", "dev"), None, "tp"),
        P(("group", "dev")),
    )
    out_specs = (P(("group", "dev"), "tp"), P(("group", "dev"), None, None))
    return jax.shard_map(
        on_device, mesh=mesh, in_specs=in_specs, out_specs=out_specs, check_vma=False
    )
```

```python
import functools

import jax
import jax.numpy as jnp
from jax import lax
from jax.experimental import pallas as pl
from jax.experimental.pallas import tpu as pltpu
from jax.sharding import PartitionSpec as P

score_scale = 0.13524
route_scale = 2.5
very_low = -1e30
LANES = 128
WAIT_FLOPS = 100_000_000_000

f32, bf16 = jnp.float32, jnp.bfloat16
ANY = pl.BlockSpec(memory_space=pl.ANY)
VMEM = pl.BlockSpec(memory_space=pltpu.VMEM)
SMEM = pl.BlockSpec(memory_space=pltpu.SMEM)

def dot(a, b, contract=((1,), (0,))):
    return lax.dot_general(a, b, (contract, ((), ())), preferred_element_type=f32)

def send(value, axis, target):
    size = lax.axis_size(axis)
    return lax.ppermute(value, axis, [(i, target(i)) for i in range(size)])

def other_core(i):
    return i ^ 1

def partner(place, step, size):
    return place ^ step if size & (size - 1) == 0 else (step - place) % size

def along_x(step, ways):
    return lambda i: partner(i // 2, step, ways) * 2 + i % 2

def over_dev(value, step, size):
    return send(value, "dev", lambda i: partner(i, step, size))

def spot_and_core():
    tp = lax.axis_index("tp")
    return tp // 2, lax.rem(tp, 2)

def local_call(kernel, outs, operands, specs, scratch=(), flops=0, nbytes=0, exps=0, limit=8):
    return pl.pallas_call(
        kernel,
        out_shape=outs,
        in_specs=specs,
        out_specs=jax.tree.map(lambda _: VMEM, outs),
        scratch_shapes=list(scratch),
        cost_estimate=pl.CostEstimate(flops=flops, bytes_accessed=nbytes, transcendentals=exps),
        compiler_params=pltpu.CompilerParams(vmem_limit_bytes=limit << 20),
    )(*operands)

def shaped(*shape):
    return jax.ShapeDtypeStruct(shape, bf16)


def stats_of(top, total, heads):
    lane = lax.broadcasted_iota(jnp.int32, (heads, LANES), 1)
    high = total.astype(bf16).astype(f32)
    stats = jnp.where(lane == 0, top, jnp.where(lane == 1, high, jnp.where(lane == 2, total - high, 0.0)))
    return stats.astype(bf16)

def attend_kernel(q_lat, q_rope, keys, rope, lengths, keep, give, state):
    rows, heads, width = q_lat.shape
    span = keys.shape[1]
    start = lax.axis_index("tp") * span
    for r in range(rows):
        logits = dot(q_lat[r], keys[r], ((1,), (1,)))
        logits += dot(q_rope[r], rope[r], ((0,), (0,)))
        valid = lax.broadcasted_iota(jnp.int32, (heads, span), 1) + start < lengths[r]
        logits = jnp.where(valid, score_scale * logits, very_low)
        top = jnp.max(logits, axis=1, keepdims=True).astype(bf16).astype(f32)
        probs = jnp.where(valid, jnp.exp(logits - top), 0.0)
        total = jnp.sum(probs, axis=1, keepdims=True)
        state[r, :, :width] = dot(probs.astype(bf16), keys[r]).astype(bf16)
        state[r, :, width:] = stats_of(top, total, heads)
    half = heads // 2
    core = lax.rem(lax.axis_index("tp"), 2)
    keep[...] = state[:, pl.ds(pl.multiple_of(core * half, half), half), :]
    give[...] = state[:, pl.ds(pl.multiple_of((1 - core) * half, half), half), :]

def attend(q_latent, q_rope, cache_latent, cache_rope, cache_len):
    rows, heads, width = q_latent.shape
    span = cache_latent.shape[1]
    half = shaped(rows, heads // 2, width + LANES)
    return local_call(
        attend_kernel,
        [half, half],
        [q_latent, q_rope, cache_latent, cache_rope, cache_len],
        [VMEM, VMEM, VMEM, VMEM, SMEM],
        [pltpu.VMEM((rows, heads, width + LANES), bf16)],
        flops=2_000_000_000,
    )

def join_kernel(last, *refs):
    states, out = refs[:-1], refs[-1]
    rows, heads, full = states[0].shape
    width = full - LANES
    for r in range(rows):
        stats = [s[r, :, width:].astype(f32) for s in states]
        tops = [t[:, 0:1] for t in stats]
        top = functools.reduce(jnp.maximum, tops)
        scales = [jnp.exp(t - top) for t in tops]
        total = sum(c * (t[:, 1:2] + t[:, 2:3]) for c, t in zip(scales, stats))
        summed = sum(c * s[r, :, :width].astype(f32) for c, s in zip(scales, states))
        if last:
            out[r] = (summed / total).astype(bf16)
        else:
            out[r, :, :width] = summed.astype(bf16)
            out[r, :, width:] = stats_of(top, total, heads)

def join(states, last):
    rows, heads, width = states[0].shape
    out = shaped(rows, heads, width - LANES if last else width)
    return local_call(functools.partial(join_kernel, last), out, states, [VMEM] * len(states))

def place_kernel(mine, theirs, out):
    half = mine.shape[1]
    core = lax.rem(lax.axis_index("tp"), 2)
    out[:, pl.ds(pl.multiple_of(core * half, half), half), :] = mine[...]
    out[:, pl.ds(pl.multiple_of((1 - core) * half, half), half), :] = theirs[...]

def place_heads(mine, theirs):
    rows, half, width = mine.shape
    return local_call(place_kernel, shaped(rows, 2 * half, width), [mine, theirs], [VMEM, VMEM])


def pack_kernel(spots, hidden, routes, out, tags, sems):
    size = out.shape[1] - LANES
    picks, rows = routes.shape
    spot, core = spot_and_core()
    start = pl.multiple_of((spot * 2 + core if spots > 1 else core) * size, size)
    columns = pltpu.make_async_copy(hidden.at[:, pl.ds(start, size)], out.at[:, pl.ds(0, size)], sems.at[0])
    named = pltpu.make_async_copy(routes, tags, sems.at[1])
    columns.start()
    named.start()
    out[:, size:] = jnp.zeros((rows, LANES), bf16)
    named.wait()
    eye = lax.broadcasted_iota(jnp.int32, (rows, rows), 0) == lax.broadcasted_iota(jnp.int32, (rows, rows), 1)
    turned = dot(eye.astype(f32).astype(bf16), tags[...].astype(f32).astype(bf16), ((1,), (1,)))
    out[:, size : size + picks] = turned.astype(bf16)
    columns.wait()

def pack_rows(hidden, routes, spots):
    rows, width = hidden.shape
    return local_call(
        functools.partial(pack_kernel, spots),
        shaped(rows, width // (2 * spots) + LANES),
        [pltpu.with_memory_space_constraint(a, pltpu.HBM) for a in (hidden, routes.T)],
        [ANY, ANY],
        [pltpu.VMEM(routes.shape[::-1], jnp.int32), pltpu.SemaphoreType.DMA((2,))],
        flops=WAIT_FLOPS,
        limit=2,
    )

def act_kernel(picks, ways, packs, own, mine, theirs, router, gate, up, down, act, outs, x, tags):
    rows = own.shape[0]
    spots = len(mine)
    size = mine[0].shape[1]
    local, _, hidden = gate.shape
    spot, core = spot_and_core()
    x[pl.ds(0, rows), :] = own[...]
    later = pl.ds(rows, mine[0].shape[0])
    for s in range(spots):
        first = partner(spot, s, ways) * 2 if spots > 1 else 0
        x[later, pl.ds(pl.multiple_of((first + core) * size, size), size)] = mine[s][...]
        x[later, pl.ds(pl.multiple_of((first + 1 - core) * size, size), size)] = theirs[s][...]
    for s, pack in enumerate(packs):
        tags[pl.ds(s * rows, rows), :] = pack[:, size:]

    scores = jax.nn.sigmoid(dot(x[...], router[...], ((1,), (1,))))
    labels = lax.broadcasted_iota(jnp.int32, scores.shape, 1)
    chosen = tags[...].astype(f32).astype(jnp.int32)
    picked = labels < 0
    for k in range(picks):
        picked = picked | (labels == chosen[:, k : k + 1])
    kept = jnp.where(picked, scores, 0.0)
    weights = route_scale * kept / jnp.sum(kept, axis=1, keepdims=True)
    first = lax.axis_index("dev") * local

    for e in range(local):
        rate = jnp.sum(jnp.where(labels == first + e, weights, 0.0), axis=1, keepdims=True)
        a = dot(x[...], gate[e])
        b = dot(x[...], up[e])
        act[:, e * hidden : (e + 1) * hidden] = (a / (1.0 + jnp.exp(-a)) * b * rate).astype(bf16)
    for out in outs:
        out[...] = dot(act[...], down[0][...]).astype(bf16)

def act_call(packs, own, mine, theirs, router, gate, up, down, picks, ways, whole):
    rows, width = own.shape
    local, _, hidden = gate.shape
    count = rows * len(packs)
    down = [down] if whole else []
    cuts = [len(packs), 1, len(mine), len(theirs), 3, len(down)]

    def kernel(*refs):
        groups = []
        for cut in cuts:
            groups.append(refs[:cut])
            refs = refs[cut:]
        packs, (own,), mine, theirs, (router, gate, up), down = groups
        act_kernel(picks, ways, packs, own, mine, theirs, router, gate, up, down, refs[0], refs[1:-2], *refs[-2:])

    parts = [shaped(count, width)] if whole else []
    operands = [*packs, own, *mine, *theirs, router, gate, up, *down]
    return local_call(
        kernel,
        [pltpu.VMEM((count, local * hidden), bf16)] + parts,
        operands,
        [VMEM] * len(operands),
        [pltpu.VMEM((count, width), bf16), pltpu.VMEM((count, LANES), bf16)],
        limit=10 if count <= 256 else 48,
    )

def down_call(act, down, pairs, ways):
    count = act.shape[0]
    width = down.shape[1]

    def kernel(act, down, *outs):
        spot, core = spot_and_core()
        for out, (shift, side) in zip(outs, pairs):
            size = out.shape[1]
            owner = partner(spot, shift, ways) * 2 + (1 - core if side else core)
            out[...] = dot(act[...], down[:, pl.ds(pl.multiple_of(owner * size, size), size)]).astype(bf16)

    return local_call(
        kernel,
        [shaped(count, width // (2 * ways))] * len(pairs),
        [act, down],
        [VMEM, VMEM],

    )


def on_device(
    hidden,
    routes,
    router_weight,
    gate_weight,
    up_weight,
    down_weight,
    q_latent,
    q_rope,
    cache_latent,
    cache_rope,
    cache_len,
):
    rows, width = hidden.shape
    local, _, units = gate_weight.shape
    n_dev, n_tp = lax.axis_size("dev"), lax.axis_size("tp")
    ways = n_tp // 2
    aligned = width % (n_tp * LANES) == 0
    spots = ways if aligned else 1
    share = width // (2 * spots)

    pack = pack_rows(hidden, routes, spots)
    pack, q_latent = lax.optimization_barrier((pack, q_latent))
    first = n_dev // 2
    far = over_dev(pack, first, n_dev)
    keep, give = attend(q_latent, q_rope, cache_latent, cache_rope, cache_len)
    again, keep, give = lax.optimization_barrier((pack, keep, give))
    packs = [pack] + [far if s == first else over_dev(again, s, n_dev) for s in range(1, n_dev)]
    near = [p[:, :share] for p in packs[1:]]
    first -= 1
    early = [send(near[first], "tp", along_x(s, ways)) for s in range(1, spots)]
    state = join([keep, send(give, "tp", other_core)], False)
    others = [s for s in reversed(range(1, n_dev)) if s != first + 1]
    rest = jnp.concatenate([near[s - 1] for s in others], axis=0)
    rest, state = lax.optimization_barrier((rest, state))
    late = [send(rest, "tp", along_x(s, ways)) for s in range(1, spots)]
    mine = [jnp.concatenate(near, axis=0)]
    for a, b in zip(early, late):
        come = {s: b[i * rows : (i + 1) * rows] for i, s in enumerate(others)}
        mine.append(jnp.concatenate([come.get(s, a) for s in range(1, n_dev)], axis=0))
    theirs = [send(m, "tp", other_core) for m in mine]
    states = [send(state, "tp", along_x(s, ways)) for s in range(1, ways)]
    theirs, state = lax.optimization_barrier((theirs, state))
    states = [state] + states

    gate, up, down = [
        pltpu.with_memory_space_constraint(w, pltpu.VMEM)
        for w in (gate_weight, up_weight, down_weight.reshape(local * units, width))
    ]
    act, *parts = act_call(
        packs, hidden, mine, theirs, router_weight.T, gate, up, down, routes.shape[1], ways, not aligned
    )
    def added(a, b):
        return a.astype(f32) + b.astype(f32)

    act, states = lax.optimization_barrier((act, states))
    if aligned:
        steps = range(1, ways)
        far = [send(p, "tp", other_core) for p in down_call(act, down, [(s, 1) for s in steps], ways)]
        *own, there = down_call(act, down, [(s, 0) for s in steps] + [(0, 1)], ways)
        there = send(there, "tp", other_core)
        sums = [added(a, b).astype(bf16) for a, b in zip(own, far)]
        act, sums = lax.optimization_barrier((act, sums))
        (here,) = down_call(act, down, [(0, 0)], ways)
    else:
        spot, core = spot_and_core()
        size = width // n_tp

        def block(step, side):
            return lax.dynamic_slice_in_dim(parts[0], (partner(spot, step, ways) * 2 + side) * size, size, 1)

        own = [block(s, core) for s in range(ways)]
        far = [send(block(s, 1 - core), "tp", other_core) for s in range(ways)]
        sums = [added(a, b).astype(bf16) for a, b in zip(own[1:], far[1:])]
        here, there = own[0], far[0]
    far_rows = [send(p[2 * rows :], "tp", along_x(s, ways)) for s, p in enumerate(sums, 1)]
    kept = added(here, there)
    near_rows = [kept[rows : 2 * rows].astype(bf16)] + [p[rows : 2 * rows] for p in sums]
    near_rows, far_rows = lax.optimization_barrier((jnp.concatenate(near_rows, axis=1), far_rows))
    near_rows = over_dev(near_rows, 1, n_dev).astype(f32)
    near_rows, states = lax.optimization_barrier((jnp.split(near_rows, ways, axis=1), states))
    mine = lax.optimization_barrier([added(p[:rows], q).astype(bf16) for p, q in zip(sums, near_rows[1:])])
    mine = [send(p, "tp", along_x(s, ways)) for s, p in enumerate(mine, 1)]
    kept_far = lax.optimization_barrier(kept[2 * rows :])
    for p in far_rows:
        kept_far = kept_far + p.astype(f32)
    joined = join(states, True)
    attended = place_heads(joined, send(joined, "tp", other_core))
    moe = kept[:rows] + near_rows[0]
    for s in reversed(range(2, n_dev)):
        block = kept_far[(s - 2) * rows : (s - 1) * rows].astype(bf16)
        moe, attended = lax.optimization_barrier((moe + over_dev(block, s, n_dev).astype(f32), attended))
    for p in mine:
        moe = moe + p.astype(f32)
    return (moe.astype(bf16), attended)

def solution(mesh):
    in_specs = (
        P(("group", "dev"), None),
        P(("group", "dev"), None),
        P(),
        P("dev", None, "tp"),
        P("dev", None, "tp"),
        P("dev", "tp", None),
        P(("group", "dev"), None, None),
        P(("group", "dev"), None, None),
        P(("group", "dev"), "tp", None),
        P(("group", "dev"), None, "tp"),
        P(("group", "dev")),
    )
    out_specs = (P(("group", "dev"), "tp"), P(("group", "dev"), None, None))
    return jax.shard_map(
        on_device, mesh=mesh, in_specs=in_specs, out_specs=out_specs, check_vma=False
    )
```

```python
import functools

import jax
import jax.numpy as jnp
from jax import lax
from jax.experimental import pallas as pl
from jax.experimental.pallas import tpu as pltpu
from jax.sharding import PartitionSpec as P

score_scale = 0.13524
route_scale = 2.5
very_low = -1e30
LANES = 128
WAIT_FLOPS = 100_000_000_000

f32, bf16 = jnp.float32, jnp.bfloat16
ANY = pl.BlockSpec(memory_space=pl.ANY)
VMEM = pl.BlockSpec(memory_space=pltpu.VMEM)
SMEM = pl.BlockSpec(memory_space=pltpu.SMEM)

def dot(a, b, contract=((1,), (0,))):
    return lax.dot_general(a, b, (contract, ((), ())), preferred_element_type=f32)

def send(value, axis, target):
    size = lax.axis_size(axis)
    return lax.ppermute(value, axis, [(i, target(i)) for i in range(size)])

def other_core(i):
    return i ^ 1

def partner(place, step, size):
    return place ^ step if size & (size - 1) == 0 else (step - place) % size

def along_x(step, ways):
    return lambda i: partner(i // 2, step, ways) * 2 + i % 2

def over_dev(value, step, size):
    return send(value, "dev", lambda i: partner(i, step, size))

def spot_and_core():
    tp = lax.axis_index("tp")
    return tp // 2, lax.rem(tp, 2)

def local_call(kernel, outs, operands, specs, scratch=(), flops=0, nbytes=0, exps=0, limit=8):
    return pl.pallas_call(
        kernel,
        out_shape=outs,
        in_specs=specs,
        out_specs=jax.tree.map(lambda _: VMEM, outs),
        scratch_shapes=list(scratch),
        cost_estimate=pl.CostEstimate(flops=flops, bytes_accessed=nbytes, transcendentals=exps),
        compiler_params=pltpu.CompilerParams(vmem_limit_bytes=limit << 20),
    )(*operands)

def shaped(*shape):
    return jax.ShapeDtypeStruct(shape, bf16)


def stats_of(top, total, heads):
    lane = lax.broadcasted_iota(jnp.int32, (heads, LANES), 1)
    high = total.astype(bf16).astype(f32)
    stats = jnp.where(lane == 0, top, jnp.where(lane == 1, high, jnp.where(lane == 2, total - high, 0.0)))
    return stats.astype(bf16)

def attend_kernel(q_lat, q_rope, keys, rope, lengths, keep, give, state):
    rows, heads, width = q_lat.shape
    span = keys.shape[1]
    start = lax.axis_index("tp") * span
    for r in range(rows):
        logits = dot(q_lat[r], keys[r], ((1,), (1,)))
        logits += dot(q_rope[r], rope[r], ((0,), (0,)))
        valid = lax.broadcasted_iota(jnp.int32, (heads, span), 1) + start < lengths[r]
        logits = jnp.where(valid, score_scale * logits, very_low)
        top = jnp.max(logits, axis=1, keepdims=True).astype(bf16).astype(f32)
        probs = jnp.where(valid, jnp.exp(logits - top), 0.0)
        total = jnp.sum(probs, axis=1, keepdims=True)
        state[r, :, :width] = dot(probs.astype(bf16), keys[r]).astype(bf16)
        state[r, :, width:] = stats_of(top, total, heads)
    half = heads // 2
    core = lax.rem(lax.axis_index("tp"), 2)
    keep[...] = state[:, pl.ds(pl.multiple_of(core * half, half), half), :]
    give[...] = state[:, pl.ds(pl.multiple_of((1 - core) * half, half), half), :]

def attend(q_latent, q_rope, cache_latent, cache_rope, cache_len):
    rows, heads, width = q_latent.shape
    span = cache_latent.shape[1]
    half = shaped(rows, heads // 2, width + LANES)
    return local_call(
        attend_kernel,
        [half, half],
        [q_latent, q_rope, cache_latent, cache_rope, cache_len],
        [VMEM, VMEM, VMEM, VMEM, SMEM],
        [pltpu.VMEM((rows, heads, width + LANES), bf16)],
        flops=2_000_000_000,
    )

def join_kernel(last, *refs):
    states, out = refs[:-1], refs[-1]
    rows, heads, full = states[0].shape
    width = full - LANES
    for r in range(rows):
        stats = [s[r, :, width:].astype(f32) for s in states]
        tops = [t[:, 0:1] for t in stats]
        top = functools.reduce(jnp.maximum, tops)
        scales = [jnp.exp(t - top) for t in tops]
        total = sum(c * (t[:, 1:2] + t[:, 2:3]) for c, t in zip(scales, stats))
        summed = sum(c * s[r, :, :width].astype(f32) for c, s in zip(scales, states))
        if last:
            out[r] = (summed / total).astype(bf16)
        else:
            out[r, :, :width] = summed.astype(bf16)
            out[r, :, width:] = stats_of(top, total, heads)

def join(states, last):
    rows, heads, width = states[0].shape
    out = shaped(rows, heads, width - LANES if last else width)
    return local_call(functools.partial(join_kernel, last), out, states, [VMEM] * len(states))

def place_kernel(mine, theirs, out):
    half = mine.shape[1]
    core = lax.rem(lax.axis_index("tp"), 2)
    out[:, pl.ds(pl.multiple_of(core * half, half), half), :] = mine[...]
    out[:, pl.ds(pl.multiple_of((1 - core) * half, half), half), :] = theirs[...]

def place_heads(mine, theirs):
    rows, half, width = mine.shape
    return local_call(place_kernel, shaped(rows, 2 * half, width), [mine, theirs], [VMEM, VMEM])


def pack_kernel(spots, hidden, routes, out, tags, sems):
    size = out.shape[1] - LANES
    picks, rows = routes.shape
    spot, core = spot_and_core()
    start = pl.multiple_of((spot * 2 + core if spots > 1 else core) * size, size)
    columns = pltpu.make_async_copy(hidden.at[:, pl.ds(start, size)], out.at[:, pl.ds(0, size)], sems.at[0])
    named = pltpu.make_async_copy(routes, tags, sems.at[1])
    columns.start()
    named.start()
    out[:, size:] = jnp.zeros((rows, LANES), bf16)
    named.wait()
    eye = lax.broadcasted_iota(jnp.int32, (rows, rows), 0) == lax.broadcasted_iota(jnp.int32, (rows, rows), 1)
    turned = dot(eye.astype(f32).astype(bf16), tags[...].astype(f32).astype(bf16), ((1,), (1,)))
    out[:, size : size + picks] = turned.astype(bf16)
    columns.wait()

def pack_rows(hidden, routes, spots):
    rows, width = hidden.shape
    return local_call(
        functools.partial(pack_kernel, spots),
        shaped(rows, width // (2 * spots) + LANES),
        [pltpu.with_memory_space_constraint(a, pltpu.HBM) for a in (hidden, routes.T)],
        [ANY, ANY],
        [pltpu.VMEM(routes.shape[::-1], jnp.int32), pltpu.SemaphoreType.DMA((2,))],
        flops=WAIT_FLOPS,
        limit=2,
    )

def act_kernel(picks, ways, packs, own, mine, theirs, router, gate, up, down, act, outs, x, tags):
    rows = own.shape[0]
    spots = len(mine)
    size = mine[0].shape[1]
    local, _, hidden = gate.shape
    spot, core = spot_and_core()
    x[pl.ds(0, rows), :] = own[...]
    later = pl.ds(rows, mine[0].shape[0])
    for s in range(spots):
        first = partner(spot, s, ways) * 2 if spots > 1 else 0
        x[later, pl.ds(pl.multiple_of((first + core) * size, size), size)] = mine[s][...]
        x[later, pl.ds(pl.multiple_of((first + 1 - core) * size, size), size)] = theirs[s][...]
    for s, pack in enumerate(packs):
        tags[pl.ds(s * rows, rows), :] = pack[:, size:]

    scores = jax.nn.sigmoid(dot(x[...], router[...], ((1,), (1,))))
    labels = lax.broadcasted_iota(jnp.int32, scores.shape, 1)
    chosen = tags[...].astype(f32).astype(jnp.int32)
    picked = labels < 0
    for k in range(picks):
        picked = picked | (labels == chosen[:, k : k + 1])
    kept = jnp.where(picked, scores, 0.0)
    weights = route_scale * kept / jnp.sum(kept, axis=1, keepdims=True)
    first = lax.axis_index("dev") * local

    for e in range(local):
        rate = jnp.sum(jnp.where(labels == first + e, weights, 0.0), axis=1, keepdims=True)
        a = dot(x[...], gate[e])
        b = dot(x[...], up[e])
        act[:, e * hidden : (e + 1) * hidden] = (a / (1.0 + jnp.exp(-a)) * b * rate).astype(bf16)
    for out in outs:
        out[...] = dot(act[...], down[0][...]).astype(bf16)

def act_call(packs, own, mine, theirs, router, gate, up, down, picks, ways, whole):
    rows, width = own.shape
    local, _, hidden = gate.shape
    count = rows * len(packs)
    down = [down] if whole else []
    cuts = [len(packs), 1, len(mine), len(theirs), 3, len(down)]

    def kernel(*refs):
        groups = []
        for cut in cuts:
            groups.append(refs[:cut])
            refs = refs[cut:]
        packs, (own,), mine, theirs, (router, gate, up), down = groups
        act_kernel(picks, ways, packs, own, mine, theirs, router, gate, up, down, refs[0], refs[1:-2], *refs[-2:])

    parts = [shaped(count, width)] if whole else []
    operands = [*packs, own, *mine, *theirs, router, gate, up, *down]
    return local_call(
        kernel,
        [pltpu.VMEM((count, local * hidden), bf16)] + parts,
        operands,
        [VMEM] * len(operands),
        [pltpu.VMEM((count, width), bf16), pltpu.VMEM((count, LANES), bf16)],
        limit=10 if count <= 256 else 48,
    )

def down_call(act, down, pairs, ways):
    count = act.shape[0]
    width = down.shape[1]

    def kernel(act, down, *outs):
        spot, core = spot_and_core()
        for out, (shift, side) in zip(outs, pairs):
            size = out.shape[1]
            owner = partner(spot, shift, ways) * 2 + (1 - core if side else core)
            out[...] = dot(act[...], down[:, pl.ds(pl.multiple_of(owner * size, size), size)]).astype(bf16)

    return local_call(
        kernel,
        [shaped(count, width // (2 * ways))] * len(pairs),
        [act, down],
        [VMEM, VMEM],
    )


def on_device(
    hidden,
    routes,
    router_weight,
    gate_weight,
    up_weight,
    down_weight,
    q_latent,
    q_rope,
    cache_latent,
    cache_rope,
    cache_len,
):
    rows, width = hidden.shape
    local, _, units = gate_weight.shape
    n_dev, n_tp = lax.axis_size("dev"), lax.axis_size("tp")
    ways = n_tp // 2
    aligned = width % (n_tp * LANES) == 0
    spots = ways if aligned else 1
    share = width // (2 * spots)

    pack = pack_rows(hidden, routes, spots)
    pack, q_latent = lax.optimization_barrier((pack, q_latent))
    first = n_dev - 1
    far = over_dev(pack, first, n_dev)
    keep, give = attend(q_latent, q_rope, cache_latent, cache_rope, cache_len)
    again, keep, give = lax.optimization_barrier((pack, keep, give))
    packs = [pack] + [far if s == first else over_dev(again, s, n_dev) for s in range(1, n_dev)]
    near = [p[:, :share] for p in packs[1:]]
    first -= 1
    early = [send(near[first], "tp", along_x(s, ways)) for s in range(1, spots)]
    state = join([keep, send(give, "tp", other_core)], False)
    others = [s for s in reversed(range(1, n_dev)) if s != first + 1]
    rest = jnp.concatenate([near[s - 1] for s in others], axis=0)
    rest, state = lax.optimization_barrier((rest, state))
    late = [send(rest, "tp", along_x(s, ways)) for s in range(1, spots)]
    mine = [jnp.concatenate(near, axis=0)]
    for a, b in zip(early, late):
        come = {s: b[i * rows : (i + 1) * rows] for i, s in enumerate(others)}
        mine.append(jnp.concatenate([come.get(s, a) for s in range(1, n_dev)], axis=0))
    theirs = [send(m, "tp", other_core) for m in mine]
    states = [send(state, "tp", along_x(s, ways)) for s in range(1, ways)]
    theirs, state = lax.optimization_barrier((theirs, state))
    states = [state] + states

    gate, up, down = [
        pltpu.with_memory_space_constraint(w, pltpu.VMEM)
        for w in (gate_weight, up_weight, down_weight.reshape(local * units, width))
    ]
    act, *parts = act_call(
        packs, hidden, mine, theirs, router_weight.T, gate, up, down, routes.shape[1], ways, not aligned
    )
    def added(a, b):
        return a.astype(f32) + b.astype(f32)

    act, states = lax.optimization_barrier((act, states))
    if aligned:
        steps = range(1, ways)
        far = [send(p, "tp", other_core) for p in down_call(act, down, [(s, 1) for s in steps], ways)]
        *own, there = down_call(act, down, [(s, 0) for s in steps] + [(0, 1)], ways)
        there = send(there, "tp", other_core)
        sums = [added(a, b).astype(bf16) for a, b in zip(own, far)]
        act, sums, states = lax.optimization_barrier((act, sums, states))
        (here,) = down_call(act, down, [(0, 0)], ways)
    else:
        spot, core = spot_and_core()
        size = width // n_tp

        def block(step, side):
            return lax.dynamic_slice_in_dim(parts[0], (partner(spot, step, ways) * 2 + side) * size, size, 1)

        own = [block(s, core) for s in range(ways)]
        far = [send(block(s, 1 - core), "tp", other_core) for s in range(ways)]
        sums = [added(a, b).astype(bf16) for a, b in zip(own[1:], far[1:])]
        here, there = own[0], far[0]
    total = added(here, there)
    for s, p in enumerate(sums, 1):
        total = total + send(p, "tp", along_x(s, ways)).astype(f32)
    joined = join(states, True)
    attended = place_heads(joined, send(joined, "tp", other_core))
    blocks = [total[i : i + rows] for i in range(0, total.shape[0], rows)]
    moe = blocks[0]
    for s in reversed(range(1, n_dev)):
        moe, attended = lax.optimization_barrier((moe, attended))
        moe = moe + over_dev(blocks[s].astype(bf16), s, n_dev).astype(f32)
    return (moe.astype(bf16), attended)

def solution(mesh):
    in_specs = (
        P(("group", "dev"), None),
        P(("group", "dev"), None),
        P(),
        P("dev", None, "tp"),
        P("dev", None, "tp"),
        P("dev", "tp", None),
        P(("group", "dev"), None, None),
        P(("group", "dev"), None, None),
        P(("group", "dev"), "tp", None),
        P(("group", "dev"), None, "tp"),
        P(("group", "dev")),
    )
    out_specs = (P(("group", "dev"), "tp"), P(("group", "dev"), None, None))
    return jax.shard_map(
        on_device, mesh=mesh, in_specs=in_specs, out_specs=out_specs, check_vma=False
    )
```

```python
import functools

import jax
import jax.numpy as jnp
from jax import lax
from jax.experimental import pallas as pl
from jax.experimental.pallas import tpu as pltpu
from jax.sharding import PartitionSpec as P

score_scale = 0.13524
route_scale = 2.5
very_low = -1e30
LANES = 128
WAIT_FLOPS = 100_000_000_000

f32, bf16 = jnp.float32, jnp.bfloat16
ANY = pl.BlockSpec(memory_space=pl.ANY)
VMEM = pl.BlockSpec(memory_space=pltpu.VMEM)
SMEM = pl.BlockSpec(memory_space=pltpu.SMEM)

def dot(a, b, contract=((1,), (0,))):
    return lax.dot_general(a, b, (contract, ((), ())), preferred_element_type=f32)

def send(value, axis, target):
    size = lax.axis_size(axis)
    return lax.ppermute(value, axis, [(i, target(i)) for i in range(size)])

def other_core(i):
    return i ^ 1

def partner(place, step, size):
    return place ^ step if size & (size - 1) == 0 else (step - place) % size

def along_x(step, ways):
    return lambda i: partner(i // 2, step, ways) * 2 + i % 2

def over_dev(value, step, size):
    return send(value, "dev", lambda i: partner(i, step, size))

def spot_and_core():
    tp = lax.axis_index("tp")
    return tp // 2, lax.rem(tp, 2)

def local_call(kernel, outs, operands, specs, scratch=(), flops=0, nbytes=0, exps=0, limit=8):
    return pl.pallas_call(
        kernel,
        out_shape=outs,
        in_specs=specs,
        out_specs=jax.tree.map(lambda _: VMEM, outs),
        scratch_shapes=list(scratch),
        cost_estimate=pl.CostEstimate(flops=flops, bytes_accessed=nbytes, transcendentals=exps),
        compiler_params=pltpu.CompilerParams(vmem_limit_bytes=limit << 20),
    )(*operands)

def shaped(*shape):
    return jax.ShapeDtypeStruct(shape, bf16)


def stats_of(top, total, heads):
    lane = lax.broadcasted_iota(jnp.int32, (heads, LANES), 1)
    high = total.astype(bf16).astype(f32)
    stats = jnp.where(lane == 0, top, jnp.where(lane == 1, high, jnp.where(lane == 2, total - high, 0.0)))
    return stats.astype(bf16)

def attend_kernel(q_lat, q_rope, keys, rope, lengths, keep, give, state):
    rows, heads, width = q_lat.shape
    span = keys.shape[1]
    start = lax.axis_index("tp") * span
    for r in range(rows):
        logits = dot(q_lat[r], keys[r], ((1,), (1,)))
        logits += dot(q_rope[r], rope[r], ((0,), (0,)))
        valid = lax.broadcasted_iota(jnp.int32, (heads, span), 1) + start < lengths[r]
        logits = jnp.where(valid, score_scale * logits, very_low)
        top = jnp.max(logits, axis=1, keepdims=True).astype(bf16).astype(f32)
        probs = jnp.where(valid, jnp.exp(logits - top), 0.0)
        total = jnp.sum(probs, axis=1, keepdims=True)
        state[r, :, :width] = dot(probs.astype(bf16), keys[r]).astype(bf16)
        state[r, :, width:] = stats_of(top, total, heads)
    half = heads // 2
    core = lax.rem(lax.axis_index("tp"), 2)
    keep[...] = state[:, pl.ds(pl.multiple_of(core * half, half), half), :]
    give[...] = state[:, pl.ds(pl.multiple_of((1 - core) * half, half), half), :]

def attend(q_latent, q_rope, cache_latent, cache_rope, cache_len):
    rows, heads, width = q_latent.shape
    span = cache_latent.shape[1]
    half = shaped(rows, heads // 2, width + LANES)
    return local_call(
        attend_kernel,
        [half, half],
        [q_latent, q_rope, cache_latent, cache_rope, cache_len],
        [VMEM, VMEM, VMEM, VMEM, SMEM],
        [pltpu.VMEM((rows, heads, width + LANES), bf16)],
        flops=2_000_000_000,
    )

def join_kernel(last, *refs):
    states, out = refs[:-1], refs[-1]
    rows, heads, full = states[0].shape
    width = full - LANES
    for r in range(rows):
        stats = [s[r, :, width:].astype(f32) for s in states]
        tops = [t[:, 0:1] for t in stats]
        top = functools.reduce(jnp.maximum, tops)
        scales = [jnp.exp(t - top) for t in tops]
        total = sum(c * (t[:, 1:2] + t[:, 2:3]) for c, t in zip(scales, stats))
        summed = sum(c * s[r, :, :width].astype(f32) for c, s in zip(scales, states))
        if last:
            out[r] = (summed / total).astype(bf16)
        else:
            out[r, :, :width] = summed.astype(bf16)
            out[r, :, width:] = stats_of(top, total, heads)

def join(states, last):
    rows, heads, width = states[0].shape
    out = shaped(rows, heads, width - LANES if last else width)
    return local_call(functools.partial(join_kernel, last), out, states, [VMEM] * len(states))

def place_kernel(mine, theirs, out):
    half = mine.shape[1]
    core = lax.rem(lax.axis_index("tp"), 2)
    out[:, pl.ds(pl.multiple_of(core * half, half), half), :] = mine[...]
    out[:, pl.ds(pl.multiple_of((1 - core) * half, half), half), :] = theirs[...]

def place_heads(mine, theirs):
    rows, half, width = mine.shape
    return local_call(place_kernel, shaped(rows, 2 * half, width), [mine, theirs], [VMEM, VMEM])


def pack_kernel(spots, ways, hidden, routes, wide, narrow, tags, sems):
    size = narrow.shape[1] - LANES
    picks, rows = routes.shape
    spot, core = spot_and_core()
    copies = [pltpu.make_async_copy(routes, tags, sems.at[0])]
    for s in range(spots):
        first = partner(spot, s, ways) * 2 if spots > 1 else 0
        columns = hidden.at[:, pl.ds(pl.multiple_of((first + core) * size, size), size)]
        copies.append(pltpu.make_async_copy(columns, wide.at[:, pl.ds(s * size, size)], sems.at[1 + s]))
        if s == 0:
            copies.append(pltpu.make_async_copy(columns, narrow.at[:, pl.ds(0, size)], sems.at[1 + spots]))
    for copy in copies:
        copy.start()
    blank = jnp.zeros((rows, LANES), bf16)
    wide[:, spots * size :] = blank
    narrow[:, size:] = blank
    copies[0].wait()
    eye = lax.broadcasted_iota(jnp.int32, (rows, rows), 0) == lax.broadcasted_iota(jnp.int32, (rows, rows), 1)
    turned = dot(eye.astype(f32).astype(bf16), tags[...].astype(f32).astype(bf16), ((1,), (1,))).astype(bf16)
    wide[:, spots * size : spots * size + picks] = turned
    narrow[:, size : size + picks] = turned
    for copy in copies[1:]:
        copy.wait()

def pack_rows(hidden, routes, spots, ways):
    rows, width = hidden.shape
    return local_call(
        functools.partial(pack_kernel, spots, ways),
        [shaped(rows, width // 2 + LANES), shaped(rows, width // (2 * spots) + LANES)],
        [pltpu.with_memory_space_constraint(a, pltpu.HBM) for a in (hidden, routes.T)],
        [ANY, ANY],
        [pltpu.VMEM(routes.shape[::-1], jnp.int32), pltpu.SemaphoreType.DMA((2 + spots,))],
        flops=WAIT_FLOPS,
        limit=2,
    )

def act_kernel(picks, ways, packs, own, mine, theirs, router, gate, up, down, act, outs, x, tags):
    rows = own.shape[0]
    spots = len(mine)
    size = mine[0].shape[1]
    local, _, hidden = gate.shape
    spot, core = spot_and_core()
    x[pl.ds(0, rows), :] = own[...]
    later = pl.ds(rows, mine[0].shape[0])
    for s in range(spots):
        first = partner(spot, s, ways) * 2 if spots > 1 else 0
        x[later, pl.ds(pl.multiple_of((first + core) * size, size), size)] = mine[s][...]
        x[later, pl.ds(pl.multiple_of((first + 1 - core) * size, size), size)] = theirs[s][...]
    for s, pack in enumerate(packs):
        tags[pl.ds(s * rows, rows), :] = pack[:, pack.shape[1] - LANES :]

    scores = jax.nn.sigmoid(dot(x[...], router[...], ((1,), (1,))))
    labels = lax.broadcasted_iota(jnp.int32, scores.shape, 1)
    chosen = tags[...].astype(f32).astype(jnp.int32)
    picked = labels < 0
    for k in range(picks):
        picked = picked | (labels == chosen[:, k : k + 1])
    kept = jnp.where(picked, scores, 0.0)
    weights = route_scale * kept / jnp.sum(kept, axis=1, keepdims=True)
    first = lax.axis_index("dev") * local

    for e in range(local):
        rate = jnp.sum(jnp.where(labels == first + e, weights, 0.0), axis=1, keepdims=True)
        a = dot(x[...], gate[e])
        b = dot(x[...], up[e])
        act[:, e * hidden : (e + 1) * hidden] = (a / (1.0 + jnp.exp(-a)) * b * rate).astype(bf16)
    for out in outs:
        out[...] = dot(act[...], down[0][...]).astype(bf16)

def act_call(packs, own, mine, theirs, router, gate, up, down, picks, ways, whole):
    rows, width = own.shape
    local, _, hidden = gate.shape
    count = rows * len(packs)
    down = [down] if whole else []
    cuts = [len(packs), 1, len(mine), len(theirs), 3, len(down)]

    def kernel(*refs):
        groups = []
        for cut in cuts:
            groups.append(refs[:cut])
            refs = refs[cut:]
        packs, (own,), mine, theirs, (router, gate, up), down = groups
        act_kernel(picks, ways, packs, own, mine, theirs, router, gate, up, down, refs[0], refs[1:-2], *refs[-2:])

    parts = [shaped(count, width)] if whole else []
    operands = [*packs, own, *mine, *theirs, router, gate, up, *down]
    return local_call(
        kernel,
        [pltpu.VMEM((count, local * hidden), bf16)] + parts,
        operands,
        [VMEM] * len(operands),
        [pltpu.VMEM((count, width), bf16), pltpu.VMEM((count, LANES), bf16)],
        limit=10 if count <= 256 else 48,
    )

def down_call(act, down, pairs, ways):
    count = act.shape[0]
    width = down.shape[1]

    def kernel(act, down, *outs):
        spot, core = spot_and_core()
        for out, (shift, side) in zip(outs, pairs):
            size = out.shape[1]
            owner = partner(spot, shift, ways) * 2 + (1 - core if side else core)
            out[...] = dot(act[...], down[:, pl.ds(pl.multiple_of(owner * size, size), size)]).astype(bf16)

    return local_call(
        kernel,
        [shaped(count, width // (2 * ways))] * len(pairs),
        [act, down],
        [VMEM, VMEM],
    )


def on_device(
    hidden,
    routes,
    router_weight,
    gate_weight,
    up_weight,
    down_weight,
    q_latent,
    q_rope,
    cache_latent,
    cache_rope,
    cache_len,
):
    rows, width = hidden.shape
    local, _, units = gate_weight.shape
    n_dev, n_tp = lax.axis_size("dev"), lax.axis_size("tp")
    ways = n_tp // 2
    aligned = width % (n_tp * LANES) == 0
    spots = ways if aligned else 1
    share = width // (2 * spots)

    wide, narrow = pack_rows(hidden, routes, spots, ways)
    wide, narrow, q_latent = lax.optimization_barrier((wide, narrow, q_latent))
    first = n_dev - 1
    far = over_dev(narrow, first, n_dev)
    keep, give = attend(q_latent, q_rope, cache_latent, cache_rope, cache_len)
    wide, again, keep, give = lax.optimization_barrier((wide, narrow, keep, give))
    packs = [narrow, over_dev(wide, 1, n_dev)]
    packs += [far if s == first else over_dev(again, s, n_dev) for s in range(2, n_dev)]
    near = [p[:, :share] for p in packs[1:]]
    early = [send(near[first - 1], "tp", along_x(s, ways)) for s in range(1, spots)]
    state = join([keep, send(give, "tp", other_core)], False)
    rest = jnp.concatenate(near[1 : first - 1], axis=0)
    rest, early = lax.optimization_barrier((rest, early))
    late = [send(rest, "tp", along_x(s, ways)) for s in range(1, spots)]
    neighbour, late, state = lax.optimization_barrier((packs[1], late, state))
    packs[1] = neighbour
    near[0] = neighbour[:, :share]
    mine = [jnp.concatenate(near, axis=0)]
    for s, (a, b) in enumerate(zip(early, late), 1):
        mine.append(jnp.concatenate([neighbour[:, s * share : (s + 1) * share], b, a], axis=0))
    theirs = jnp.split(send(jnp.concatenate(mine, axis=0), "tp", other_core), spots)
    states = [send(state, "tp", along_x(s, ways)) for s in range(1, ways)]
    theirs, state = lax.optimization_barrier((theirs, state))
    states = [state] + states

    gate, up, down = [
        pltpu.with_memory_space_constraint(w, pltpu.VMEM)
        for w in (gate_weight, up_weight, down_weight.reshape(local * units, width))
    ]
    act, *parts = act_call(
        packs, hidden, mine, theirs, router_weight.T, gate, up, down, routes.shape[1], ways, not aligned
    )
    def added(a, b):
        return a.astype(f32) + b.astype(f32)

    if aligned:
        steps = range(1, ways)
        far = down_call(act, down, [(s, 1) for s in steps], ways)
        far, act, states = lax.optimization_barrier((far, act, states))
        far = [send(p, "tp", other_core) for p in far]
        *own, there = down_call(act, down, [(s, 0) for s in steps] + [(0, 1)], ways)
        there = send(there, "tp", other_core)
        sums = [added(a, b).astype(bf16) for a, b in zip(own, far)]
        act, sums, states = lax.optimization_barrier((act, sums, states))
        (here,) = down_call(act, down, [(0, 0)], ways)
    else:
        spot, core = spot_and_core()
        size = width // n_tp

        def block(step, side):
            return lax.dynamic_slice_in_dim(parts[0], (partner(spot, step, ways) * 2 + side) * size, size, 1)

        own = [block(s, core) for s in range(ways)]
        far = [send(block(s, 1 - core), "tp", other_core) for s in range(ways)]
        sums = [added(a, b).astype(bf16) for a, b in zip(own[1:], far[1:])]
        here, there = own[0], far[0]
    sums = [send(p, "tp", along_x(s, ways)) for s, p in enumerate(sums, 1)]
    joined = join(states, True)
    attended = place_heads(joined, send(joined, "tp", other_core))
    sums, attended = lax.optimization_barrier((sums, attended))
    total = added(here, there)
    for p in sums:
        total = total + p.astype(f32)
    blocks = [total[i : i + rows] for i in range(0, total.shape[0], rows)]
    moe = blocks[0]
    for s in reversed(range(1, n_dev)):
        moe = lax.optimization_barrier(moe)
        moe = moe + over_dev(blocks[s].astype(bf16), s, n_dev).astype(f32)
    return (moe.astype(bf16), attended)

def solution(mesh):
    in_specs = (
        P(("group", "dev"), None),
        P(("group", "dev"), None),
        P(),
        P("dev", None, "tp"),
        P("dev", None, "tp"),
        P("dev", "tp", None),
        P(("group", "dev"), None, None),
        P(("group", "dev"), None, None),
        P(("group", "dev"), "tp", None),
        P(("group", "dev"), None, "tp"),
        P(("group", "dev")),
    )
    out_specs = (P(("group", "dev"), "tp"), P(("group", "dev"), None, None))
    return jax.shard_map(
        on_device, mesh=mesh, in_specs=in_specs, out_specs=out_specs, check_vma=False
    )
```

```python
import functools

import jax
import jax.numpy as jnp
from jax import lax
from jax.experimental import pallas as pl
from jax.experimental.pallas import tpu as pltpu
from jax.sharding import PartitionSpec as P

score_scale = 0.13524
route_scale = 2.5
very_low = -1e30
LANES = 128
WAIT_FLOPS = 100_000_000_000

f32, bf16 = jnp.float32, jnp.bfloat16
ANY = pl.BlockSpec(memory_space=pl.ANY)
VMEM = pl.BlockSpec(memory_space=pltpu.VMEM)
SMEM = pl.BlockSpec(memory_space=pltpu.SMEM)

def dot(a, b, contract=((1,), (0,))):
    return lax.dot_general(a, b, (contract, ((), ())), preferred_element_type=f32)

def send(value, axis, target):
    size = lax.axis_size(axis)
    return lax.ppermute(value, axis, [(i, target(i)) for i in range(size)])

def other_core(i):
    return i ^ 1

def partner(place, step, size):
    return place ^ step if size & (size - 1) == 0 else (step - place) % size

def along_x(step, ways):
    return lambda i: partner(i // 2, step, ways) * 2 + i % 2

def over_dev(value, step, size):
    return send(value, "dev", lambda i: partner(i, step, size))

def spot_and_core():
    tp = lax.axis_index("tp")
    return tp // 2, lax.rem(tp, 2)

def local_call(kernel, outs, operands, specs, scratch=(), flops=0, nbytes=0, exps=0, limit=8):
    return pl.pallas_call(
        kernel,
        out_shape=outs,
        in_specs=specs,
        out_specs=jax.tree.map(lambda _: VMEM, outs),
        scratch_shapes=list(scratch),
        cost_estimate=pl.CostEstimate(flops=flops, bytes_accessed=nbytes, transcendentals=exps),
        compiler_params=pltpu.CompilerParams(vmem_limit_bytes=limit << 20),
    )(*operands)

def shaped(*shape):
    return jax.ShapeDtypeStruct(shape, bf16)


def stats_of(top, total, heads):
    lane = lax.broadcasted_iota(jnp.int32, (heads, LANES), 1)
    high = total.astype(bf16).astype(f32)
    stats = jnp.where(lane == 0, top, jnp.where(lane == 1, high, jnp.where(lane == 2, total - high, 0.0)))
    return stats.astype(bf16)

def attend_kernel(q_lat, q_rope, keys, rope, lengths, keep, give, state):
    rows, heads, width = q_lat.shape
    span = keys.shape[1]
    start = lax.axis_index("tp") * span
    for r in range(rows):
        logits = dot(q_lat[r], keys[r], ((1,), (1,)))
        logits += dot(q_rope[r], rope[r], ((0,), (0,)))
        valid = lax.broadcasted_iota(jnp.int32, (heads, span), 1) + start < lengths[r]
        logits = jnp.where(valid, score_scale * logits, very_low)
        top = jnp.max(logits, axis=1, keepdims=True).astype(bf16).astype(f32)
        probs = jnp.where(valid, jnp.exp(logits - top), 0.0)
        total = jnp.sum(probs, axis=1, keepdims=True)
        state[r, :, :width] = dot(probs.astype(bf16), keys[r]).astype(bf16)
        state[r, :, width:] = stats_of(top, total, heads)
    half = heads // 2
    core = lax.rem(lax.axis_index("tp"), 2)
    keep[...] = state[:, pl.ds(pl.multiple_of(core * half, half), half), :]
    give[...] = state[:, pl.ds(pl.multiple_of((1 - core) * half, half), half), :]

def attend(q_latent, q_rope, cache_latent, cache_rope, cache_len):
    rows, heads, width = q_latent.shape
    span = cache_latent.shape[1]
    half = shaped(rows, heads // 2, width + LANES)
    return local_call(
        attend_kernel,
        [half, half],
        [q_latent, q_rope, cache_latent, cache_rope, cache_len],
        [VMEM, VMEM, VMEM, VMEM, SMEM],
        [pltpu.VMEM((rows, heads, width + LANES), bf16)],
        flops=2_000_000_000,
    )

def join_kernel(last, *refs):
    states, out = refs[:-1], refs[-1]
    rows, heads, full = states[0].shape
    width = full - LANES
    for r in range(rows):
        stats = [s[r, :, width:].astype(f32) for s in states]
        tops = [t[:, 0:1] for t in stats]
        top = functools.reduce(jnp.maximum, tops)
        scales = [jnp.exp(t - top) for t in tops]
        total = sum(c * (t[:, 1:2] + t[:, 2:3]) for c, t in zip(scales, stats))
        summed = sum(c * s[r, :, :width].astype(f32) for c, s in zip(scales, states))
        if last:
            out[r] = (summed / total).astype(bf16)
        else:
            out[r, :, :width] = summed.astype(bf16)
            out[r, :, width:] = stats_of(top, total, heads)

def join(states, last):
    rows, heads, width = states[0].shape
    out = shaped(rows, heads, width - LANES if last else width)
    return local_call(functools.partial(join_kernel, last), out, states, [VMEM] * len(states))

def place_kernel(mine, theirs, out):
    half = mine.shape[1]
    core = lax.rem(lax.axis_index("tp"), 2)
    out[:, pl.ds(pl.multiple_of(core * half, half), half), :] = mine[...]
    out[:, pl.ds(pl.multiple_of((1 - core) * half, half), half), :] = theirs[...]

def place_heads(mine, theirs):
    rows, half, width = mine.shape
    return local_call(place_kernel, shaped(rows, 2 * half, width), [mine, theirs], [VMEM, VMEM])


def pack_kernel(spots, hidden, routes, out, tags, sems):
    size = out.shape[1] - LANES
    picks, rows = routes.shape
    spot, core = spot_and_core()
    start = pl.multiple_of((spot * 2 + core if spots > 1 else core) * size, size)
    columns = pltpu.make_async_copy(hidden.at[:, pl.ds(start, size)], out.at[:, pl.ds(0, size)], sems.at[0])
    named = pltpu.make_async_copy(routes, tags, sems.at[1])
    columns.start()
    named.start()
    out[:, size:] = jnp.zeros((rows, LANES), bf16)
    named.wait()
    eye = lax.broadcasted_iota(jnp.int32, (rows, rows), 0) == lax.broadcasted_iota(jnp.int32, (rows, rows), 1)
    turned = dot(eye.astype(f32).astype(bf16), tags[...].astype(f32).astype(bf16), ((1,), (1,)))
    out[:, size : size + picks] = turned.astype(bf16)
    columns.wait()

def pack_rows(hidden, routes, spots):
    rows, width = hidden.shape
    return local_call(
        functools.partial(pack_kernel, spots),
        shaped(rows, width // (2 * spots) + LANES),
        [pltpu.with_memory_space_constraint(a, pltpu.HBM) for a in (hidden, routes.T)],
        [ANY, ANY],
        [pltpu.VMEM(routes.shape[::-1], jnp.int32), pltpu.SemaphoreType.DMA((2,))],
        flops=WAIT_FLOPS,
        limit=2,
    )

def act_kernel(picks, ways, packs, own, mine, theirs, router, gate, up, down, act, outs, x, tags):
    rows = own.shape[0]
    spots = len(mine)
    size = mine[0].shape[1]
    local, _, hidden = gate.shape
    spot, core = spot_and_core()
    x[pl.ds(0, rows), :] = own[...]
    later = pl.ds(rows, mine[0].shape[0])
    for s in range(spots):
        first = partner(spot, s, ways) * 2 if spots > 1 else 0
        x[later, pl.ds(pl.multiple_of((first + core) * size, size), size)] = mine[s][...]
        x[later, pl.ds(pl.multiple_of((first + 1 - core) * size, size), size)] = theirs[s][...]
    for s, pack in enumerate(packs):
        tags[pl.ds(s * rows, rows), :] = pack[:, size:]

    scores = jax.nn.sigmoid(dot(x[...], router[...], ((1,), (1,))))
    labels = lax.broadcasted_iota(jnp.int32, scores.shape, 1)
    chosen = tags[...].astype(f32).astype(jnp.int32)
    picked = labels < 0
    for k in range(picks):
        picked = picked | (labels == chosen[:, k : k + 1])
    kept = jnp.where(picked, scores, 0.0)
    weights = route_scale * kept / jnp.sum(kept, axis=1, keepdims=True)
    first = lax.axis_index("dev") * local

    for e in range(local):
        rate = jnp.sum(jnp.where(labels == first + e, weights, 0.0), axis=1, keepdims=True)
        a = dot(x[...], gate[e])
        b = dot(x[...], up[e])
        act[:, e * hidden : (e + 1) * hidden] = (a / (1.0 + jnp.exp(-a)) * b * rate).astype(bf16)
    for out in outs:
        out[...] = dot(act[...], down[0][...]).astype(bf16)

def act_call(packs, own, mine, theirs, router, gate, up, down, picks, ways, whole):
    rows, width = own.shape
    local, _, hidden = gate.shape
    count = rows * len(packs)
    down = [down] if whole else []
    cuts = [len(packs), 1, len(mine), len(theirs), 3, len(down)]

    def kernel(*refs):
        groups = []
        for cut in cuts:
            groups.append(refs[:cut])
            refs = refs[cut:]
        packs, (own,), mine, theirs, (router, gate, up), down = groups
        act_kernel(picks, ways, packs, own, mine, theirs, router, gate, up, down, refs[0], refs[1:-2], *refs[-2:])

    parts = [shaped(count, width)] if whole else []
    operands = [*packs, own, *mine, *theirs, router, gate, up, *down]
    return local_call(
        kernel,
        [pltpu.VMEM((count, local * hidden), bf16)] + parts,
        operands,
        [VMEM] * len(operands),
        [pltpu.VMEM((count, width), bf16), pltpu.VMEM((count, LANES), bf16)],
        limit=10 if count <= 256 else 48,
    )

def down_call(act, down, pairs, ways):
    count = act.shape[0]
    width = down.shape[1]

    def kernel(act, down, *outs):
        spot, core = spot_and_core()
        for out, (shift, side) in zip(outs, pairs):
            size = out.shape[1]
            owner = partner(spot, shift, ways) * 2 + (1 - core if side else core)
            out[...] = dot(act[...], down[:, pl.ds(pl.multiple_of(owner * size, size), size)]).astype(bf16)

    return local_call(
        kernel,
        [shaped(count, width // (2 * ways))] * len(pairs),
        [act, down],
        [VMEM, VMEM],
    )


def on_device(
    hidden,
    routes,
    router_weight,
    gate_weight,
    up_weight,
    down_weight,
    q_latent,
    q_rope,
    cache_latent,
    cache_rope,
    cache_len,
):
    rows, width = hidden.shape
    local, _, units = gate_weight.shape
    n_dev, n_tp = lax.axis_size("dev"), lax.axis_size("tp")
    ways = n_tp // 2
    aligned = width % (n_tp * LANES) == 0
    spots = ways if aligned else 1
    share = width // (2 * spots)

    pack = pack_rows(hidden, routes, spots)
    pack, q_latent = lax.optimization_barrier((pack, q_latent))
    first = n_dev - 1
    far = over_dev(pack, first, n_dev)
    keep, give = attend(q_latent, q_rope, cache_latent, cache_rope, cache_len)
    again, keep, give = lax.optimization_barrier((pack, keep, give))
    packs = [pack] + [far if s == first else over_dev(again, s, n_dev) for s in range(1, n_dev)]
    near = [p[:, :share] for p in packs[1:]]
    first -= 1
    early = [send(near[first], "tp", along_x(s, ways)) for s in range(1, spots)]
    state = join([keep, send(give, "tp", other_core)], False)
    others = [s for s in reversed(range(1, n_dev)) if s != first + 1]
    rest = jnp.concatenate([near[s - 1] for s in others], axis=0)
    rest, state = lax.optimization_barrier((rest, state))
    late = [send(rest, "tp", along_x(s, ways)) for s in range(1, spots)]
    mine = [jnp.concatenate(near, axis=0)]
    for a, b in zip(early, late):
        come = {s: b[i * rows : (i + 1) * rows] for i, s in enumerate(others)}
        mine.append(jnp.concatenate([come.get(s, a) for s in range(1, n_dev)], axis=0))
    theirs = [send(m, "tp", other_core) for m in mine]
    states = [send(state, "tp", along_x(s, ways)) for s in range(1, ways)]
    theirs, state = lax.optimization_barrier((theirs, state))
    states = [state] + states

    gate, up, down = [
        pltpu.with_memory_space_constraint(w, pltpu.VMEM)
        for w in (gate_weight, up_weight, down_weight.reshape(local * units, width))
    ]
    act, *parts = act_call(
        packs, hidden, mine, theirs, router_weight.T, gate, up, down, routes.shape[1], ways, not aligned
    )
    def added(a, b):
        return a.astype(f32) + b.astype(f32)

    if aligned:
        steps = range(1, ways)
        far = down_call(act, down, [(s, 1) for s in steps], ways)
        far, act, states = lax.optimization_barrier((far, act, states))
        far = [send(p, "tp", other_core) for p in far]
        *own, there = down_call(act, down, [(s, 0) for s in steps] + [(0, 1)], ways)
        there = send(there, "tp", other_core)
        sums = [added(a, b).astype(bf16) for a, b in zip(own, far)]
        act, sums, states = lax.optimization_barrier((act, sums, states))
        (here,) = down_call(act, down, [(0, 0)], ways)
    else:
        spot, core = spot_and_core()
        size = width // n_tp

        def block(step, side):
            return lax.dynamic_slice_in_dim(parts[0], (partner(spot, step, ways) * 2 + side) * size, size, 1)

        own = [block(s, core) for s in range(ways)]
        far = [send(block(s, 1 - core), "tp", other_core) for s in range(ways)]
        sums = [added(a, b).astype(bf16) for a, b in zip(own[1:], far[1:])]
        here, there = own[0], far[0]
    sums = [send(p, "tp", along_x(s, ways)) for s, p in enumerate(sums, 1)]
    joined = join(states, True)
    attended = place_heads(joined, send(joined, "tp", other_core))
    sums, attended = lax.optimization_barrier((sums, attended))
    total = added(here, there)
    for p in sums:
        total = total + p.astype(f32)
    blocks = [total[i : i + rows] for i in range(0, total.shape[0], rows)]
    moe = blocks[0]
    for s in reversed(range(1, n_dev)):
        moe = lax.optimization_barrier(moe)
        moe = moe + over_dev(blocks[s].astype(bf16), s, n_dev).astype(f32)
    return (moe.astype(bf16), attended)

def solution(mesh):
    in_specs = (
        P(("group", "dev"), None),
        P(("group", "dev"), None),
        P(),
        P("dev", None, "tp"),
        P("dev", None, "tp"),
        P("dev", "tp", None),
        P(("group", "dev"), None, None),
        P(("group", "dev"), None, None),
        P(("group", "dev"), "tp", None),
        P(("group", "dev"), None, "tp"),
        P(("group", "dev")),
    )
    out_specs = (P(("group", "dev"), "tp"), P(("group", "dev"), None, None))
    return jax.shard_map(
        on_device, mesh=mesh, in_specs=in_specs, out_specs=out_specs, check_vma=False
    )
```

```python
import functools

import jax
import jax.numpy as jnp
from jax import lax
from jax.experimental import pallas as pl
from jax.experimental.pallas import tpu as pltpu
from jax.sharding import PartitionSpec as P

score_scale = 0.13524
route_scale = 2.5
very_low = -1e30
LANES = 128
WAIT_FLOPS = 100_000_000_000

f32, bf16 = jnp.float32, jnp.bfloat16
ANY = pl.BlockSpec(memory_space=pl.ANY)
VMEM = pl.BlockSpec(memory_space=pltpu.VMEM)
SMEM = pl.BlockSpec(memory_space=pltpu.SMEM)

def dot(a, b, contract=((1,), (0,))):
    return lax.dot_general(a, b, (contract, ((), ())), preferred_element_type=f32)

def send(value, axis, target):
    size = lax.axis_size(axis)
    return lax.ppermute(value, axis, [(i, target(i)) for i in range(size)])

def other_core(i):
    return i ^ 1

def partner(place, step, size):
    return place ^ step if size & (size - 1) == 0 else (step - place) % size

def along_x(step, ways):
    return lambda i: partner(i // 2, step, ways) * 2 + i % 2

def over_dev(value, step, size):
    return send(value, "dev", lambda i: partner(i, step, size))

def spot_and_core():
    tp = lax.axis_index("tp")
    return tp // 2, lax.rem(tp, 2)

def local_call(kernel, outs, operands, specs, scratch=(), flops=0, nbytes=0, exps=0, limit=8):
    return pl.pallas_call(
        kernel,
        out_shape=outs,
        in_specs=specs,
        out_specs=jax.tree.map(lambda _: VMEM, outs),
        scratch_shapes=list(scratch),
        cost_estimate=pl.CostEstimate(flops=flops, bytes_accessed=nbytes, transcendentals=exps),
        compiler_params=pltpu.CompilerParams(vmem_limit_bytes=limit << 20),
    )(*operands)

def shaped(*shape):
    return jax.ShapeDtypeStruct(shape, bf16)


def stats_of(top, total, heads):
    lane = lax.broadcasted_iota(jnp.int32, (heads, LANES), 1)
    high = total.astype(bf16).astype(f32)
    stats = jnp.where(lane == 0, top, jnp.where(lane == 1, high, jnp.where(lane == 2, total - high, 0.0)))
    return stats.astype(bf16)

def attend_kernel(q_lat, q_rope, keys, rope, lengths, keep, give, state):
    rows, heads, width = q_lat.shape
    span = keys.shape[1]
    start = lax.axis_index("tp") * span
    for r in range(rows):
        logits = dot(q_lat[r], keys[r], ((1,), (1,)))
        logits += dot(q_rope[r], rope[r], ((0,), (0,)))
        valid = lax.broadcasted_iota(jnp.int32, (heads, span), 1) + start < lengths[r]
        logits = jnp.where(valid, score_scale * logits, very_low)
        top = jnp.max(logits, axis=1, keepdims=True).astype(bf16).astype(f32)
        probs = jnp.where(valid, jnp.exp(logits - top), 0.0)
        total = jnp.sum(probs, axis=1, keepdims=True)
        state[r, :, :width] = dot(probs.astype(bf16), keys[r]).astype(bf16)
        state[r, :, width:] = stats_of(top, total, heads)
    half = heads // 2
    core = lax.rem(lax.axis_index("tp"), 2)
    keep[...] = state[:, pl.ds(pl.multiple_of(core * half, half), half), :]
    give[...] = state[:, pl.ds(pl.multiple_of((1 - core) * half, half), half), :]

def attend(q_latent, q_rope, cache_latent, cache_rope, cache_len):
    rows, heads, width = q_latent.shape
    span = cache_latent.shape[1]
    half = shaped(rows, heads // 2, width + LANES)
    return local_call(
        attend_kernel,
        [half, half],
        [q_latent, q_rope, cache_latent, cache_rope, cache_len],
        [VMEM, VMEM, VMEM, VMEM, SMEM],
        [pltpu.VMEM((rows, heads, width + LANES), bf16)],
        flops=2_000_000_000,
    )

def join_kernel(last, *refs):
    states, out = refs[:-1], refs[-1]
    rows, heads, full = states[0].shape
    width = full - LANES
    for r in range(rows):
        stats = [s[r, :, width:].astype(f32) for s in states]
        tops = [t[:, 0:1] for t in stats]
        top = functools.reduce(jnp.maximum, tops)
        scales = [jnp.exp(t - top) for t in tops]
        total = sum(c * (t[:, 1:2] + t[:, 2:3]) for c, t in zip(scales, stats))
        summed = sum(c * s[r, :, :width].astype(f32) for c, s in zip(scales, states))
        if last:
            out[r] = (summed / total).astype(bf16)
        else:
            out[r, :, :width] = summed.astype(bf16)
            out[r, :, width:] = stats_of(top, total, heads)

def join(states, last):
    rows, heads, width = states[0].shape
    out = shaped(rows, heads, width - LANES if last else width)
    return local_call(functools.partial(join_kernel, last), out, states, [VMEM] * len(states))

def place_kernel(mine, theirs, out):
    half = mine.shape[1]
    core = lax.rem(lax.axis_index("tp"), 2)
    out[:, pl.ds(pl.multiple_of(core * half, half), half), :] = mine[...]
    out[:, pl.ds(pl.multiple_of((1 - core) * half, half), half), :] = theirs[...]

def place_heads(mine, theirs):
    rows, half, width = mine.shape
    return local_call(place_kernel, shaped(rows, 2 * half, width), [mine, theirs], [VMEM, VMEM])


def pack_kernel(spots, hidden, routes, out, tags, sems):
    size = out.shape[1] - LANES
    picks, rows = routes.shape
    spot, core = spot_and_core()
    start = pl.multiple_of((spot * 2 + core if spots > 1 else core) * size, size)
    columns = pltpu.make_async_copy(hidden.at[:, pl.ds(start, size)], out.at[:, pl.ds(0, size)], sems.at[0])
    named = pltpu.make_async_copy(routes, tags, sems.at[1])
    columns.start()
    named.start()
    out[:, size:] = jnp.zeros((rows, LANES), bf16)
    named.wait()
    eye = lax.broadcasted_iota(jnp.int32, (rows, rows), 0) == lax.broadcasted_iota(jnp.int32, (rows, rows), 1)
    turned = dot(eye.astype(f32).astype(bf16), tags[...].astype(f32).astype(bf16), ((1,), (1,)))
    out[:, size : size + picks] = turned.astype(bf16)
    columns.wait()

def pack_rows(hidden, routes, spots):
    rows, width = hidden.shape
    return local_call(
        functools.partial(pack_kernel, spots),
        shaped(rows, width // (2 * spots) + LANES),
        [pltpu.with_memory_space_constraint(a, pltpu.HBM) for a in (hidden, routes.T)],
        [ANY, ANY],
        [pltpu.VMEM(routes.shape[::-1], jnp.int32), pltpu.SemaphoreType.DMA((2,))],
        flops=WAIT_FLOPS,
        limit=2,
    )

def act_kernel(picks, ways, packs, own, mine, theirs, router, gate, up, down, act, outs, x, tags):
    rows = own.shape[0]
    spots = len(mine)
    size = mine[0].shape[1]
    local, _, hidden = gate.shape
    spot, core = spot_and_core()
    x[pl.ds(0, rows), :] = own[...]
    later = pl.ds(rows, mine[0].shape[0])
    for s in range(spots):
        first = partner(spot, s, ways) * 2 if spots > 1 else 0
        x[later, pl.ds(pl.multiple_of((first + core) * size, size), size)] = mine[s][...]
        x[later, pl.ds(pl.multiple_of((first + 1 - core) * size, size), size)] = theirs[s][...]
    for s, pack in enumerate(packs):
        tags[pl.ds(s * rows, rows), :] = pack[:, size:]

    scores = jax.nn.sigmoid(dot(x[...], router[...], ((1,), (1,))))
    labels = lax.broadcasted_iota(jnp.int32, scores.shape, 1)
    chosen = tags[...].astype(f32).astype(jnp.int32)
    picked = labels < 0
    for k in range(picks):
        picked = picked | (labels == chosen[:, k : k + 1])
    kept = jnp.where(picked, scores, 0.0)
    weights = route_scale * kept / jnp.sum(kept, axis=1, keepdims=True)
    first = lax.axis_index("dev") * local

    for e in range(local):
        rate = jnp.sum(jnp.where(labels == first + e, weights, 0.0), axis=1, keepdims=True)
        a = dot(x[...], gate[e])
        b = dot(x[...], up[e])
        act[:, e * hidden : (e + 1) * hidden] = (a / (1.0 + jnp.exp(-a)) * b * rate).astype(bf16)
    for out in outs:
        out[...] = dot(act[...], down[0][...]).astype(bf16)

def act_call(packs, own, mine, theirs, router, gate, up, down, picks, ways, whole):
    rows, width = own.shape
    local, _, hidden = gate.shape
    count = rows * len(packs)
    down = [down] if whole else []
    cuts = [len(packs), 1, len(mine), len(theirs), 3, len(down)]

    def kernel(*refs):
        groups = []
        for cut in cuts:
            groups.append(refs[:cut])
            refs = refs[cut:]
        packs, (own,), mine, theirs, (router, gate, up), down = groups
        act_kernel(picks, ways, packs, own, mine, theirs, router, gate, up, down, refs[0], refs[1:-2], *refs[-2:])

    parts = [shaped(count, width)] if whole else []
    operands = [*packs, own, *mine, *theirs, router, gate, up, *down]
    return local_call(
        kernel,
        [pltpu.VMEM((count, local * hidden), bf16)] + parts,
        operands,
        [VMEM] * len(operands),
        [pltpu.VMEM((count, width), bf16), pltpu.VMEM((count, LANES), bf16)],
        limit=10 if count <= 256 else 48,
    )

def down_call(act, down, pairs, ways):
    count = act.shape[0]
    width = down.shape[1]

    def kernel(act, down, *outs):
        spot, core = spot_and_core()
        for out, (shift, side) in zip(outs, pairs):
            size = out.shape[1]
            owner = partner(spot, shift, ways) * 2 + (1 - core if side else core)
            out[...] = dot(act[...], down[:, pl.ds(pl.multiple_of(owner * size, size), size)]).astype(bf16)

    return local_call(
        kernel,
        [shaped(count, width // (2 * ways))] * len(pairs),
        [act, down],
        [VMEM, VMEM],
    )


def on_device(
    hidden,
    routes,
    router_weight,
    gate_weight,
    up_weight,
    down_weight,
    q_latent,
    q_rope,
    cache_latent,
    cache_rope,
    cache_len,
):
    rows, width = hidden.shape
    local, _, units = gate_weight.shape
    n_dev, n_tp = lax.axis_size("dev"), lax.axis_size("tp")
    ways = n_tp // 2
    aligned = width % (n_tp * LANES) == 0
    spots = ways if aligned else 1
    share = width // (2 * spots)

    pack = pack_rows(hidden, routes, spots)
    pack, q_latent = lax.optimization_barrier((pack, q_latent))
    first = n_dev - 1
    far = over_dev(pack, first, n_dev)
    keep, give = attend(q_latent, q_rope, cache_latent, cache_rope, cache_len)
    again, keep, give = lax.optimization_barrier((pack, keep, give))
    packs = [pack] + [far if s == first else over_dev(again, s, n_dev) for s in range(1, n_dev)]
    near = [p[:, :share] for p in packs[1:]]
    first -= 1
    early = [send(near[first], "tp", along_x(s, ways)) for s in range(1, spots)]
    state = join([keep, send(give, "tp", other_core)], False)
    others = [s for s in reversed(range(1, n_dev)) if s != first + 1]
    rest = jnp.concatenate([near[s - 1] for s in others], axis=0)
    rest, state = lax.optimization_barrier((rest, state))
    late = [send(rest, "tp", along_x(s, ways)) for s in range(1, spots)]
    mine = [jnp.concatenate(near, axis=0)]
    for a, b in zip(early, late):
        come = {s: b[i * rows : (i + 1) * rows] for i, s in enumerate(others)}
        mine.append(jnp.concatenate([come.get(s, a) for s in range(1, n_dev)], axis=0))
    theirs = [send(m, "tp", other_core) for m in mine]
    states = [send(state, "tp", along_x(s, ways)) for s in range(1, ways)]
    theirs, state = lax.optimization_barrier((theirs, state))
    states = [state] + states

    gate, up, down = [
        pltpu.with_memory_space_constraint(w, pltpu.VMEM)
        for w in (gate_weight, up_weight, down_weight.reshape(local * units, width))
    ]
    act, *parts = act_call(
        packs, hidden, mine, theirs, router_weight.T, gate, up, down, routes.shape[1], ways, not aligned
    )
    def added(a, b):
        return a.astype(f32) + b.astype(f32)

    if aligned:
        steps = range(1, ways)
        far = down_call(act, down, [(s, 1) for s in steps], ways)
        far, act, states = lax.optimization_barrier((far, act, states))
        far = [send(p, "tp", other_core) for p in far]
        own = down_call(act, down, [(s, 0) for s in steps], ways)
        sums = [added(a, b).astype(bf16) for a, b in zip(own, far)]
        act, sums, states = lax.optimization_barrier((act, sums, states))
        there, here = down_call(act, down, [(0, 1), (0, 0)], ways)
        there = send(there, "tp", other_core)
    else:
        spot, core = spot_and_core()
        size = width // n_tp

        def block(step, side):
            return lax.dynamic_slice_in_dim(parts[0], (partner(spot, step, ways) * 2 + side) * size, size, 1)

        own = [block(s, core) for s in range(ways)]
        far = [send(block(s, 1 - core), "tp", other_core) for s in range(ways)]
        sums = [added(a, b).astype(bf16) for a, b in zip(own[1:], far[1:])]
        here, there = own[0], far[0]
    sums = [send(p, "tp", along_x(s, ways)) for s, p in enumerate(sums, 1)]
    joined = join(states, True)
    attended = place_heads(joined, send(joined, "tp", other_core))
    sums, attended = lax.optimization_barrier((sums, attended))
    total = added(here, there)
    for p in sums:
        total = total + p.astype(f32)
    blocks = [total[i : i + rows] for i in range(0, total.shape[0], rows)]
    moe = blocks[0]
    for s in reversed(range(1, n_dev)):
        moe = lax.optimization_barrier(moe)
        moe = moe + over_dev(blocks[s].astype(bf16), s, n_dev).astype(f32)
    return (moe.astype(bf16), attended)

def solution(mesh):
    in_specs = (
        P(("group", "dev"), None),
        P(("group", "dev"), None),
        P(),
        P("dev", None, "tp"),
        P("dev", None, "tp"),
        P("dev", "tp", None),
        P(("group", "dev"), None, None),
        P(("group", "dev"), None, None),
        P(("group", "dev"), "tp", None),
        P(("group", "dev"), None, "tp"),
        P(("group", "dev")),
    )
    out_specs = (P(("group", "dev"), "tp"), P(("group", "dev"), None, None))
    return jax.shard_map(
        on_device, mesh=mesh, in_specs=in_specs, out_specs=out_specs, check_vma=False
    )
```

```python
import functools

import jax
import jax.numpy as jnp
from jax import lax
from jax.experimental import pallas as pl
from jax.experimental.pallas import tpu as pltpu
from jax.sharding import PartitionSpec as P

score_scale = 0.13524
route_scale = 2.5
very_low = -1e30
LANES = 128
WAIT_FLOPS = 100_000_000_000

f32, bf16 = jnp.float32, jnp.bfloat16
ANY = pl.BlockSpec(memory_space=pl.ANY)
VMEM = pl.BlockSpec(memory_space=pltpu.VMEM)
SMEM = pl.BlockSpec(memory_space=pltpu.SMEM)

def dot(a, b, contract=((1,), (0,))):
    return lax.dot_general(a, b, (contract, ((), ())), preferred_element_type=f32)

def send(value, axis, target):
    size = lax.axis_size(axis)
    return lax.ppermute(value, axis, [(i, target(i)) for i in range(size)])

def other_core(i):
    return i ^ 1

def partner(place, step, size):
    return place ^ step if size & (size - 1) == 0 else (step - place) % size

def along_x(step, ways):
    return lambda i: partner(i // 2, step, ways) * 2 + i % 2

def over_dev(value, step, size):
    return send(value, "dev", lambda i: partner(i, step, size))

def spot_and_core():
    tp = lax.axis_index("tp")
    return tp // 2, lax.rem(tp, 2)

def local_call(kernel, outs, operands, specs, scratch=(), flops=0, nbytes=0, exps=0, limit=8):
    return pl.pallas_call(
        kernel,
        out_shape=outs,
        in_specs=specs,
        out_specs=jax.tree.map(lambda _: VMEM, outs),
        scratch_shapes=list(scratch),
        cost_estimate=pl.CostEstimate(flops=flops, bytes_accessed=nbytes, transcendentals=exps),
        compiler_params=pltpu.CompilerParams(vmem_limit_bytes=limit << 20),
    )(*operands)

def shaped(*shape):
    return jax.ShapeDtypeStruct(shape, bf16)


def stats_of(top, total, heads):
    lane = lax.broadcasted_iota(jnp.int32, (heads, LANES), 1)
    high = total.astype(bf16).astype(f32)
    stats = jnp.where(lane == 0, top, jnp.where(lane == 1, high, jnp.where(lane == 2, total - high, 0.0)))
    return stats.astype(bf16)

def attend_kernel(q_lat, q_rope, keys, rope, lengths, keep, give, state):
    rows, heads, width = q_lat.shape
    span = keys.shape[1]
    start = lax.axis_index("tp") * span
    for r in range(rows):
        logits = dot(q_lat[r], keys[r], ((1,), (1,)))
        logits += dot(q_rope[r], rope[r], ((0,), (0,)))
        valid = lax.broadcasted_iota(jnp.int32, (heads, span), 1) + start < lengths[r]
        logits = jnp.where(valid, score_scale * logits, very_low)
        top = jnp.max(logits, axis=1, keepdims=True).astype(bf16).astype(f32)
        probs = jnp.where(valid, jnp.exp(logits - top), 0.0)
        total = jnp.sum(probs, axis=1, keepdims=True)
        state[r, :, :width] = dot(probs.astype(bf16), keys[r]).astype(bf16)
        state[r, :, width:] = stats_of(top, total, heads)
    half = heads // 2
    core = lax.rem(lax.axis_index("tp"), 2)
    keep[...] = state[:, pl.ds(pl.multiple_of(core * half, half), half), :]
    give[...] = state[:, pl.ds(pl.multiple_of((1 - core) * half, half), half), :]

def attend(q_latent, q_rope, cache_latent, cache_rope, cache_len):
    rows, heads, width = q_latent.shape
    span = cache_latent.shape[1]
    half = shaped(rows, heads // 2, width + LANES)
    return local_call(
        attend_kernel,
        [half, half],
        [q_latent, q_rope, cache_latent, cache_rope, cache_len],
        [VMEM, VMEM, VMEM, VMEM, SMEM],
        [pltpu.VMEM((rows, heads, width + LANES), bf16)],
        flops=2_000_000_000,
    )

def join_kernel(last, *refs):
    states, out = refs[:-1], refs[-1]
    rows, heads, full = states[0].shape
    width = full - LANES
    for r in range(rows):
        stats = [s[r, :, width:].astype(f32) for s in states]
        tops = [t[:, 0:1] for t in stats]
        top = functools.reduce(jnp.maximum, tops)
        scales = [jnp.exp(t - top) for t in tops]
        total = sum(c * (t[:, 1:2] + t[:, 2:3]) for c, t in zip(scales, stats))
        summed = sum(c * s[r, :, :width].astype(f32) for c, s in zip(scales, states))
        if last:
            out[r] = (summed / total).astype(bf16)
        else:
            out[r, :, :width] = summed.astype(bf16)
            out[r, :, width:] = stats_of(top, total, heads)

def join(states, last):
    rows, heads, width = states[0].shape
    out = shaped(rows, heads, width - LANES if last else width)
    return local_call(functools.partial(join_kernel, last), out, states, [VMEM] * len(states))

def place_kernel(mine, theirs, out):
    half = mine.shape[1]
    core = lax.rem(lax.axis_index("tp"), 2)
    out[:, pl.ds(pl.multiple_of(core * half, half), half), :] = mine[...]
    out[:, pl.ds(pl.multiple_of((1 - core) * half, half), half), :] = theirs[...]

def place_heads(mine, theirs):
    rows, half, width = mine.shape
    return local_call(place_kernel, shaped(rows, 2 * half, width), [mine, theirs], [VMEM, VMEM])


def pack_kernel(spots, hidden, routes, out, tags, sems):
    size = out.shape[1] - LANES
    picks, rows = routes.shape
    spot, core = spot_and_core()
    start = pl.multiple_of((spot * 2 + core if spots > 1 else core) * size, size)
    columns = pltpu.make_async_copy(hidden.at[:, pl.ds(start, size)], out.at[:, pl.ds(0, size)], sems.at[0])
    named = pltpu.make_async_copy(routes, tags, sems.at[1])
    columns.start()
    named.start()
    out[:, size:] = jnp.zeros((rows, LANES), bf16)
    named.wait()
    eye = lax.broadcasted_iota(jnp.int32, (rows, rows), 0) == lax.broadcasted_iota(jnp.int32, (rows, rows), 1)
    turned = dot(eye.astype(f32).astype(bf16), tags[...].astype(f32).astype(bf16), ((1,), (1,)))
    out[:, size : size + picks] = turned.astype(bf16)
    columns.wait()

def pack_rows(hidden, routes, spots):
    rows, width = hidden.shape
    return local_call(
        functools.partial(pack_kernel, spots),
        shaped(rows, width // (2 * spots) + LANES),
        [pltpu.with_memory_space_constraint(a, pltpu.HBM) for a in (hidden, routes.T)],
        [ANY, ANY],
        [pltpu.VMEM(routes.shape[::-1], jnp.int32), pltpu.SemaphoreType.DMA((2,))],
        flops=WAIT_FLOPS,
        limit=2,
    )

def act_kernel(picks, ways, packs, own, mine, theirs, router, gate, up, down, act, outs, x, tags):
    rows = own.shape[0]
    spots = len(mine)
    size = mine[0].shape[1]
    local, _, hidden = gate.shape
    spot, core = spot_and_core()
    x[pl.ds(0, rows), :] = own[...]
    later = pl.ds(rows, mine[0].shape[0])
    for s in range(spots):
        first = partner(spot, s, ways) * 2 if spots > 1 else 0
        x[later, pl.ds(pl.multiple_of((first + core) * size, size), size)] = mine[s][...]
        x[later, pl.ds(pl.multiple_of((first + 1 - core) * size, size), size)] = theirs[s][...]
    for s, pack in enumerate(packs):
        tags[pl.ds(s * rows, rows), :] = pack[:, size:]

    scores = jax.nn.sigmoid(dot(x[...], router[...], ((1,), (1,))))
    labels = lax.broadcasted_iota(jnp.int32, scores.shape, 1)
    chosen = tags[...].astype(f32).astype(jnp.int32)
    picked = labels < 0
    for k in range(picks):
        picked = picked | (labels == chosen[:, k : k + 1])
    kept = jnp.where(picked, scores, 0.0)
    weights = route_scale * kept / jnp.sum(kept, axis=1, keepdims=True)
    first = lax.axis_index("dev") * local

    for e in range(local):
        rate = jnp.sum(jnp.where(labels == first + e, weights, 0.0), axis=1, keepdims=True)
        a = dot(x[...], gate[e])
        b = dot(x[...], up[e])
        act[:, e * hidden : (e + 1) * hidden] = (a / (1.0 + jnp.exp(-a)) * b * rate).astype(bf16)
    for out in outs:
        out[...] = dot(act[...], down[0][...]).astype(bf16)

def act_call(packs, own, mine, theirs, router, gate, up, down, picks, ways, whole):
    rows, width = own.shape
    local, _, hidden = gate.shape
    count = rows * len(packs)
    down = [down] if whole else []
    cuts = [len(packs), 1, len(mine), len(theirs), 3, len(down)]

    def kernel(*refs):
        groups = []
        for cut in cuts:
            groups.append(refs[:cut])
            refs = refs[cut:]
        packs, (own,), mine, theirs, (router, gate, up), down = groups
        act_kernel(picks, ways, packs, own, mine, theirs, router, gate, up, down, refs[0], refs[1:-2], *refs[-2:])

    parts = [shaped(count, width)] if whole else []
    operands = [*packs, own, *mine, *theirs, router, gate, up, *down]
    return local_call(
        kernel,
        [pltpu.VMEM((count, local * hidden), bf16)] + parts,
        operands,
        [VMEM] * len(operands),
        [pltpu.VMEM((count, width), bf16), pltpu.VMEM((count, LANES), bf16)],
        limit=10 if count <= 256 else 48,
    )

def down_call(act, down, pairs, ways):
    count = act.shape[0]
    width = down.shape[1]

    def kernel(act, down, *outs):
        spot, core = spot_and_core()
        for out, (shift, side) in zip(outs, pairs):
            size = out.shape[1]
            owner = partner(spot, shift, ways) * 2 + (1 - core if side else core)
            out[...] = dot(act[...], down[:, pl.ds(pl.multiple_of(owner * size, size), size)]).astype(bf16)

    return local_call(
        kernel,
        [shaped(count, width // (2 * ways))] * len(pairs),
        [act, down],
        [VMEM, VMEM],
    )


def on_device(
    hidden,
    routes,
    router_weight,
    gate_weight,
    up_weight,
    down_weight,
    q_latent,
    q_rope,
    cache_latent,
    cache_rope,
    cache_len,
):
    rows, width = hidden.shape
    local, _, units = gate_weight.shape
    n_dev, n_tp = lax.axis_size("dev"), lax.axis_size("tp")
    ways = n_tp // 2
    aligned = width % (n_tp * LANES) == 0
    spots = ways if aligned else 1
    share = width // (2 * spots)

    pack = pack_rows(hidden, routes, spots)
    pack, q_latent = lax.optimization_barrier((pack, q_latent))
    first = n_dev - 1
    far = over_dev(pack, first, n_dev)
    keep, give = attend(q_latent, q_rope, cache_latent, cache_rope, cache_len)
    again, keep, give = lax.optimization_barrier((pack, keep, give))
    packs = [pack] + [far if s == first else over_dev(again, s, n_dev) for s in range(1, n_dev)]
    near = [p[:, :share] for p in packs[1:]]
    first -= 1
    early = [send(near[first], "tp", along_x(s, ways)) for s in range(1, spots)]
    state = join([keep, send(give, "tp", other_core)], False)
    others = [s for s in reversed(range(1, n_dev)) if s != first + 1]
    rest = jnp.concatenate([near[s - 1] for s in others], axis=0)
    late = [send(rest, "tp", along_x(s, ways)) for s in range(1, spots)]
    late, state = lax.optimization_barrier((late, state))
    mine = [jnp.concatenate(near, axis=0)]
    for a, b in zip(early, late):
        come = {s: b[i * rows : (i + 1) * rows] for i, s in enumerate(others)}
        mine.append(jnp.concatenate([come.get(s, a) for s in range(1, n_dev)], axis=0))
    theirs = [send(m, "tp", other_core) for m in mine]
    states = [send(state, "tp", along_x(s, ways)) for s in range(1, ways)]
    theirs, state = lax.optimization_barrier((theirs, state))
    states = [state] + states

    gate, up, down = [
        pltpu.with_memory_space_constraint(w, pltpu.VMEM)
        for w in (gate_weight, up_weight, down_weight.reshape(local * units, width))
    ]
    act, *parts = act_call(
        packs, hidden, mine, theirs, router_weight.T, gate, up, down, routes.shape[1], ways, not aligned
    )
    def added(a, b):
        return a.astype(f32) + b.astype(f32)

    if aligned:
        steps = range(1, ways)
        far = down_call(act, down, [(s, 1) for s in steps], ways)
        far, act, states = lax.optimization_barrier((far, act, states))
        far = [send(p, "tp", other_core) for p in far]
        *own, there = down_call(act, down, [(s, 0) for s in steps] + [(0, 1)], ways)
        there = send(there, "tp", other_core)
        sums = [added(a, b).astype(bf16) for a, b in zip(own, far)]
        act, sums, states = lax.optimization_barrier((act, sums, states))
        (here,) = down_call(act, down, [(0, 0)], ways)
    else:
        spot, core = spot_and_core()
        size = width // n_tp

        def block(step, side):
            return lax.dynamic_slice_in_dim(parts[0], (partner(spot, step, ways) * 2 + side) * size, size, 1)

        own = [block(s, core) for s in range(ways)]
        far = [send(block(s, 1 - core), "tp", other_core) for s in range(ways)]
        sums = [added(a, b).astype(bf16) for a, b in zip(own[1:], far[1:])]
        here, there = own[0], far[0]
    sums = [send(p, "tp", along_x(s, ways)) for s, p in enumerate(sums, 1)]
    joined = join(states, True)
    attended = place_heads(joined, send(joined, "tp", other_core))
    sums, attended = lax.optimization_barrier((sums, attended))
    total = added(here, there)
    for p in sums:
        total = total + p.astype(f32)
    blocks = [total[i : i + rows] for i in range(0, total.shape[0], rows)]
    moe = blocks[0]
    for s in reversed(range(1, n_dev)):
        moe = lax.optimization_barrier(moe)
        moe = moe + over_dev(blocks[s].astype(bf16), s, n_dev).astype(f32)
    return (moe.astype(bf16), attended)

def solution(mesh):
    in_specs = (
        P(("group", "dev"), None),
        P(("group", "dev"), None),
        P(),
        P("dev", None, "tp"),
        P("dev", None, "tp"),
        P("dev", "tp", None),
        P(("group", "dev"), None, None),
        P(("group", "dev"), None, None),
        P(("group", "dev"), "tp", None),
        P(("group", "dev"), None, "tp"),
        P(("group", "dev")),
    )
    out_specs = (P(("group", "dev"), "tp"), P(("group", "dev"), None, None))
    return jax.shard_map(
        on_device, mesh=mesh, in_specs=in_specs, out_specs=out_specs, check_vma=False
    )
```
